32 devices in a mesh: dp: 2 (over y), mp: 16 (over z, x, core).
Axes of the slice: x: 2, y: 2, z: 4, core: 2. Of those that a mesh axis runs over, the one named last changes fastest.
Arguments:
- inputs: bfloat16 [16384, 2048], P(('dp', 'mp')), may hold values from -6 to 6
- item_counts: int32 [2, 4], P('dp'), may hold values from 1 to 8, 16 in all within a row
- first_gain: bfloat16 [2048], replicated, may hold values from 0.5 to 1.5
- first_shift: bfloat16 [2048], replicated, may hold values from -0.59765625 to 0.59765625
- query_weight: bfloat16 [2048, 2048], P(None, 'mp'), may hold values from -0.125 to 0.125
- query_bias: bfloat16 [2048], P('mp'), may hold values from -3 to 3
- key_weight: bfloat16 [2048, 2048], P(None, 'mp'), may hold values from -0.125 to 0.125
- value_weight: bfloat16 [2048, 2048], P(None, 'mp'), may hold values from -0.125 to 0.125
- value_bias: bfloat16 [2048], P('mp'), may hold values from -0.59765625 to 0.59765625
- output_weight: bfloat16 [2048, 2048], P('mp'), may hold values from -0.5 to 0.5
- output_bias: bfloat16 [2048], replicated, may hold values from -3 to 3
- second_gain: bfloat16 [2048], replicated, may hold values from 0.5 to 1.5
- second_shift: bfloat16 [2048], replicated, may hold values from -3 to 3
- expand_weight: bfloat16 [2048, 8192], P(None, 'mp'), may hold values from -0.125 to 0.125
- expand_bias: bfloat16 [8192], P('mp'), may hold values from -3 to 3
- contract_weight: bfloat16 [8192, 2048], P('mp'), may hold values from -0.0625 to 0.0625
- contract_bias: bfloat16 [2048], replicated, may hold values from -3 to 3
- cotangent: bfloat16 [16384, 2048], P(('dp', 'mp')), may hold values from -6 to 6
Outputs:
- layer_out: bfloat16 [16384, 2048], P(('dp', 'mp'))
- input_grad: bfloat16 [16384, 2048], P(('dp', 'mp'))
- first_gain_grad: float32 [2048], replicated
- first_shift_grad: float32 [2048], replicated
- query_weight_grad: float32 [2048, 2048], P(None, 'mp')
- query_bias_grad: float32 [2048], P('mp')
- key_weight_grad: float32 [2048, 2048], P(None, 'mp')
- value_weight_grad: float32 [2048, 2048], P(None, 'mp')
- value_bias_grad: float32 [2048], P('mp')
- output_weight_grad: float32 [2048, 2048], P('mp')
- output_bias_grad: float32 [2048], replicated
- second_gain_grad: float32 [2048], replicated
- second_shift_grad: float32 [2048], replicated
- expand_weight_grad: float32 [2048, 8192], P(None, 'mp')
- expand_bias_grad: float32 [8192], P('mp')
- contract_weight_grad: float32 [8192, 2048], P('mp')
- contract_bias_grad: float32 [2048], replicated
The draws below stay inside these ranges and needn't reach their ends.
Inputs may be any that keep to these rules, and one draw needn't show every extreme that they name: Each row of item_counts sums to 16, and some item of each row has exactly 8 segments.
All inputs are finite; a program needn't handle non-finite values.
Results may differ from the reference program's by a relative error of at most 0.02.
Values may be sent and summed in bfloat16 or wider, within the bound.
No kernel may reach another device: no remote copies, remote signals or barrier semaphores. Data moves between devices by JAX's collectives and lax.ppermute only.
A program may use at most 576 MiB of HBM per device.

```python
import math
import jax
import jax.numpy as jnp
import numpy as np
from jax import lax

D = 2048
HD = 64
FF = 8192
SEG = 512
NSUM = 50
ITEMS_GRP = 4
SLOTS = 16
MOST_SEGS = 8
GROUPS = 2
ROWS = 16384
N_DP = 2
N_MP = 16


def steps_of(rng, dims, shards, smallest, top_value):
    loudness, own = 1.0, jax.random.fold_in(rng, 6)
    for position, parts in shards:
        heights = jnp.exp(jax.random.uniform(jax.random.fold_in(own, position), (parts,), jnp.float32, smallest / len(shards), top_value / len(shards)))
        loudness = loudness * jnp.repeat(heights, dims[position] // parts).reshape([-1 if axis == position else 1 for axis in range(len(dims))])
    return loudness


def split_up(number_of, total, most, lean):
    weights = [(1 << 20) // math.isqrt(grade ** lean) + 1 for grade in range(2, number_of + 1)]
    rest, given = total - most - (number_of - 1), [1] * (number_of - 1)
    while rest > 0:
        candidates = [i for i in range(number_of - 1) if given[i] < most]
        pool, remaining = sum([weights[i] for i in candidates]), rest
        for i in candidates:
            more = min(most - given[i], max(1, remaining * weights[i] // pool), rest)
            given[i] = given[i] + more
            rest = rest - more
    return np.array([most] + given)


def uneven_parts(own_key, count, total, limit, lean):
    if count == 2:
        one = jax.random.randint(own_key, (), max(1, total - limit), min(limit, total - 1) + 1)
        return jnp.stack([one, total - one])
    tallies = jnp.asarray(split_up(count, total, limit, lean), jnp.int32)
    pairs = (count - 1) // 2
    donor, sink = tallies[1:1 + 2 * pairs:2], tallies[2:2 + 2 * pairs:2]
    margin = jnp.minimum(donor - 1, limit - sink)
    shifted = jax.random.randint(jax.random.fold_in(own_key, 1), (pairs,), 0, 1 << 20) % (margin + 1)
    tallies = tallies.at[1:1 + 2 * pairs:2].set(donor - shifted).at[2:2 + 2 * pairs:2].set(sink + shifted)
    return tallies[jax.random.permutation(jax.random.fold_in(own_key, 2), count)]


def noise(key, extent, scale, most, split=(), held_as=jnp.bfloat16):
    entries = jax.random.normal(key, extent, jnp.float32) * scale
    if len(split) > 0:
        entries = steps_of(key, extent, split, -0.22, 0.18) * entries
    return jnp.clip(entries, min=-most, max=most).astype(held_as)


def setup_inputs(seed: int = 0) -> dict:
    seeds = jax.random.split(jax.random.key(seed), 19)
    return {
        "inputs": noise(seeds[0], (ROWS, D), 1.0, 6.0, ((0, 32),)),
        "item_counts": jax.vmap(lambda own: uneven_parts(own, ITEMS_GRP, SLOTS, MOST_SEGS, 2))(jax.random.split(seeds[1], GROUPS)).reshape((GROUPS, ITEMS_GRP)).astype(jnp.int32),
        "first_gain": jnp.clip(jax.random.uniform(seeds[2], (D,), jnp.float32, 0.5, 1.5), 0.5, 1.5).astype(jnp.bfloat16),
        "first_shift": noise(seeds[3], (D,), 0.1, 0.59765625),
        "query_weight": noise(seeds[4], (D, D), D ** -0.5, 0.125, ((1, 16),)),
        "query_bias": noise(seeds[5], (D,), 0.5, 3.0, ((0, 16),)),
        "key_weight": noise(seeds[6], (D, D), D ** -0.5, 0.125, ((1, 16),)),
        "value_weight": noise(seeds[7], (D, D), D ** -0.5, 0.125, ((1, 16),)),
        "value_bias": noise(seeds[8], (D,), 0.1, 0.59765625, ((0, 16),)),
        "output_weight": noise(seeds[9], (D, D), (max(D // 16, 1)) ** -0.5, 0.5, ((0, 16),)),
        "output_bias": noise(seeds[10], (D,), 0.5, 3.0),
        "second_gain": jnp.clip(jax.random.uniform(seeds[11], (D,), jnp.float32, 0.5, 1.5), 0.5, 1.5).astype(jnp.bfloat16),
        "second_shift": noise(seeds[12], (D,), 0.5, 3.0),
        "expand_weight": noise(seeds[13], (D, FF), D ** -0.5, 0.125, ((1, 16),)),
        "expand_bias": noise(seeds[14], (FF,), 0.5, 3.0, ((0, 16),)),
        "contract_weight": noise(seeds[15], (FF, D), FF ** -0.5, 0.0625, ((0, 16),)),
        "contract_bias": noise(seeds[16], (D,), 0.5, 3.0),
        "cotangent": noise(seeds[17], (ROWS, D), 1.0, 6.0, ((0, 32),)),
    }


@jax.custom_vjp
def low(v):
    return lax.optimization_barrier(v.astype(jnp.bfloat16)).astype(jnp.float32)

@jax.custom_vjp
def low_back(v):
    return v

def low_keep(v):
    return (low(v), None)

def low_pass(kept, grad):
    return (grad,)

def back_keep(v):
    return (v, None)

def back_low(kept, grad):
    return (low(grad),)
low.defvjp(low_keep, low_pass)
low_back.defvjp(back_keep, back_low)
EPSILON = 1e-05
MASKED = -1e+30
PRECISE = lax.Precision.HIGHEST

def smooth_gate(values):
    return 0.5 * values * (1.0 + jnp.tanh(0.7978845608 * (values + 0.044715 * values * values * values)))

def product(former, latter):
    return jnp.dot(former, latter, precision=PRECISE, preferred_element_type=jnp.float32)

def normalize(values, scaling, offset):
    centre = lax.optimization_barrier(jnp.mean(values, axis=-1, keepdims=True))
    centred = values - centre
    spread = lax.optimization_barrier(jnp.mean(centred * centred, axis=-1, keepdims=True))
    return centred * lax.rsqrt(spread + EPSILON) * scaling + offset

def slot_items(counts):
    item_ends = jnp.cumsum(counts.astype(jnp.int32)).astype(jnp.int32)
    places = jnp.arange(SLOTS, dtype=jnp.int32)
    return lax.optimization_barrier(jnp.sum((places[:, None] >= item_ends[None, :]).astype(jnp.int32), axis=1)).astype(jnp.int32)

def summary_allowed(slot_item):
    slot_count = slot_item.shape[0]
    key_items = jnp.repeat(slot_item, NSUM)
    key_slots = jnp.repeat(jnp.arange(slot_count, dtype=jnp.int32), NSUM)
    own_slots = jnp.arange(slot_count, dtype=jnp.int32)
    return (key_items[None, :] == slot_item[:, None]) & (key_slots[None, :] < own_slots[:, None])

def attend(queries, key_all, value_all, allowed):
    head_count = queries.shape[1] // HD
    query_blocks = queries.reshape(SLOTS, SEG, head_count, HD)
    key_blocks = key_all.reshape(SLOTS, SEG, head_count, HD)
    value_blocks = value_all.reshape(SLOTS, SEG, head_count, HD)
    summary_keys = key_blocks[:, SEG - NSUM:].reshape(SLOTS * NSUM, head_count, HD)
    summary_values = value_blocks[:, SEG - NSUM:].reshape(SLOTS * NSUM, head_count, HD)
    row_pos = jnp.arange(SEG, dtype=jnp.int32)
    causal = row_pos[:, None] >= row_pos[None, :]

    def one_block(pieces):
        query_block, key_block, value_block, allow_row = pieces
        visible = jnp.concatenate([causal, jnp.broadcast_to(allow_row[None, :], (SEG, SLOTS * NSUM))], axis=1)
        key_rows = jnp.concatenate([key_block, summary_keys], axis=0)
        value_rows = jnp.concatenate([value_block, summary_values], axis=0)
        scores = low_back(jnp.einsum('qhd,khd->hqk', query_block, key_rows, precision=PRECISE))
        scores = jnp.where(visible[None], scores, MASKED)
        highest = lax.optimization_barrier(jnp.max(scores, axis=-1, keepdims=True))
        weights = jnp.exp(scores - highest)
        shares = low(weights / lax.optimization_barrier(jnp.sum(weights, axis=-1, keepdims=True)))
        mixture = jnp.einsum('hqk,khd->qhd', shares, value_rows, precision=PRECISE)
        return mixture.reshape(SEG, head_count * HD)
    mixture = lax.map(jax.checkpoint(one_block), (query_blocks, key_blocks, value_blocks, allowed))
    return mixture.reshape(SLOTS * SEG, head_count * HD)

def group_forward(hidden_in, counts, params):
    first_gain, first_shift, query_weight, query_bias, key_weight, value_weight, value_bias, output_weight, output_bias, second_gain, second_shift, expand_weight, expand_bias, contract_weight, contract_bias = params
    allowed = summary_allowed(slot_items(counts))
    query_scale = HD ** (-0.5)
    col_width = D // N_MP
    feed_width = FF // N_MP
    normed = low(normalize(hidden_in, first_gain, first_shift))
    attention_pieces = (query_weight.reshape(D, N_MP, col_width).transpose(1, 0, 2), query_bias.reshape(N_MP, col_width), key_weight.reshape(D, N_MP, col_width).transpose(1, 0, 2), value_weight.reshape(D, N_MP, col_width).transpose(1, 0, 2), value_bias.reshape(N_MP, col_width), output_weight.reshape(N_MP, col_width, D))

    def attention_shard(running, pieces):
        shard_query, shard_qbias, shard_key, shard_value, shard_vbias, shard_output = pieces
        shard_in = low_back(normed)
        queries = low(low_back((product(shard_in, shard_query) + shard_qbias) * query_scale))
        key_all = low(low_back(product(shard_in, shard_key)))
        value_all = low(low_back(product(shard_in, shard_value) + shard_vbias))
        mixture = low(low_back(attend(queries, key_all, value_all, allowed)))
        return (running + low(product(mixture, shard_output)), None)
    branch, ignored = lax.scan(jax.checkpoint(attention_shard), jnp.zeros_like(hidden_in), attention_pieces)
    middle = hidden_in + low_back(branch) + output_bias
    normed_two = low(normalize(middle, second_gain, second_shift))
    feed_pieces = (expand_weight.reshape(D, N_MP, feed_width).transpose(1, 0, 2), expand_bias.reshape(N_MP, feed_width), contract_weight.reshape(N_MP, feed_width, D))

    def feed_shard(running, pieces):
        shard_expand, shard_ebias, shard_contract = pieces
        shard_in = low_back(normed_two)
        before = low_back(product(shard_in, shard_expand) + shard_ebias)
        active = low(smooth_gate(before))
        return (running + low(product(active, shard_contract)), None)
    branch_two, ignored = lax.scan(jax.checkpoint(feed_shard), jnp.zeros_like(hidden_in), feed_pieces)
    return middle + low_back(branch_two) + contract_bias

def add_pair(augend, addend):
    return augend + addend

def reference(inputs, item_counts, first_gain, first_shift, query_weight, query_bias, key_weight, value_weight, value_bias, output_weight, output_bias, second_gain, second_shift, expand_weight, expand_bias, contract_weight, contract_bias, cotangent):
    params = tuple((weight.astype(jnp.float32) for weight in (first_gain, first_shift, query_weight, query_bias, key_weight, value_weight, value_bias, output_weight, output_bias, second_gain, second_shift, expand_weight, expand_bias, contract_weight, contract_bias)))
    group_rows = SLOTS * SEG
    blocks_in = inputs.reshape(N_DP, group_rows, D)
    blocks_cot = cotangent.reshape(N_DP, group_rows, D)

    def one_group(totals, pieces):
        group_in, counts, group_cot = pieces

        def forward(values, weights):
            return group_forward(values, counts, weights)
        group_out, pull_back = jax.vjp(forward, group_in.astype(jnp.float32), params)
        group_grad, param_grads = pull_back(group_cot.astype(jnp.float32))
        totals = jax.tree.map(add_pair, totals, param_grads)
        return (totals, (group_out.astype(jnp.bfloat16), group_grad.astype(jnp.bfloat16)))
    zero_grads = tuple((jnp.zeros_like(weight) for weight in params))
    totals, (group_outs, group_grads) = lax.scan(one_group, zero_grads, (blocks_in, item_counts, blocks_cot))
    return (group_outs.reshape(ROWS, D), group_grads.reshape(ROWS, D), totals[0], totals[1], totals[2], totals[3], totals[4], totals[5], totals[6], totals[7], totals[8], totals[9], totals[10], totals[11], totals[12], totals[13], totals[14])
```

```python
import functools

import jax
import jax.numpy as jnp
from jax import lax
from jax.experimental import pallas as pl
from jax.experimental.pallas import tpu as pltpu
from jax.sharding import PartitionSpec as P

HD = 64
SEG = 512
NSUM = 50
TAIL = 64
TEAM = 4
PAIR = 2 * HD
QB = 256
EPSILON = 1e-05
MASKED = -1e30
LIGHT = pl.CostEstimate(flops=1024, bytes_accessed=1024, transcendentals=0)
F32 = jnp.float32
BF16 = jnp.bfloat16


def gelu_and_slope(v):
    inner = 0.7978845608 * (v + 0.044715 * v * v * v)
    t = jnp.tanh(inner)
    value = 0.5 * v * (1.0 + t)
    slope = 0.5 * (1.0 + t) + 0.5 * v * (1.0 - t * t) * (
        0.7978845608 * (1.0 + 3.0 * 0.044715 * v * v)
    )
    return value, slope


def normalize(values, scaling, offset):
    centre = jnp.mean(values, axis=-1, keepdims=True)
    centred = values - centre
    spread = jnp.mean(centred * centred, axis=-1, keepdims=True)
    return centred * lax.rsqrt(spread + EPSILON) * scaling + offset


def slot_items(counts, slot_count):
    item_ends = jnp.cumsum(counts)
    places = jnp.arange(slot_count, dtype=jnp.int32)
    return jnp.sum((places[:, None] >= item_ends[None, :]).astype(jnp.int32), axis=1)


def dot(a, b):
    return jnp.dot(a, b, preferred_element_type=F32)


def dot_nt(a, b):
    return lax.dot_general(a, b, (((1,), (1,)), ((), ())), preferred_element_type=F32)


def dot_tn(a, b):
    return lax.dot_general(a, b, (((0,), (0,)), ((), ())), preferred_element_type=F32)


def head_only(block, h):
    lane = lax.broadcasted_iota(jnp.int32, block.shape, 1)
    return jnp.where((lane // HD) == h, block, jnp.zeros_like(block))


def causal(block):
    key = lax.broadcasted_iota(jnp.int32, block.shape, 0)
    query = lax.broadcasted_iota(jnp.int32, block.shape, 1)
    return jnp.where(query >= key, block, MASKED)


def hide_rows(block, count):
    key = lax.broadcasted_iota(jnp.int32, block.shape, 0)
    return jnp.where(key >= count, block, MASKED)


def key_blocks(info_ref, e):
    slots = info_ref.shape[0] - 2
    team, mine = info_ref[slots], info_ref[slots + 1]
    i = mine ^ e
    item = info_ref[team * TEAM + i]

    def hidden(other):
        same = info_ref[jnp.maximum(other, 0)] == item
        return jnp.where(jnp.logical_and(other >= 0, same), TAIL - NSUM, TAIL)

    rows = TEAM * SEG
    out = [(rows + 2 * f * TAIL, hidden((team - 1) * TEAM + (mine ^ f))) for f in range(TEAM)]
    for d in range(1, TEAM):
        j = i ^ d
        inside = j < i
        start = jnp.where(
            inside, (e ^ d) * SEG + SEG - TAIL, rows + (2 * (e ^ d) + 1) * TAIL
        )
        out.append((start, hidden(jnp.where(inside, team, team - 2) * TEAM + j)))
    return out


def attend_kernel(first, count, info_ref, qkv_ref, mix_ref, log_ref):
    def segment(e, carry):
        base = pl.multiple_of(e * SEG, SEG)
        place = pl.multiple_of((e - first) * SEG, SEG)
        extra = key_blocks(info_ref, e)
        keys = qkv_ref[pl.ds(base, SEG), PAIR : 2 * PAIR]
        value_t = qkv_ref[pl.ds(base, SEG), 2 * PAIR : 3 * PAIR].T
        extra_keys = [
            qkv_ref[pl.ds(pl.multiple_of(s, TAIL), TAIL), PAIR : 2 * PAIR] for s, _ in extra
        ]
        extra_values = [
            qkv_ref[pl.ds(pl.multiple_of(s, TAIL), TAIL), 2 * PAIR : 3 * PAIR] for s, _ in extra
        ]
        extra_keys = jnp.concatenate(extra_keys, axis=0)
        extra_value_t = jnp.concatenate(extra_values, axis=0).T
        for qb in range(SEG // QB):
            query = qkv_ref[pl.ds(base + qb * QB, QB), 0:PAIR]
            seen = (qb + 1) * QB
            outs = []
            for h in range(2):
                qh = head_only(query, h)
                own = dot_nt(keys[:seen], qh)
                parts = [own[: qb * QB]] if qb else []
                parts.append(causal(own[qb * QB :]))
                far = dot_nt(extra_keys, qh)
                for n, (_, hidden) in enumerate(extra):
                    parts.append(hide_rows(far[n * TAIL : (n + 1) * TAIL], hidden))
                high = functools.reduce(
                    jnp.maximum, [jnp.max(p, axis=0, keepdims=True) for p in parts]
                )
                parts = [jnp.exp(p - high) for p in parts]
                total = functools.reduce(
                    jnp.add, [jnp.sum(p, axis=0, keepdims=True) for p in parts]
                )
                cut = 2 if qb else 1
                p_own = jnp.concatenate([p.astype(BF16) for p in parts[:cut]], axis=0)
                p_far = jnp.concatenate([p.astype(BF16) for p in parts[cut:]], axis=0)
                rows = slice(h * HD, (h + 1) * HD)
                mixed = dot(value_t[rows, :seen], p_own) + dot(extra_value_t[rows], p_far)
                outs.append(mixed / total)
                log_ref[0, e - first, h : h + 1, qb * QB : (qb + 1) * QB] = high + jnp.log(total)
            mix_ref[pl.ds(place + qb * QB, QB), :] = jnp.concatenate(outs, axis=0).T.astype(BF16)
        return carry

    lax.fori_loop(first, first + count, segment, 0)


def attend(info, qkv, first, count):
    pieces = qkv.shape[1] // (3 * PAIR)
    rows = count * SEG
    return pl.pallas_call(
        functools.partial(attend_kernel, first, count),
        grid_spec=pltpu.PrefetchScalarGridSpec(
            num_scalar_prefetch=1,
            grid=(pieces,),
            in_specs=[pl.BlockSpec((qkv.shape[0], 3 * PAIR), lambda r, t: (0, r))],
            out_specs=[
                pl.BlockSpec((rows, PAIR), lambda r, t: (0, r)),
                pl.BlockSpec((1, count, 2, SEG), lambda r, t: (r, 0, 0, 0)),
            ],
        ),
        out_shape=[
            jax.ShapeDtypeStruct((rows, pieces * PAIR), BF16),
            jax.ShapeDtypeStruct((pieces, count, 2, SEG), F32),
        ],
        compiler_params=pltpu.CompilerParams(vmem_limit_bytes=56 * 1024 * 1024),
        cost_estimate=LIGHT,
        name="attend",
    )(info, qkv)


def attend_back_kernel(first, count, info_ref, qkv_ref, mix_ref, grad_ref, log_ref, *rest):
    out_ref, key_acc, value_acc = rest[-3:]
    if len(rest) == 4:
        before_ref = rest[0]
        key_acc[...] = before_ref[:, PAIR : 2 * PAIR].astype(F32)
        value_acc[...] = before_ref[:, 2 * PAIR : 3 * PAIR].astype(F32)
        out_ref[:, 0:PAIR] = before_ref[:, 0:PAIR]
    else:
        key_acc[...] = jnp.zeros_like(key_acc)
        value_acc[...] = jnp.zeros_like(value_acc)
        out_ref[:, 0:PAIR] = jnp.zeros((out_ref.shape[0], PAIR), BF16)

    def segment(e, carry):
        base = pl.multiple_of(e * SEG, SEG)
        place = pl.multiple_of((e - first) * SEG, SEG)
        extra = key_blocks(info_ref, e)
        keys = qkv_ref[pl.ds(base, SEG), PAIR : 2 * PAIR]
        values = qkv_ref[pl.ds(base, SEG), 2 * PAIR : 3 * PAIR]
        key_t = keys.T
        extra_keys = jnp.concatenate(
            [qkv_ref[pl.ds(pl.multiple_of(s, TAIL), TAIL), PAIR : 2 * PAIR] for s, _ in extra],
            axis=0,
        )
        extra_values = jnp.concatenate(
            [qkv_ref[pl.ds(pl.multiple_of(s, TAIL), TAIL), 2 * PAIR : 3 * PAIR] for s, _ in extra],
            axis=0,
        )
        extra_key_t = extra_keys.T
        for qb in range(SEG // QB):
            here = pl.ds(base + qb * QB, QB)
            query = qkv_ref[here, 0:PAIR]
            grad = grad_ref[pl.ds(place + qb * QB, QB), :]
            both = (grad.astype(F32) * mix_ref[pl.ds(place + qb * QB, QB), :].astype(F32)).T
            seen = (qb + 1) * QB
            key_own, value_own, key_far, value_far = 0.0, 0.0, 0.0, 0.0
            query_grads = []
            for h in range(2):
                rows = slice(h * HD, (h + 1) * HD)
                qh, gh = head_only(query, h), head_only(grad, h)
                centre = jnp.sum(both[rows], axis=0, keepdims=True)
                log = log_ref[0, e - first, h : h + 1, qb * QB : (qb + 1) * QB]
                own = dot_nt(keys[:seen], qh)
                parts = [own[: qb * QB]] if qb else []
                parts.append(causal(own[qb * QB :]))
                own = jnp.exp((jnp.concatenate(parts, axis=0) if qb else parts[0]) - log)
                far = dot_nt(extra_keys, qh)
                far = jnp.concatenate(
                    [
                        hide_rows(far[n * TAIL : (n + 1) * TAIL], hidden)
                        for n, (_, hidden) in enumerate(extra)
                    ],
                    axis=0,
                )
                far = jnp.exp(far - log)
                own_step = (own * (dot_nt(values[:seen], gh) - centre)).astype(BF16)
                far_step = (far * (dot_nt(extra_values, gh) - centre)).astype(BF16)
                value_own += dot(own.astype(BF16), gh)
                value_far += dot(far.astype(BF16), gh)
                key_own += dot(own_step, qh)
                key_far += dot(far_step, qh)
                query_grads.append(dot(key_t[rows, :seen], own_step) + dot(extra_key_t[rows], far_step))
            query_grad = jnp.concatenate(query_grads, axis=0).T * (HD**-0.5)
            out_ref[here, 0:PAIR] = query_grad.astype(BF16)
            key_acc[pl.ds(base, seen), :] += key_own
            value_acc[pl.ds(base, seen), :] += value_own
            for n, (s, _) in enumerate(extra):
                there = pl.ds(pl.multiple_of(s, TAIL), TAIL)
                key_acc[there, :] += key_far[n * TAIL : (n + 1) * TAIL]
                value_acc[there, :] += value_far[n * TAIL : (n + 1) * TAIL]
        return carry

    lax.fori_loop(first, first + count, segment, 0)
    out_ref[:, PAIR : 2 * PAIR] = key_acc[...].astype(BF16)
    out_ref[:, 2 * PAIR : 3 * PAIR] = value_acc[...].astype(BF16)


def attend_back(info, qkv, mixture, grad, logs, first, count, before=None):
    pieces = qkv.shape[1] // (3 * PAIR)
    rows = count * SEG
    wide = pl.BlockSpec((qkv.shape[0], 3 * PAIR), lambda r, t: (0, r))
    narrow = pl.BlockSpec((rows, PAIR), lambda r, t: (0, r))
    more = () if before is None else (before,)
    return pl.pallas_call(
        functools.partial(attend_back_kernel, first, count),
        grid_spec=pltpu.PrefetchScalarGridSpec(
            num_scalar_prefetch=1,
            grid=(pieces,),
            in_specs=[
                wide,
                narrow,
                narrow,
                pl.BlockSpec((1, count, 2, SEG), lambda r, t: (r, 0, 0, 0)),
            ]
            + [wide] * len(more),
            out_specs=wide,
            scratch_shapes=[
                pltpu.VMEM((qkv.shape[0], PAIR), F32),
                pltpu.VMEM((qkv.shape[0], PAIR), F32),
            ],
        ),
        out_shape=jax.ShapeDtypeStruct(qkv.shape, BF16),
        compiler_params=pltpu.CompilerParams(vmem_limit_bytes=56 * 1024 * 1024),
        cost_estimate=LIGHT,
        name="attend_back",
    )(info, qkv, mixture, grad, logs, *more)


def weight_grad_kernel(order_ref, *refs):
    out_ref = refs[-1]
    total = None
    for left, right in zip(refs[:-1:2], refs[1:-1:2]):
        term = dot_tn(left[...], right[...])
        total = term if total is None else total + term
    out_ref[...] = total.astype(out_ref.dtype)


def weight_grad(pairs, column=0, columns=None, step=256, order=None):
    height = pairs[0][0].shape[1]
    columns = columns or pairs[0][1].shape[1]
    if order is None:
        order = jnp.arange(height // step, dtype=jnp.int32)
    specs = []
    for left, right, n in pairs:
        specs.append(pl.BlockSpec((left.shape[0], step), lambda i, o: (0, i)))
        specs.append(pl.BlockSpec((left.shape[0], columns), lambda i, o, n=n: (n, column)))
    return pl.pallas_call(
        weight_grad_kernel,
        grid_spec=pltpu.PrefetchScalarGridSpec(
            num_scalar_prefetch=1,
            grid=(height // step,),
            in_specs=specs,
            out_specs=pl.BlockSpec((step, columns), lambda i, o: (o[i], 0)),
        ),
        out_shape=jax.ShapeDtypeStruct((height, columns), BF16),
        compiler_params=pltpu.CompilerParams(vmem_limit_bytes=56 * 1024 * 1024),
        cost_estimate=LIGHT,
        name="weight_grad",
    )(order, *[v for pair in pairs for v in pair[:2]])


def project_kernel(pieces, which_ref, *refs):
    weights, rows, out_ref, first, last = (
        refs[: 2 * pieces],
        refs[2 * pieces : -3],
        refs[-3],
        refs[-2],
        refs[-1],
    )
    depth, block = first.shape[0], first.shape[1] // pieces
    for n in range(pieces):
        first[:, n * block : (n + 1) * block] = weights[2 * n][:depth, :]
        last[:, n * block : (n + 1) * block] = weights[2 * n + 1][:depth, :]
    bias = jnp.concatenate(
        [weights[2 * n][depth : depth + 1, :].astype(F32) for n in range(pieces)], axis=1
    )
    lane = lax.broadcasted_iota(jnp.int32, bias.shape, 1)
    scale = jnp.where(lane % block < PAIR, HD**-0.5, 1.0)
    held = pl.ds(pl.multiple_of(which_ref[0] * depth, depth), depth)
    other = pl.ds(pl.multiple_of((1 - which_ref[0]) * depth, depth), depth)
    at = 0
    for ref in rows:
        chunk = min(256, ref.shape[0])
        for start in range(0, ref.shape[0], chunk):
            here = slice(start, start + chunk)
            value = dot(ref[here, held], first[...]) + dot(ref[here, other], last[...])
            out_ref[at + start : at + start + chunk, :] = ((value + bias) * scale).astype(BF16)
        at += ref.shape[0]


def project(which, weights, rows):
    pieces = len(weights)
    depth, block = rows[0].shape[1] // 2, weights[0][0].shape[1]
    height = sum(v.shape[0] for v in rows)
    return pl.pallas_call(
        functools.partial(project_kernel, pieces),
        grid_spec=pltpu.PrefetchScalarGridSpec(
            num_scalar_prefetch=1,
            grid=(),
            in_specs=[pl.BlockSpec(memory_space=pltpu.VMEM)] * (2 * pieces + len(rows)),
            out_specs=pl.BlockSpec(memory_space=pltpu.VMEM),
            scratch_shapes=[pltpu.VMEM((depth, pieces * block), BF16)] * 2,
        ),
        out_shape=jax.ShapeDtypeStruct((height, pieces * block), BF16),
        compiler_params=pltpu.CompilerParams(vmem_limit_bytes=56 * 1024 * 1024),
        cost_estimate=LIGHT,
        name="project",
    )(which, *[v for pair in weights for v in pair], *rows)


def matmul_kernel(transposed, left_ref, right_ref, *rest):
    out_ref = rest[-1]
    chunk = min(256, left_ref.shape[0])
    for start in range(0, left_ref.shape[0], chunk):
        rows = slice(start, start + chunk)
        value = (dot_nt if transposed else dot)(left_ref[rows, :], right_ref[...])
        if len(rest) == 2:
            value = value * rest[0][rows, :].astype(F32)
        out_ref[rows, :] = value.astype(BF16)


def matmul(left, right, transposed, scale=None, place=0, rows=None, step=512):
    rows = rows or left.shape[0]
    depth = left.shape[1]
    columns = right.shape[0] if transposed else right.shape[1]
    right_spec = (
        pl.BlockSpec((step, depth), lambda i: (i, 0))
        if transposed
        else pl.BlockSpec((depth, step), lambda i: (0, i))
    )
    out_spec = pl.BlockSpec((rows, step), lambda i: (0, i))
    more = () if scale is None else (scale,)
    return pl.pallas_call(
        functools.partial(matmul_kernel, transposed),
        grid=(columns // step,),
        in_specs=[pl.BlockSpec((rows, depth), lambda i: (place, 0)), right_spec]
        + [out_spec] * len(more),
        out_specs=out_spec,
        out_shape=jax.ShapeDtypeStruct((rows, columns), BF16),
        compiler_params=pltpu.CompilerParams(vmem_limit_bytes=56 * 1024 * 1024),
        cost_estimate=LIGHT,
        name="matmul",
    )(left, right, *more)


def body(
    inputs,
    item_counts,
    first_gain,
    first_shift,
    query_weight,
    query_bias,
    key_weight,
    value_weight,
    value_bias,
    output_weight,
    output_bias,
    second_gain,
    second_shift,
    expand_weight,
    expand_bias,
    contract_weight,
    contract_bias,
    cotangent,
):
    n_mp, n_dp = lax.axis_size("mp"), lax.axis_size("dp")
    teams = n_mp // TEAM
    me = lax.axis_index("mp")
    team, mine = me // TEAM, me % TEAM
    second = lax.axis_index("dp") % 2

    def core_swap(v):
        return lax.ppermute(v, "mp", [(i, i ^ 1) for i in range(n_mp)])

    def chip_swap(v):
        return lax.ppermute(v, "mp", [(i, i ^ 2) for i in range(n_mp)])

    def ring_up(v, by=1):
        return lax.ppermute(v, "mp", [(i, (i + by * TEAM) % n_mp) for i in range(n_mp)])

    def ring_down(v):
        return lax.ppermute(v, "mp", [(i, (i - TEAM) % n_mp) for i in range(n_mp)])

    def line_up(v, by=1):
        return lax.ppermute(v, "mp", [(i, i + by * TEAM) for i in range(n_mp - by * TEAM)])

    def line_down(v, by=1):
        return lax.ppermute(v, "mp", [(i + by * TEAM, i) for i in range(n_mp - by * TEAM)])

    def group_swap(v, bit=1):
        return lax.ppermute(v, "dp", [(i, i ^ bit) for i in range(n_dp)])

    def half(v, axis, which):
        size = v.shape[axis] // 2
        return lax.dynamic_slice_in_dim(v, which * size, size, axis)

    def ordered(held, other, axis):
        return jnp.where(
            second == 0,
            jnp.concatenate([held, other], axis=axis),
            jnp.concatenate([other, held], axis=axis),
        )

    def add(*terms):
        return functools.reduce(jnp.add, [t.astype(F32) for t in terms]).astype(BF16)

    def other_groups(v):
        bit = 2
        while bit < n_dp:
            v = add(v, group_swap(v, bit))
            bit *= 2
        return v

    def sync(*values):
        return lax.optimization_barrier(values)

    slot_count = teams * TEAM
    items = slot_items(item_counts[0], slot_count)
    info = jnp.pad(items, (0, 2))
    at = lax.iota(jnp.int32, slot_count + 2)
    info = jnp.where(at == slot_count, team, jnp.where(at == slot_count + 1, mine, info))

    gain_first, shift_first = first_gain.astype(F32), first_shift.astype(F32)
    gain_second, shift_second = second_gain.astype(F32), second_shift.astype(F32)
    width = inputs.shape[1]
    cols = query_bias.shape[0]
    hid = expand_bias.shape[0]
    wide = hid // 2
    team_rows, near_rows = TEAM * SEG, 2 * SEG
    span = TEAM * TAIL
    block = 3 * PAIR
    pad = 16

    def with_bias(weight, bias):
        return jnp.concatenate(
            [weight, jnp.broadcast_to(bias[None], (pad, bias.shape[0]))], axis=0
        )

    def send_in(terms):
        size = terms.shape[0] // 2
        return add(terms[:size], core_swap(terms[size:]))

    def shard_halves(v):
        return [
            [v[:, (2 * r + k) * wide : (2 * r + k + 1) * wide] for k in range(2)]
            for r in range(teams)
        ]

    part = SEG // 2
    pairs_along = [
        [(first + d) * n_mp + t * TEAM + i for t in range(teams) for d in range(2)]
        for first in range(0, n_dp, 2)
        for i in range(TEAM)
    ]

    def scatter_sum(v):
        return lax.psum_scatter(
            v, ("dp", "mp"), scatter_dimension=0, axis_index_groups=pairs_along, tiled=True
        )

    def cat(*parts, axis=0):
        return jnp.concatenate(parts, axis=axis)

    qkv_local = cat(query_weight, key_weight, value_weight, axis=1)
    qkv_bias_local = cat(query_bias, jnp.zeros_like(query_bias), value_bias)
    packed = with_bias(half(qkv_local, 0, second), qkv_bias_local)
    q0_o = half(qkv_local, 0, 1 - second)
    hidden_in = inputs.astype(F32)
    normed = normalize(hidden_in, gain_first, shift_first).astype(BF16)
    packed, normed = sync(packed, normed)
    q1 = ring_up(packed)
    normed_xa = chip_swap(normed[:part])
    normed_c = core_swap(normed)
    early = line_up(normed[SEG - TAIL :])
    earlier = line_up(normed[SEG - TAIL :], 2)
    q1, normed_xa, normed_c, early, earlier, normed = sync(
        q1, normed_xa, normed_c, early, earlier, normed
    )
    q2 = ring_up(q1)
    q1_o = group_swap(q1)
    normed_xb = chip_swap(normed[part:])
    rest = cat(early, earlier)
    rest_x = chip_swap(rest)
    rest_c = core_swap(rest)
    q2, q1_o, normed_xb, rest_x, rest_c, cot = sync(q2, q1_o, normed_xb, rest_x, rest_c, cotangent)
    q3 = ring_up(q2)
    q2_o = group_swap(q2)
    normed_x = cat(normed_xa, normed_xb)
    normed_xc = core_swap(normed_x)
    rest_xc = core_swap(rest_x)
    cot_xa = chip_swap(cot[:part])
    tops = width // 2
    out_half = half(output_weight, 0, second)
    q3, q2_o, normed_xc, rest_xc, cot_xa, cot_late, out_half, expand_weight, expand_bias = sync(
        q3, q2_o, normed_xc, rest_xc, cot_xa, cot, out_half, expand_weight, expand_bias
    )
    q3_o = group_swap(q3)
    out_h = [ring_up(out_half, r) for r in range(1, teams)]
    cot_xb = chip_swap(cot_late[part:])
    row_blocks = [normed, normed_c, normed_x, normed_xc, rest, rest_c, rest_x, rest_xc]
    which = jnp.reshape(second, (1,)).astype(jnp.int32)
    qkv_a = project(which, [(packed, q0_o), (q1, q1_o), (q2, q2_o)], row_blocks)
    expand_own, expand_rest = half(expand_weight, 1, second), half(expand_weight, 1, 1 - second)
    expand_bias_own = half(expand_bias, 0, second)
    expand_bias_rest = half(expand_bias, 0, 1 - second)
    q3_o, cot_xb, qkv_a, e0, cot_late, *out_h = sync(
        q3_o, cot_xb, qkv_a, with_bias(expand_own, expand_bias_own), cot_late, *out_h
    )
    e1 = ring_up(e0)
    out_o = group_swap(cat(*out_h))
    cot_c = core_swap(cot_late)
    mix_far_a, log_far_a = attend(info, qkv_a, 2, 2)
    e1, out_o, cot_c, mix_far_a, cot_x = sync(e1, out_o, cot_c, mix_far_a, cat(cot_xa, cot_xb))
    e2 = ring_up(e1)
    e1_o = group_swap(e1)
    cot_xc = core_swap(cot_x)
    qkv_b = project(which, [(q3, q3_o)], row_blocks)
    mix_far_b, log_far_b = attend(info, qkv_b, 2, 2)
    quarter = cols // 2
    out_all = cat(
        output_weight,
        *[ordered(v, out_o[r * quarter : (r + 1) * quarter], 0) for r, v in enumerate(out_h)],
    )
    mix_far = cat(mix_far_a, mix_far_b, axis=1)
    far = matmul(mix_far, out_all, False)
    e2, e1_o, cot_xc, qkv_b, far, out_all, contract_weight = sync(
        e2, e1_o, cot_xc, qkv_b, far, out_all, contract_weight
    )
    far_c = core_swap(far[SEG:])
    far, far_c, qkv_a = sync(far, far_c, qkv_a)
    branch_in = add(far[:SEG], far_c)
    branch_xa = chip_swap(branch_in[:part])
    e3 = ring_up(e2)
    e2_o = group_swap(e2)
    mix_near_a, log_near_a = attend(info, qkv_a, 0, 2)
    contract_own = half(contract_weight, 0, second)
    contract_rest = half(contract_weight, 0, 1 - second)
    branch_xa, e3, e2_o, mix_near_a, branch_in, contract_own, qkv_b = sync(
        branch_xa, e3, e2_o, mix_near_a, branch_in, contract_own, qkv_b
    )
    branch_xb = chip_swap(branch_in[part:])
    k1 = ring_up(contract_own)
    e3_o = group_swap(e3)
    mix_near_b, log_near_b = attend(info, qkv_b, 0, 2)
    mix_near = cat(mix_near_a, mix_near_b, axis=1)
    near = matmul(mix_near, out_all, False)
    branch_xb, k1, e3_o, near, mix_near = sync(branch_xb, k1, e3_o, near, mix_near)
    near_c = core_swap(near[SEG:])
    near, near_c, k1 = sync(near, near_c, k1)
    branch_x = cat(branch_xa, branch_xb)
    branch = near[:SEG].astype(F32) + near_c.astype(F32) + branch_x.astype(F32)
    middle = hidden_in + branch + output_bias.astype(F32)
    normed_two = normalize(middle, gain_second, shift_second).astype(BF16)
    normed_two, k1, e3_o = sync(normed_two, k1, e3_o)
    two_xa = chip_swap(normed_two[:part])
    two_c = core_swap(normed_two)
    k2 = ring_up(k1)
    k1_o = group_swap(k1)
    expand_pairs = (e1, e1_o, e2, e2_o, e3, e3_o)
    expand_all = cat(expand_own, expand_rest, *[v[:width] for v in expand_pairs], axis=1)
    expand_bias_all = cat(
        expand_bias_own, expand_bias_rest, *[v[width] for v in expand_pairs]
    ).astype(F32)
    two_xa, two_c, k2, k1_o, expand_all, expand_bias_all, normed_two = sync(
        two_xa, two_c, k2, k1_o, expand_all, expand_bias_all, normed_two
    )
    two_xb = chip_swap(normed_two[part:])
    k3 = ring_up(k2)
    k2_o = group_swap(k2)

    def front(rows):
        value, slope = gelu_and_slope(dot(rows, expand_all) + expand_bias_all)
        return value.astype(BF16), slope.astype(BF16)

    two_near = cat(normed_two, two_c)
    active_near, slope_near = front(two_near)
    two_xb, k3, k2_o, active_near, slope_near, two_near = sync(
        two_xb, k3, k2_o, active_near, slope_near, two_near
    )
    two_x = cat(two_xa, two_xb)
    two_xc = core_swap(two_x)
    two_xc, k3, qkv_a, qkv_b, cot_c = sync(two_xc, k3, qkv_a, qkv_b, cot_c)
    k3_o = group_swap(k3)
    two_far = cat(two_x, two_xc)
    active_far, slope_far = front(two_far)
    qkv = cat(qkv_a, qkv_b, axis=1)
    k3_o, active_far, slope_far, two_far, cot_x, q0_o = sync(
        k3_o, active_far, slope_far, two_far, cot_x, q0_o
    )
    contract_all = cat(contract_own, contract_rest, k1, k1_o, k2, k2_o, k3, k3_o)
    cot_far = cat(cot_x, cot_xc)
    before_far = matmul(cot_far, contract_all, True, slope_far)
    far = matmul(before_far, expand_all, True)
    far, before_far, contract_all = sync(far, before_far, contract_all)
    far_c = core_swap(far[SEG:])
    cot_near = cat(cot, cot_c)
    far, far_c, cot_near, slope_near = sync(far, far_c, cot_near, slope_near)
    two_grad_in = add(far[:SEG], far_c)
    two_grad_xa = chip_swap(two_grad_in[:part])
    before_near = matmul(cot_near, contract_all, True, slope_near)
    near = matmul(before_near, expand_all, True)
    two_grad_xa, two_grad_in, before_near, near, active_near = sync(
        two_grad_xa, two_grad_in, before_near, near, active_near
    )
    two_grad_xb = chip_swap(two_grad_in[part:])
    hidden_order = []
    for r in range(teams):
        owner = (team + teams - r) % teams
        hidden_order += [owner * 2 + second, owner * 2 + 1 - second]
    hidden_order = jnp.stack(hidden_order).astype(jnp.int32)
    contract_grad = weight_grad(
        [(active_near, cot_near, 0), (active_far, cot_far, 0)], step=wide, order=hidden_order
    )
    two_grad_xb, contract_grad, near = sync(two_grad_xb, contract_grad, near)
    contract_mine = scatter_sum(contract_grad)
    near_c = core_swap(near[SEG:])
    near, near_c, two_grad_xb = sync(near, near_c, two_grad_xb)
    normed_two_grad = (
        near[:SEG].astype(F32)
        + near_c.astype(F32)
        + cat(two_grad_xa, two_grad_xb).astype(F32)
    )
    cot_local = cotangent.astype(F32)
    _, pull_second = jax.vjp(normalize, middle, gain_second, shift_second)
    middle_part, second_gain_grad, second_shift_grad = pull_second(normed_two_grad)
    middle_grad = cot_local + middle_part
    middle_low, before_near, active_far = sync(middle_grad.astype(BF16), before_near, active_far)
    middle_xa = chip_swap(middle_low[:part])
    middle_c = core_swap(middle_low)
    expand_grad = weight_grad([(two_near, before_near, 0), (two_far, before_far, 0)])
    middle_xa, middle_c, expand_grad, middle_low = sync(
        middle_xa, middle_c, expand_grad, middle_low
    )
    middle_xb = chip_swap(middle_low[part:])
    halves = shard_halves(expand_grad)
    s3_o = group_swap(halves[3][1])
    s2_o = group_swap(halves[2][1])
    middle_near = cat(middle_low, middle_c)
    mix_grad_near = matmul(middle_near, out_all, True)
    log_near = cat(log_near_a, log_near_b)
    part_grad = attend_back(info, qkv, mix_near, mix_grad_near, log_near, 0, 2)
    two_far_branch = matmul(active_far, contract_all, False)
    middle_xb, s3_o, s2_o, part_grad, expand_grad, middle_near, two_far_branch, q0_late = sync(
        middle_xb, s3_o, s2_o, part_grad, expand_grad, middle_near, two_far_branch, q0_o
    )
    middle_x = cat(middle_xa, middle_xb)
    middle_xc = core_swap(middle_x)
    out_c = core_swap(two_far_branch[SEG:])
    middle_xc, out_c, expand_grad = sync(middle_xc, out_c, expand_grad)
    halves = shard_halves(expand_grad)
    two_branch_x = chip_swap(add(two_far_branch[:SEG], out_c))
    s1_o = group_swap(halves[1][1])
    s0_o = group_swap(halves[0][1])
    a3 = ring_down(add(halves[3][0], s3_o))
    middle_far = cat(middle_x, middle_xc)
    mix_grad_far = matmul(middle_far, out_all, True)
    log_far = cat(log_far_a, log_far_b)
    qkv_grad = attend_back(info, qkv, mix_far, mix_grad_far, log_far, 2, 2, part_grad)
    qkv_all = cat(
        *[
            ordered(v[:tops], o, 0)
            for v, o in ((packed, q0_late), (q1, q1_o[:tops]), (q2, q2_o[:tops]), (q3, q3_o[:tops]))
        ],
        axis=1,
    )
    far = matmul(qkv_grad, qkv_all, True, place=1, rows=near_rows)
    s1_o, s0_o, a3, far, qkv_grad, expand_grad, middle_far, contract_mine, two_branch_x = sync(
        s1_o, s0_o, a3, far, qkv_grad, expand_grad, middle_far, contract_mine, two_branch_x
    )
    far_c = core_swap(far[SEG:])
    far, far_c, qkv_grad = sync(far, far_c, qkv_grad)

    def turn(v, by):
        shift = (by % teams) * block
        return cat(v[:, shift:], v[:, :shift], axis=1) if shift else v

    normed_in = add(far[:SEG], far_c)
    normed_ga = chip_swap(normed_in[:part])
    far_rows = qkv_grad[team_rows:].reshape(TEAM, 2, TAIL, -1)
    one = line_down(far_rows[:, 0].reshape(span, -1))
    two = line_down(far_rows[:, 1].reshape(span, -1), 2)
    contract_sum = other_groups(contract_mine)
    contract_other = group_swap(contract_sum)
    grad_pairs = [
        (v, qkv_grad, n)
        for n, v in enumerate([normed, normed_c, normed_x, normed_xc, cat(rest, rest_c, rest_x, rest_xc)])
    ]
    last_grad = weight_grad(grad_pairs, 1, 2 * block)
    near = matmul(qkv_grad, qkv_all, True, place=0, rows=near_rows)
    place_order = jnp.stack([(team + teams - r) % teams for r in range(teams)]).astype(jnp.int32)
    out_grad = weight_grad(
        [(mix_near, middle_near, 0), (mix_far, middle_far, 0)], step=cols, order=place_order
    )
    normed_ga, normed_in, one, two, last_grad, near, qkv_grad, contract_other, out_grad = sync(
        normed_ga, normed_in, one, two, last_grad, near, qkv_grad, contract_other, out_grad
    )

    def qkv_halves(v, k):
        piece = v[:, k * block : (k + 1) * block]
        return half(piece, 0, second), half(piece, 0, 1 - second)

    out_mine = scatter_sum(out_grad)
    normed_gb = chip_swap(normed_in[part:])
    kept3, sent3 = qkv_halves(last_grad, 1)
    kept2, sent2 = qkv_halves(last_grad, 0)
    q3_in = group_swap(sent3)
    q2_in = group_swap(sent2)
    near_c = core_swap(near[SEG:])
    late = add(turn(one, 1), turn(two, 2))
    late_terms = matmul(late, qkv_all, True)
    grad_pairs = [(v, qkv_grad, n) for v, _, n in grad_pairs]
    first_grad = weight_grad(grad_pairs, 0, 2 * block)
    normed_gb, q3_in, q2_in, near_c, late_terms, first_grad, expand_grad = sync(
        normed_gb, q3_in, q2_in, near_c, late_terms, first_grad, expand_grad
    )
    late_c, late_cn = core_swap(late_terms[3 * TAIL :]), core_swap(late_terms[TAIL : 2 * TAIL])
    late_c, late_cn, late_terms, first_grad, expand_grad = sync(
        late_c, late_cn, late_terms, first_grad, expand_grad
    )
    late_x = chip_swap(add(late_terms[2 * TAIL : 3 * TAIL], late_c))
    kept1, sent1 = qkv_halves(first_grad, 1)
    kept0, sent0 = qkv_halves(first_grad, 0)
    q1_in = group_swap(sent1)
    qa3 = ring_down(add(kept3, q3_in))
    halves = shard_halves(expand_grad)
    late_x, q1_in, qa3, sent0, expand_grad, active_near = sync(
        late_x, q1_in, qa3, sent0, expand_grad, active_near
    )
    q0_in = group_swap(sent0)
    qa2 = ring_down(add(qa3, add(kept2, q2_in)))
    halves = shard_halves(expand_grad)
    a2 = ring_down(add(a3, add(halves[2][0], s2_o)))
    normed_grad = near[:SEG].astype(F32) + near_c.astype(F32) + cat(normed_ga, normed_gb).astype(F32)
    tail = add(late_terms[:TAIL], late_cn).astype(F32) + late_x.astype(F32)
    normed_grad = normed_grad + cat(jnp.zeros((SEG - TAIL, width), F32), tail)
    _, pull_first = jax.vjp(normalize, hidden_in, gain_first, shift_first)
    input_part, first_gain_grad, first_shift_grad = pull_first(normed_grad)
    input_grad = (middle_grad + input_part).astype(BF16)
    qkv_bias_sums = jnp.sum(qkv_grad.astype(F32), axis=0)
    expand_bias_sums = jnp.sum(before_near.astype(F32), axis=0) + jnp.sum(
        before_far.astype(F32), axis=0
    )
    q0_in, qa2, a2, first_gain_grad, first_shift_grad, expand_grad, active_near = sync(
        q0_in, qa2, a2, first_gain_grad, first_shift_grad, expand_grad, active_near
    )
    halves = shard_halves(expand_grad)
    qa1 = ring_down(add(qa2, add(kept1, q1_in)))
    a1 = ring_down(add(a2, add(halves[1][0], s1_o)))
    two_near_branch = matmul(active_near, contract_all, False)
    expand_mine = other_groups(add(a1, add(halves[0][0], s0_o)))
    expand_other = group_swap(expand_mine)
    qkv_mine = other_groups(add(qa1, add(kept0, q0_in)))
    qkv_other = group_swap(qkv_mine)
    out_sum = other_groups(out_mine)
    out_other = group_swap(out_sum)
    small = jnp.concatenate(
        [
            first_gain_grad,
            first_shift_grad,
            jnp.sum(middle_grad, axis=0),
            second_gain_grad,
            second_shift_grad,
            jnp.sum(cot_local, axis=0),
        ]
    )
    place = block + hid
    owners = jnp.zeros((n_mp * place,), F32)
    for r in range(teams):
        owner = (team + teams - r) % teams
        mine_hid = ordered(
            expand_bias_sums[2 * r * wide : (2 * r + 1) * wide],
            expand_bias_sums[(2 * r + 1) * wide : (2 * r + 2) * wide],
            0,
        )
        piece = jnp.concatenate(
            [qkv_bias_sums[r * block : (r + 1) * block], mine_hid]
        )
        owners = lax.dynamic_update_slice(owners, piece, ((owner * TEAM + mine) * place,))

    def total(v, axes):
        for axis, size in axes:
            bit = 1
            while bit < size:
                v = v + lax.ppermute(v, axis, [(i, i ^ bit) for i in range(size)])
                bit *= 2
        return v

    vector = total(jnp.concatenate([small, owners]), (("mp", n_mp), ("dp", n_dp)))
    mine_spot = lax.dynamic_slice(vector, (6 * width + me * place,), (place,))
    six = [vector[k * width : (k + 1) * width] for k in range(6)]

    branch_two = (
        two_near_branch[:SEG].astype(F32)
        + core_swap(two_near_branch[SEG:]).astype(F32)
        + two_branch_x.astype(F32)
    )
    layer_out = (middle + branch_two + contract_bias.astype(F32)).astype(BF16)
    qkv_final = ordered(qkv_mine, qkv_other, 0).astype(F32)
    return (
        layer_out,
        input_grad,
        six[0],
        six[1],
        qkv_final[:, :cols],
        mine_spot[:cols],
        qkv_final[:, cols : 2 * cols],
        qkv_final[:, 2 * cols :],
        mine_spot[2 * cols : 3 * cols],
        ordered(out_sum, out_other, 0).astype(F32),
        six[2],
        six[3],
        six[4],
        ordered(expand_mine, expand_other, 1).astype(F32),
        mine_spot[block:],
        ordered(contract_sum, contract_other, 0).astype(F32),
        six[5],
    )


def solution(mesh):
    rows = P(("dp", "mp"), None)
    in_cols, in_rows = P(None, "mp"), P("mp", None)
    placed = (
        rows,
        P("dp", None),
        P(),
        P(),
        in_cols,
        P("mp"),
        in_cols,
        in_cols,
        P("mp"),
        in_rows,
        P(),
        P(),
        P(),
        in_cols,
        P("mp"),
        in_rows,
        P(),
        rows,
    )
    return jax.shard_map(
        body,
        mesh=mesh,
        in_specs=placed,
        out_specs=(
            rows,
            rows,
            P(),
            P(),
            in_cols,
            P("mp"),
            in_cols,
            in_cols,
            P("mp"),
            in_rows,
            P(),
            P(),
            P(),
            in_cols,
            P("mp"),
            in_rows,
            P(),
        ),
        check_vma=False,
    )
```

```python
import functools

import jax
import jax.numpy as jnp
from jax import lax
from jax.experimental import pallas as pl
from jax.experimental.pallas import tpu as pltpu
from jax.sharding import PartitionSpec as P

HD = 64
SEG = 512
NSUM = 50
TAIL = 64
TEAM = 4
PAIR = 2 * HD
QB = 256
EPSILON = 1e-05
MASKED = -1e30
LIGHT = pl.CostEstimate(flops=1024, bytes_accessed=1024, transcendentals=0)
F32 = jnp.float32
BF16 = jnp.bfloat16


def gelu_and_slope(v):
    inner = 0.7978845608 * (v + 0.044715 * v * v * v)
    t = jnp.tanh(inner)
    value = 0.5 * v * (1.0 + t)
    slope = 0.5 * (1.0 + t) + 0.5 * v * (1.0 - t * t) * (
        0.7978845608 * (1.0 + 3.0 * 0.044715 * v * v)
    )
    return value, slope


def normalize(values, scaling, offset):
    centre = jnp.mean(values, axis=-1, keepdims=True)
    centred = values - centre
    spread = jnp.mean(centred * centred, axis=-1, keepdims=True)
    return centred * lax.rsqrt(spread + EPSILON) * scaling + offset


def slot_items(counts, slot_count):
    item_ends = jnp.cumsum(counts)
    places = jnp.arange(slot_count, dtype=jnp.int32)
    return jnp.sum((places[:, None] >= item_ends[None, :]).astype(jnp.int32), axis=1)


def dot(a, b):
    return jnp.dot(a, b, preferred_element_type=F32)


def dot_nt(a, b):
    return lax.dot_general(a, b, (((1,), (1,)), ((), ())), preferred_element_type=F32)


def dot_tn(a, b):
    return lax.dot_general(a, b, (((0,), (0,)), ((), ())), preferred_element_type=F32)


def head_only(block, h):
    lane = lax.broadcasted_iota(jnp.int32, block.shape, 1)
    return jnp.where((lane // HD) == h, block, jnp.zeros_like(block))


def causal(block):
    key = lax.broadcasted_iota(jnp.int32, block.shape, 0)
    query = lax.broadcasted_iota(jnp.int32, block.shape, 1)
    return jnp.where(query >= key, block, MASKED)


def hide_rows(block, count):
    key = lax.broadcasted_iota(jnp.int32, block.shape, 0)
    return jnp.where(key >= count, block, MASKED)


def key_blocks(info_ref, e):
    slots = info_ref.shape[0] - 2
    team, mine = info_ref[slots], info_ref[slots + 1]
    i = mine ^ e
    item = info_ref[team * TEAM + i]

    def hidden(other):
        same = info_ref[jnp.maximum(other, 0)] == item
        return jnp.where(jnp.logical_and(other >= 0, same), TAIL - NSUM, TAIL)

    rows = TEAM * SEG
    out = [(rows + 2 * f * TAIL, hidden((team - 1) * TEAM + (mine ^ f))) for f in range(TEAM)]
    for d in range(1, TEAM):
        j = i ^ d
        inside = j < i
        start = jnp.where(
            inside, (e ^ d) * SEG + SEG - TAIL, rows + (2 * (e ^ d) + 1) * TAIL
        )
        out.append((start, hidden(jnp.where(inside, team, team - 2) * TEAM + j)))
    return out


def attend_kernel(first, count, info_ref, qkv_ref, mix_ref, log_ref):
    def segment(e, carry):
        base = pl.multiple_of(e * SEG, SEG)
        place = pl.multiple_of((e - first) * SEG, SEG)
        extra = key_blocks(info_ref, e)
        keys = qkv_ref[pl.ds(base, SEG), PAIR : 2 * PAIR]
        value_t = qkv_ref[pl.ds(base, SEG), 2 * PAIR : 3 * PAIR].T
        extra_keys = [
            qkv_ref[pl.ds(pl.multiple_of(s, TAIL), TAIL), PAIR : 2 * PAIR] for s, _ in extra
        ]
        extra_values = [
            qkv_ref[pl.ds(pl.multiple_of(s, TAIL), TAIL), 2 * PAIR : 3 * PAIR] for s, _ in extra
        ]
        extra_keys = jnp.concatenate(extra_keys, axis=0)
        extra_value_t = jnp.concatenate(extra_values, axis=0).T
        for qb in range(SEG // QB):
            query = qkv_ref[pl.ds(base + qb * QB, QB), 0:PAIR]
            seen = (qb + 1) * QB
            outs = []
            for h in range(2):
                qh = head_only(query, h)
                own = dot_nt(keys[:seen], qh)
                parts = [own[: qb * QB]] if qb else []
                parts.append(causal(own[qb * QB :]))
                far = dot_nt(extra_keys, qh)
                for n, (_, hidden) in enumerate(extra):
                    parts.append(hide_rows(far[n * TAIL : (n + 1) * TAIL], hidden))
                high = functools.reduce(
                    jnp.maximum, [jnp.max(p, axis=0, keepdims=True) for p in parts]
                )
                parts = [jnp.exp(p - high) for p in parts]
                total = functools.reduce(
                    jnp.add, [jnp.sum(p, axis=0, keepdims=True) for p in parts]
                )
                cut = 2 if qb else 1
                p_own = jnp.concatenate([p.astype(BF16) for p in parts[:cut]], axis=0)
                p_far = jnp.concatenate([p.astype(BF16) for p in parts[cut:]], axis=0)
                rows = slice(h * HD, (h + 1) * HD)
                mixed = dot(value_t[rows, :seen], p_own) + dot(extra_value_t[rows], p_far)
                outs.append(mixed / total)
                log_ref[0, e - first, h : h + 1, qb * QB : (qb + 1) * QB] = high + jnp.log(total)
            mix_ref[pl.ds(place + qb * QB, QB), :] = jnp.concatenate(outs, axis=0).T.astype(BF16)
        return carry

    lax.fori_loop(first, first + count, segment, 0)


def attend(info, qkv, first, count):
    pieces = qkv.shape[1] // (3 * PAIR)
    rows = count * SEG
    return pl.pallas_call(
        functools.partial(attend_kernel, first, count),
        grid_spec=pltpu.PrefetchScalarGridSpec(
            num_scalar_prefetch=1,
            grid=(pieces,),
            in_specs=[pl.BlockSpec((qkv.shape[0], 3 * PAIR), lambda r, t: (0, r))],
            out_specs=[
                pl.BlockSpec((rows, PAIR), lambda r, t: (0, r)),
                pl.BlockSpec((1, count, 2, SEG), lambda r, t: (r, 0, 0, 0)),
            ],
        ),
        out_shape=[
            jax.ShapeDtypeStruct((rows, pieces * PAIR), BF16),
            jax.ShapeDtypeStruct((pieces, count, 2, SEG), F32),
        ],
        compiler_params=pltpu.CompilerParams(vmem_limit_bytes=56 * 1024 * 1024),
        cost_estimate=LIGHT,
        name="attend",
    )(info, qkv)


def attend_back_kernel(first, count, info_ref, qkv_ref, mix_ref, grad_ref, log_ref, *rest):
    out_ref, key_acc, value_acc = rest[-3:]
    if len(rest) == 4:
        before_ref = rest[0]
        key_acc[...] = before_ref[:, PAIR : 2 * PAIR].astype(F32)
        value_acc[...] = before_ref[:, 2 * PAIR : 3 * PAIR].astype(F32)
        out_ref[:, 0:PAIR] = before_ref[:, 0:PAIR]
    else:
        key_acc[...] = jnp.zeros_like(key_acc)
        value_acc[...] = jnp.zeros_like(value_acc)
        out_ref[:, 0:PAIR] = jnp.zeros((out_ref.shape[0], PAIR), BF16)

    def segment(e, carry):
        base = pl.multiple_of(e * SEG, SEG)
        place = pl.multiple_of((e - first) * SEG, SEG)
        extra = key_blocks(info_ref, e)
        keys = qkv_ref[pl.ds(base, SEG), PAIR : 2 * PAIR]
        values = qkv_ref[pl.ds(base, SEG), 2 * PAIR : 3 * PAIR]
        key_t = keys.T
        extra_keys = jnp.concatenate(
            [qkv_ref[pl.ds(pl.multiple_of(s, TAIL), TAIL), PAIR : 2 * PAIR] for s, _ in extra],
            axis=0,
        )
        extra_values = jnp.concatenate(
            [qkv_ref[pl.ds(pl.multiple_of(s, TAIL), TAIL), 2 * PAIR : 3 * PAIR] for s, _ in extra],
            axis=0,
        )
        extra_key_t = extra_keys.T
        for qb in range(SEG // QB):
            here = pl.ds(base + qb * QB, QB)
            query = qkv_ref[here, 0:PAIR]
            grad = grad_ref[pl.ds(place + qb * QB, QB), :]
            both = (grad.astype(F32) * mix_ref[pl.ds(place + qb * QB, QB), :].astype(F32)).T
            seen = (qb + 1) * QB
            key_own, value_own, key_far, value_far = 0.0, 0.0, 0.0, 0.0
            query_grads = []
            for h in range(2):
                rows = slice(h * HD, (h + 1) * HD)
                qh, gh = head_only(query, h), head_only(grad, h)
                centre = jnp.sum(both[rows], axis=0, keepdims=True)
                log = log_ref[0, e - first, h : h + 1, qb * QB : (qb + 1) * QB]
                own = dot_nt(keys[:seen], qh)
                parts = [own[: qb * QB]] if qb else []
                parts.append(causal(own[qb * QB :]))
                own = jnp.exp((jnp.concatenate(parts, axis=0) if qb else parts[0]) - log)
                far = dot_nt(extra_keys, qh)
                far = jnp.concatenate(
                    [
                        hide_rows(far[n * TAIL : (n + 1) * TAIL], hidden)
                        for n, (_, hidden) in enumerate(extra)
                    ],
                    axis=0,
                )
                far = jnp.exp(far - log)
                own_step = (own * (dot_nt(values[:seen], gh) - centre)).astype(BF16)
                far_step = (far * (dot_nt(extra_values, gh) - centre)).astype(BF16)
                value_own += dot(own.astype(BF16), gh)
                value_far += dot(far.astype(BF16), gh)
                key_own += dot(own_step, qh)
                key_far += dot(far_step, qh)
                query_grads.append(dot(key_t[rows, :seen], own_step) + dot(extra_key_t[rows], far_step))
            query_grad = jnp.concatenate(query_grads, axis=0).T * (HD**-0.5)
            out_ref[here, 0:PAIR] = query_grad.astype(BF16)
            key_acc[pl.ds(base, seen), :] += key_own
            value_acc[pl.ds(base, seen), :] += value_own
            for n, (s, _) in enumerate(extra):
                there = pl.ds(pl.multiple_of(s, TAIL), TAIL)
                key_acc[there, :] += key_far[n * TAIL : (n + 1) * TAIL]
                value_acc[there, :] += value_far[n * TAIL : (n + 1) * TAIL]
        return carry

    lax.fori_loop(first, first + count, segment, 0)
    out_ref[:, PAIR : 2 * PAIR] = key_acc[...].astype(BF16)
    out_ref[:, 2 * PAIR : 3 * PAIR] = value_acc[...].astype(BF16)


def attend_back(info, qkv, mixture, grad, logs, first, count, before=None):
    pieces = qkv.shape[1] // (3 * PAIR)
    rows = count * SEG
    wide = pl.BlockSpec((qkv.shape[0], 3 * PAIR), lambda r, t: (0, r))
    narrow = pl.BlockSpec((rows, PAIR), lambda r, t: (0, r))
    more = () if before is None else (before,)
    return pl.pallas_call(
        functools.partial(attend_back_kernel, first, count),
        grid_spec=pltpu.PrefetchScalarGridSpec(
            num_scalar_prefetch=1,
            grid=(pieces,),
            in_specs=[
                wide,
                narrow,
                narrow,
                pl.BlockSpec((1, count, 2, SEG), lambda r, t: (r, 0, 0, 0)),
            ]
            + [wide] * len(more),
            out_specs=wide,
            scratch_shapes=[
                pltpu.VMEM((qkv.shape[0], PAIR), F32),
                pltpu.VMEM((qkv.shape[0], PAIR), F32),
            ],
        ),
        out_shape=jax.ShapeDtypeStruct(qkv.shape, BF16),
        compiler_params=pltpu.CompilerParams(vmem_limit_bytes=56 * 1024 * 1024),
        cost_estimate=LIGHT,
        name="attend_back",
    )(info, qkv, mixture, grad, logs, *more)


def weight_grad_kernel(splits, halves, pairs, source_ref, target_ref, *refs):
    outs = refs[2 * pairs :]
    total = None
    for left, right in zip(refs[: 2 * pairs : 2], refs[1 : 2 * pairs : 2]):
        term = dot_tn(left[...], right[...])
        total = term if total is None else total + term
    total = total.astype(BF16)
    width = total.shape[1] // splits
    columns = [total[:, k * width : (k + 1) * width] for k in range(splits)]
    if not halves:
        for k in range(splits):
            outs[k][...] = columns[k]
        return
    step, steps = pl.program_id(0), pl.num_programs(0)

    @pl.when(step < steps // 2)
    def _():
        for k in range(splits):
            outs[2 * k][...] = columns[k]

    @pl.when(step >= steps // 2)
    def _():
        for k in range(splits):
            outs[2 * k + 1][...] = columns[k]


def weight_grad(pairs, column=0, columns=None, step=256, splits=1, source=None, target=None, halves=False):
    height = pairs[0][0].shape[1]
    columns = columns or pairs[0][1].shape[1]
    steps, width = height // step, columns // splits
    plain = jnp.arange(steps, dtype=jnp.int32)
    specs = []
    for left, right, n in pairs:
        specs.append(pl.BlockSpec((left.shape[0], step), lambda i, s, t: (0, s[i])))
        specs.append(pl.BlockSpec((left.shape[0], columns), lambda i, s, t, n=n: (n, column)))
    if halves:
        outs = [
            pl.BlockSpec((step, width), lambda i, s, t: (jnp.minimum(i, steps // 2 - 1), 0)),
            pl.BlockSpec((step, width), lambda i, s, t: (jnp.maximum(i - steps // 2, 0), 0)),
        ] * splits
        shapes = [jax.ShapeDtypeStruct((height // 2, width), BF16)] * (2 * splits)
    else:
        outs = [pl.BlockSpec((step, width), lambda i, s, t: (t[i], 0))] * splits
        shapes = [jax.ShapeDtypeStruct((height, width), BF16)] * splits
    return pl.pallas_call(
        functools.partial(weight_grad_kernel, splits, halves, len(pairs)),
        grid_spec=pltpu.PrefetchScalarGridSpec(
            num_scalar_prefetch=2, grid=(steps,), in_specs=specs, out_specs=outs
        ),
        out_shape=shapes,
        compiler_params=pltpu.CompilerParams(vmem_limit_bytes=56 * 1024 * 1024),
        cost_estimate=LIGHT,
        name="weight_grad",
    )(
        plain if source is None else source,
        plain if target is None else target,
        *[v for pair in pairs for v in pair[:2]],
    )


def project_kernel(pieces, which_ref, *refs):
    weights, rows, out_ref, first, last = (
        refs[: 2 * pieces],
        refs[2 * pieces : -3],
        refs[-3],
        refs[-2],
        refs[-1],
    )
    depth, block = first.shape[0], first.shape[1] // pieces
    for n in range(pieces):
        first[:, n * block : (n + 1) * block] = weights[2 * n][:depth, :block]
        last[:, n * block : (n + 1) * block] = weights[2 * n + 1][:depth, :block]
    bias = jnp.concatenate(
        [weights[2 * n][depth : depth + 1, :block].astype(F32) for n in range(pieces)], axis=1
    )
    lane = lax.broadcasted_iota(jnp.int32, bias.shape, 1)
    scale = jnp.where(lane % block < PAIR, HD**-0.5, 1.0)
    held = pl.ds(pl.multiple_of(which_ref[0] * depth, depth), depth)
    other = pl.ds(pl.multiple_of((1 - which_ref[0]) * depth, depth), depth)
    at = 0
    for ref in rows:
        chunk = min(256, ref.shape[0])
        for start in range(0, ref.shape[0], chunk):
            here = slice(start, start + chunk)
            value = dot(ref[here, held], first[...]) + dot(ref[here, other], last[...])
            out_ref[at + start : at + start + chunk, :] = ((value + bias) * scale).astype(BF16)
        at += ref.shape[0]


def project(which, weights, rows):
    pieces = len(weights)
    depth, block = rows[0].shape[1] // 2, 3 * PAIR
    height = sum(v.shape[0] for v in rows)
    return pl.pallas_call(
        functools.partial(project_kernel, pieces),
        grid_spec=pltpu.PrefetchScalarGridSpec(
            num_scalar_prefetch=1,
            grid=(),
            in_specs=[pl.BlockSpec(memory_space=pltpu.VMEM)] * (2 * pieces + len(rows)),
            out_specs=pl.BlockSpec(memory_space=pltpu.VMEM),
            scratch_shapes=[pltpu.VMEM((depth, pieces * block), BF16)] * 2,
        ),
        out_shape=jax.ShapeDtypeStruct((height, pieces * block), BF16),
        compiler_params=pltpu.CompilerParams(vmem_limit_bytes=56 * 1024 * 1024),
        cost_estimate=LIGHT,
        name="project",
    )(which, *[v for pair in weights for v in pair], *rows)


def matmul_kernel(transposed, parts, left_ref, right_ref, *rest):
    outs = rest[-parts:]
    rows = left_ref.shape[0] // parts
    chunk = min(256, rows)
    for start in range(0, left_ref.shape[0], chunk):
        here = slice(start, start + chunk)
        value = (dot_nt if transposed else dot)(left_ref[here, :], right_ref[...])
        if len(rest) > parts:
            value = value * rest[0][here, :].astype(F32)
        at = start % rows
        outs[start // rows][at : at + chunk, :] = value.astype(BF16)


def matmul(left, right, transposed, scale=None, place=0, rows=None, step=512, parts=1):
    rows = rows or left.shape[0]
    depth = left.shape[1]
    columns = right.shape[0] if transposed else right.shape[1]
    right_spec = (
        pl.BlockSpec((step, depth), lambda i: (i, 0))
        if transposed
        else pl.BlockSpec((depth, step), lambda i: (0, i))
    )
    more = () if scale is None else (scale,)
    out = pl.pallas_call(
        functools.partial(matmul_kernel, transposed, parts),
        grid=(columns // step,),
        in_specs=[pl.BlockSpec((rows, depth), lambda i: (place, 0)), right_spec]
        + [pl.BlockSpec((rows, step), lambda i: (0, i))] * len(more),
        out_specs=[pl.BlockSpec((rows // parts, step), lambda i: (0, i))] * parts,
        out_shape=[jax.ShapeDtypeStruct((rows // parts, columns), BF16)] * parts,
        compiler_params=pltpu.CompilerParams(vmem_limit_bytes=56 * 1024 * 1024),
        cost_estimate=LIGHT,
        name="matmul",
    )(left, right, *more)
    return out if parts > 1 else out[0]


def body(
    inputs,
    item_counts,
    first_gain,
    first_shift,
    query_weight,
    query_bias,
    key_weight,
    value_weight,
    value_bias,
    output_weight,
    output_bias,
    second_gain,
    second_shift,
    expand_weight,
    expand_bias,
    contract_weight,
    contract_bias,
    cotangent,
):
    n_mp, n_dp = lax.axis_size("mp"), lax.axis_size("dp")
    teams = n_mp // TEAM
    me = lax.axis_index("mp")
    team, mine = me // TEAM, me % TEAM
    second = lax.axis_index("dp") % 2

    def core_swap(v):
        return lax.ppermute(v, "mp", [(i, i ^ 1) for i in range(n_mp)])

    def chip_swap(v):
        return lax.ppermute(v, "mp", [(i, i ^ 2) for i in range(n_mp)])

    def ring_up(v, by=1):
        return lax.ppermute(v, "mp", [(i, (i + by * TEAM) % n_mp) for i in range(n_mp)])

    def ring_down(v):
        return lax.ppermute(v, "mp", [(i, (i - TEAM) % n_mp) for i in range(n_mp)])

    def line_up(v, by=1):
        return lax.ppermute(v, "mp", [(i, i + by * TEAM) for i in range(n_mp - by * TEAM)])

    def line_down(v, by=1):
        return lax.ppermute(v, "mp", [(i + by * TEAM, i) for i in range(n_mp - by * TEAM)])

    def group_swap(v, bit=1):
        return lax.ppermute(v, "dp", [(i, i ^ bit) for i in range(n_dp)])

    def half(v, axis, which):
        size = v.shape[axis] // 2
        return lax.dynamic_slice_in_dim(v, which * size, size, axis)

    def ordered(held, other, axis):
        return jnp.where(
            second == 0,
            jnp.concatenate([held, other], axis=axis),
            jnp.concatenate([other, held], axis=axis),
        )

    def add(*terms):
        return functools.reduce(jnp.add, [t.astype(F32) for t in terms]).astype(BF16)

    def other_groups(v):
        bit = 2
        while bit < n_dp:
            v = add(v, group_swap(v, bit))
            bit *= 2
        return v

    def sync(*values):
        return lax.optimization_barrier(values)

    slot_count = teams * TEAM
    items = slot_items(item_counts[0], slot_count)
    info = jnp.pad(items, (0, 2))
    at = lax.iota(jnp.int32, slot_count + 2)
    info = jnp.where(at == slot_count, team, jnp.where(at == slot_count + 1, mine, info))

    gain_first, shift_first = first_gain.astype(F32), first_shift.astype(F32)
    gain_second, shift_second = second_gain.astype(F32), second_shift.astype(F32)
    width = inputs.shape[1]
    cols = query_bias.shape[0]
    hid = expand_bias.shape[0]
    wide = hid // 2
    team_rows, near_rows = TEAM * SEG, 2 * SEG
    span = TEAM * TAIL
    block = 3 * PAIR
    pad = 16

    def across_swap(v):
        return lax.ppermute(v, "mp", [(i, i ^ 3) for i in range(n_mp)])

    def with_bias(weight, bias):
        return jnp.concatenate(
            [weight, jnp.broadcast_to(bias[None], (pad, bias.shape[0]))], axis=0
        )

    def send_in(terms):
        size = terms.shape[0] // 2
        return add(terms[:size], core_swap(terms[size:]))

    along = [[t * TEAM + i for t in range(teams)] for i in range(TEAM)]
    part = SEG // 2
    pairs_along = [
        [(first + d) * n_mp + t * TEAM + i for t in range(teams) for d in range(2)]
        for first in range(0, n_dp, 2)
        for i in range(TEAM)
    ]

    def scatter_sum(v):
        return lax.psum_scatter(
            v, ("dp", "mp"), scatter_dimension=0, axis_index_groups=pairs_along, tiled=True
        )

    def cat(*parts, axis=0):
        return jnp.concatenate(parts, axis=axis)

    qkv_local = cat(query_weight, key_weight, value_weight, output_weight.T, axis=1)
    qkv_bias_local = cat(
        query_bias, jnp.zeros_like(query_bias), value_bias, jnp.zeros_like(query_bias)
    )
    packed = with_bias(half(qkv_local, 0, second), qkv_bias_local)
    q0_o = half(qkv_local, 0, 1 - second)
    hidden_in = inputs.astype(F32)
    normed = normalize(hidden_in, gain_first, shift_first).astype(BF16)
    packed, normed = sync(packed, normed)
    q1 = ring_up(packed)
    normed_xa = chip_swap(normed[:part])
    normed_c = core_swap(normed)
    normed_tail, normed_b = normed[SEG - TAIL :], normed[part:]
    q1, normed_xa, normed_c, normed_tail, normed_b = sync(
        q1, normed_xa, normed_c, normed_tail, normed_b
    )
    q2 = ring_up(q1)
    normed_xb = chip_swap(normed_b)
    q1_o = group_swap(q1)
    early = line_up(normed_tail)
    earlier = line_up(normed_tail, 2)
    q2, q1_o, normed_x, rest = sync(q2, q1_o, cat(normed_xa, normed_xb), cat(early, earlier))
    q3 = ring_up(q2)
    q2_o = group_swap(q2)
    normed_xc = core_swap(normed_x)
    rest_x = chip_swap(rest)
    rest_xc = across_swap(rest)
    rest_c = core_swap(rest)
    tops = width // 2
    expand_own, expand_rest = half(expand_weight, 1, second), half(expand_weight, 1, 1 - second)
    expand_bias_own = half(expand_bias, 0, second)
    expand_bias_rest = half(expand_bias, 0, 1 - second)
    q3, q2_o, normed_xc, rest_x, rest_xc, rest_c, cot_a, cot_b, e0 = sync(
        q3,
        q2_o,
        normed_xc,
        rest_x,
        rest_xc,
        rest_c,
        cotangent[:part],
        cotangent[part:],
        with_bias(expand_own, expand_bias_own),
    )
    q3_o = group_swap(q3)
    e1 = ring_up(e0)
    cot_xa = chip_swap(cot_a)
    row_blocks = [normed, normed_c, normed_x, normed_xc, rest, rest_c, rest_x, rest_xc]
    which = jnp.reshape(second, (1,)).astype(jnp.int32)
    qkv_a = project(which, [(packed, q0_o), (q1, q1_o), (q2, q2_o)], row_blocks)
    q3_o, cot_xa, qkv_a, e1, cot_b, cot = sync(q3_o, cot_xa, qkv_a, e1, cot_b, cotangent)
    e2 = ring_up(e1)
    e1_o = group_swap(e1)
    cot_xb = chip_swap(cot_b)
    cot_c = core_swap(cot)
    mix_far_a, log_far_a = attend(info, qkv_a, 2, 2)
    qkv_b = project(which, [(q3, q3_o)], row_blocks)
    mix_far_b, log_far_b = attend(info, qkv_b, 2, 2)
    held_pieces = ((packed, q0_o), (q1, q1_o[:tops]), (q2, q2_o[:tops]), (q3, q3_o[:tops]))
    out_all = cat(*[ordered(v[:tops, block:], o[:, block:], 0) for v, o in held_pieces], axis=1)
    mix_far = cat(mix_far_a, mix_far_b, axis=1)
    far, far_sent = matmul(mix_far, out_all, True, parts=2)
    cot_x = cat(cot_xa, cot_xb)
    e2, e1_o, cot_x, cot_c, qkv_a, qkv_b, far, far_sent, out_all, contract_weight = sync(
        e2, e1_o, cot_x, cot_c, qkv_a, qkv_b, far, far_sent, out_all, contract_weight
    )
    cot_xc = core_swap(cot_x)
    far_c = core_swap(far_sent)
    contract_own = half(contract_weight, 0, second)
    contract_rest = half(contract_weight, 0, 1 - second)
    far, far_c, qkv_a, cot_xc = sync(far, far_c, qkv_a, cot_xc)
    branch_in = add(far[part:], far_c[part:])
    branch_xa = chip_swap(add(far[:part], far_c[:part]))
    e3 = ring_up(e2)
    e2_o = group_swap(e2)
    mix_near_a, log_near_a = attend(info, qkv_a, 0, 2)
    branch_xa, e3, e2_o, mix_near_a, branch_in, contract_own, qkv_b = sync(
        branch_xa, e3, e2_o, mix_near_a, branch_in, contract_own, qkv_b
    )
    branch_xb = chip_swap(branch_in)
    k1 = ring_up(contract_own)
    e3_o = group_swap(e3)
    mix_near_b, log_near_b = attend(info, qkv_b, 0, 2)
    mix_near = cat(mix_near_a, mix_near_b, axis=1)
    near, near_sent = matmul(mix_near, out_all, True, parts=2)
    branch_xb, k1, e3_o, near, near_sent, mix_near = sync(
        branch_xb, k1, e3_o, near, near_sent, mix_near
    )
    near_c = core_swap(near_sent)
    near, near_c, k1 = sync(near, near_c, k1)
    branch_x = cat(branch_xa, branch_xb)
    branch = near.astype(F32) + near_c.astype(F32) + branch_x.astype(F32)
    middle = hidden_in + branch + output_bias.astype(F32)
    normed_two = normalize(middle, gain_second, shift_second).astype(BF16)
    normed_two, k1, e3_o, *held = sync(normed_two, k1, e3_o, *[v for p in held_pieces for v in p])
    two_xa = chip_swap(normed_two[:part])
    two_c = core_swap(normed_two)
    k2 = ring_up(k1)
    k1_o = group_swap(k1)
    expand_pairs = (e1, e1_o, e2, e2_o, e3, e3_o)
    expand_all = cat(expand_own, expand_rest, *[v[:width] for v in expand_pairs], axis=1)
    qkv_all = cat(
        *[ordered(v[:tops, :block], o[:, :block], 0) for v, o in zip(held[0::2], held[1::2])], axis=1
    )
    expand_bias_all = cat(
        expand_bias_own, expand_bias_rest, *[v[width] for v in expand_pairs]
    ).astype(F32)
    two_xa, two_c, k2, k1_o, expand_all, expand_bias_all, normed_two, qkv_all = sync(
        two_xa, two_c, k2, k1_o, expand_all, expand_bias_all, normed_two, qkv_all
    )
    two_xb = chip_swap(normed_two[part:])
    k3 = ring_up(k2)
    k2_o = group_swap(k2)

    def front(rows):
        value, slope = gelu_and_slope(dot(rows, expand_all) + expand_bias_all)
        return value.astype(BF16), slope.astype(BF16)

    two_xac = core_swap(two_xa)
    two_near = cat(normed_two, two_c)
    active_near, slope_near = front(two_near)
    two_xb, k3, k2_o, active_near, slope_near, two_near, two_xac = sync(
        two_xb, k3, k2_o, active_near, slope_near, two_near, two_xac
    )
    two_xbc = core_swap(two_xb)
    two_xbc, k3, qkv_a, qkv_b, cot_c = sync(two_xbc, k3, qkv_a, qkv_b, cot_c)
    k3_o = group_swap(k3)
    two_far = cat(two_xa, two_xb, two_xac, two_xbc)
    active_far, slope_far = front(two_far)
    qkv = cat(qkv_a, qkv_b, axis=1)
    k3_o, active_far, slope_far, two_far, cot_x = sync(k3_o, active_far, slope_far, two_far, cot_x)
    contract_all = cat(contract_own, contract_rest, k1, k1_o, k2, k2_o, k3, k3_o)
    cot_far = cat(cot_x, cot_xc)
    before_far = matmul(cot_far, contract_all, True, slope_far)
    far, far_sent = matmul(before_far, expand_all, True, parts=2)
    far, far_sent, before_far, contract_all = sync(far, far_sent, before_far, contract_all)
    far_c = core_swap(far_sent)
    cot_near = cat(cot, cot_c)
    far, far_c, cot_near, slope_near = sync(far, far_c, cot_near, slope_near)
    two_grad_in = add(far[part:], far_c[part:])
    two_grad_xa = chip_swap(add(far[:part], far_c[:part]))
    before_near = matmul(cot_near, contract_all, True, slope_near)
    near, near_sent = matmul(before_near, expand_all, True, parts=2)
    two_grad_xa, two_grad_in, before_near, near, near_sent, active_near = sync(
        two_grad_xa, two_grad_in, before_near, near, near_sent, active_near
    )
    two_grad_xb = chip_swap(two_grad_in)
    near_c = core_swap(near_sent)
    hidden_order = []
    for r in range(teams):
        owner = (team + teams - r) % teams
        hidden_order += [owner * 2 + second, owner * 2 + 1 - second]
    hidden_order = jnp.stack(hidden_order).astype(jnp.int32)
    (contract_grad,) = weight_grad(
        [(active_near, cot_near, 0), (active_far, cot_far, 0)], step=wide, target=hidden_order
    )
    two_grad_xb, contract_grad, near, near_c = sync(two_grad_xb, contract_grad, near, near_c)
    contract_mine = scatter_sum(contract_grad)
    normed_two_grad = (
        near.astype(F32)
        + near_c.astype(F32)
        + cat(two_grad_xa, two_grad_xb).astype(F32)
    )
    cot_local = cotangent.astype(F32)
    _, pull_second = jax.vjp(normalize, middle, gain_second, shift_second)
    middle_part, second_gain_grad, second_shift_grad = pull_second(normed_two_grad)
    middle_grad = cot_local + middle_part
    middle_low, before_near, active_far = sync(middle_grad.astype(BF16), before_near, active_far)
    middle_xa = chip_swap(middle_low[:part])
    middle_c = core_swap(middle_low)
    expand_parts = weight_grad(
        [(two_near, before_near, 0), (two_far, before_far, 0)], splits=2 * teams
    )
    kept, sent = expand_parts[0::2], expand_parts[1::2]
    middle_low_b = middle_low[part:]
    middle_xa, middle_c, middle_low, middle_low_b, *sent = sync(
        middle_xa, middle_c, middle_low, middle_low_b, *sent
    )
    middle_xb = chip_swap(middle_low_b)
    middle_xac = core_swap(middle_xa)
    s3_o = group_swap(sent[3])
    middle_near = cat(middle_low, middle_c)
    mix_grad_near = matmul(middle_near, out_all, False)
    log_near = cat(log_near_a, log_near_b)
    part_grad = attend_back(info, qkv, mix_near, mix_grad_near, log_near, 0, 2)
    middle_xb, s3_o, part_grad, middle_near, active_far, middle_xac, *sent = sync(
        middle_xb, s3_o, part_grad, middle_near, active_far, middle_xac, *sent
    )
    middle_xbc = core_swap(middle_xb)
    s3 = add(kept[3], s3_o)
    middle_xbc, s3, *sent = sync(middle_xbc, s3, *sent)
    s2_o = group_swap(sent[2])
    s1_o = group_swap(sent[1])
    a3 = ring_down(s3)
    middle_far = cat(middle_xa, middle_xb, middle_xac, middle_xbc)
    mix_grad_far = matmul(middle_far, out_all, False)
    log_far = cat(log_far_a, log_far_b)
    qkv_grad = attend_back(info, qkv, mix_far, mix_grad_far, log_far, 2, 2, part_grad)
    far, far_sent = matmul(qkv_grad, qkv_all, True, place=1, rows=near_rows, parts=2)
    far_rows = qkv_grad[team_rows:].reshape(TEAM, 2, TAIL, teams, 3, PAIR)[:, :, :, :, 1:]
    one = far_rows[:, 0].reshape(span, -1)
    two = far_rows[:, 1].reshape(span, -1)
    s2_o, s1_o, a3, far, far_sent, qkv_grad, middle_far, contract_mine, one, two, sent0 = sync(
        s2_o, s1_o, a3, far, far_sent, qkv_grad, middle_far, contract_mine, one, two, sent[0]
    )
    far_c = core_swap(far_sent)
    far, far_c, qkv_grad, mix_near = sync(far, far_c, qkv_grad, mix_near)
    normed_in = add(far[part:], far_c[part:])
    normed_ga = chip_swap(add(far[:part], far_c[:part]))
    one = line_down(one)
    two = line_down(two, 2)
    s0_o = group_swap(sent0)
    contract_sum = other_groups(contract_mine)
    contract_other = group_swap(contract_sum)
    row_halves = jnp.arange(8, dtype=jnp.int32)
    row_halves = jnp.where(second == 0, row_halves, (row_halves + 4) % 8)
    grad_pairs = [
        (v, qkv_grad, n)
        for n, v in enumerate([normed, normed_c, normed_x, normed_xc, cat(rest, rest_c, rest_x, rest_xc)])
    ]
    kept2, sent2, kept3, sent3 = weight_grad(
        grad_pairs, 1, 2 * block, splits=2, source=row_halves, halves=True, step=width // 8
    )
    near, near_sent = matmul(qkv_grad, qkv_all, True, place=0, rows=near_rows, parts=2)
    a3_s2 = add(a3, add(kept[2], s2_o))
    place_order = jnp.stack([(team + teams - r) % teams for r in range(teams)]).astype(jnp.int32)
    (out_grad,) = weight_grad(
        [(mix_near, middle_near, 0), (mix_far, middle_far, 0)], step=cols, target=place_order
    )
    (
        normed_ga,
        normed_in,
        one,
        two,
        s0_o,
        sent2,
        sent3,
        near,
        near_sent,
        qkv_grad,
        a3_s2,
        active_far,
        out_grad,
        contract_other,
    ) = sync(
        normed_ga,
        normed_in,
        one,
        two,
        s0_o,
        sent2,
        sent3,
        near,
        near_sent,
        qkv_grad,
        a3_s2,
        active_far,
        out_grad,
        contract_other,
    )
    out_mine = scatter_sum(out_grad)
    normed_gb = chip_swap(normed_in)
    q3_in = group_swap(sent3)
    q2_in = group_swap(sent2)
    a2 = ring_down(a3_s2)
    near_c = core_swap(near_sent)

    def turn(v, by):
        shift = (by % teams) * 2 * PAIR
        return cat(v[:, shift:], v[:, :shift], axis=1) if shift else v

    late = add(turn(one, 1), turn(two, 2)).reshape(span, teams, 2, PAIR)
    late = jnp.pad(late, ((0, 0), (0, 0), (1, 0), (0, 0))).reshape(span, teams * block)
    late_terms = matmul(late, qkv_all, True)
    grad_pairs = [(v, qkv_grad, n) for v, _, n in grad_pairs]
    kept0, sent0, kept1, sent1 = weight_grad(
        grad_pairs, 0, 2 * block, splits=2, source=row_halves, halves=True, step=width // 8
    )
    two_far_branch, two_far_sent = matmul(active_far, contract_all, False, parts=2)
    (
        normed_gb,
        q3_in,
        q2_in,
        a2,
        near_c,
        late_terms,
        sent0,
        sent1,
        two_far_branch,
        two_far_sent,
        active_near,
    ) = sync(
        normed_gb,
        q3_in,
        q2_in,
        a2,
        near_c,
        late_terms,
        sent0,
        sent1,
        two_far_branch,
        two_far_sent,
        active_near,
    )
    out_c = core_swap(two_far_sent)
    late_n = core_swap(late_terms[TAIL : 2 * TAIL])
    late_x = chip_swap(late_terms[2 * TAIL : 3 * TAIL])
    late_xc = across_swap(late_terms[3 * TAIL :])
    q3_sum = add(kept3, q3_in)
    a2_s1 = add(a2, add(kept[1], s1_o))
    late_n, late_x, late_xc, q3_sum, a2_s1, sent0, sent1, out_c, active_near, q2_in = sync(
        late_n, late_x, late_xc, q3_sum, a2_s1, sent0, sent1, out_c, active_near, q2_in
    )
    branch_two_xa = chip_swap(add(two_far_branch[:part], out_c[:part]))
    branch_two_in = add(two_far_branch[part:], out_c[part:])
    q1_in = group_swap(sent1)
    qa3 = ring_down(q3_sum)
    normed_grad = near.astype(F32) + near_c.astype(F32) + cat(normed_ga, normed_gb).astype(F32)
    tail = functools.reduce(
        jnp.add, [v.astype(F32) for v in (late_terms[:TAIL], late_n, late_x, late_xc)]
    )
    normed_grad = normed_grad + cat(jnp.zeros((SEG - TAIL, width), F32), tail)
    _, pull_first = jax.vjp(normalize, hidden_in, gain_first, shift_first)
    input_part, first_gain_grad, first_shift_grad = pull_first(normed_grad)
    input_grad = (middle_grad + input_part).astype(BF16)
    qkv_bias_sums = jnp.sum(qkv_grad.astype(F32), axis=0)
    expand_bias_sums = jnp.sum(before_near.astype(F32), axis=0) + jnp.sum(
        before_far.astype(F32), axis=0
    )
    small = jnp.concatenate(
        [
            first_gain_grad,
            first_shift_grad,
            jnp.sum(middle_grad, axis=0),
            second_gain_grad,
            second_shift_grad,
            jnp.sum(cot_local, axis=0),
        ]
    )
    place = block + hid
    owners = jnp.zeros((n_mp * place,), F32)
    for r in range(teams):
        owner = (team + teams - r) % teams
        mine_hid = ordered(
            expand_bias_sums[2 * r * wide : (2 * r + 1) * wide],
            expand_bias_sums[(2 * r + 1) * wide : (2 * r + 2) * wide],
            0,
        )
        piece = jnp.concatenate(
            [qkv_bias_sums[r * block : (r + 1) * block], mine_hid]
        )
        owners = lax.dynamic_update_slice(owners, piece, ((owner * TEAM + mine) * place,))

    vector, q1_in, qa3, branch_two_xa, branch_two_in, sent0, a2_s1 = sync(
        cat(small, owners), q1_in, qa3, branch_two_xa, branch_two_in, sent0, a2_s1
    )

    def add_shifts(shifts, here):
        shifts = jnp.stack(shifts)
        return functools.reduce(jnp.add, [shifts[here(i)] for i in range(shifts.shape[0])])

    shifts = [vector, core_swap(vector), chip_swap(vector), across_swap(vector)]
    q0_in = group_swap(sent0)
    a1 = ring_down(a2_s1)
    qa3_sum = add(qa3, add(kept2, q2_in))
    q0_in, a1, qa3_sum, active_near, out_mine, *shifts = sync(
        q0_in, a1, qa3_sum, active_near, out_mine, *shifts
    )
    vector = add_shifts(shifts, lambda i: mine ^ i)
    shifts = [vector] + [ring_up(vector, r) for r in range(1, teams)]
    qa2 = ring_down(qa3_sum)
    expand_mine = other_groups(add(a1, add(kept[0], s0_o)))
    expand_other = group_swap(expand_mine)
    two_near_branch, two_near_sent = matmul(active_near, contract_all, False, parts=2)
    qa2, expand_other, two_near_branch, two_near_sent, branch_two_in, *shifts = sync(
        qa2, expand_other, two_near_branch, two_near_sent, branch_two_in, *shifts
    )
    vector = add_shifts(shifts, lambda i: (team + teams - i) % teams)
    bit = 1
    while bit < n_dp:
        vector = vector + group_swap(vector, bit)
        bit *= 2
    qa1 = ring_down(add(qa2, add(kept1, q1_in)))
    branch_two_xb = chip_swap(branch_two_in)
    two_near_c = core_swap(two_near_sent)
    out_sum = other_groups(out_mine)
    out_other = group_swap(out_sum)
    vector, qa1, branch_two_xb, two_near_c, out_other = sync(
        vector, qa1, branch_two_xb, two_near_c, out_other
    )
    qkv_mine = other_groups(add(qa1, add(kept0, q0_in)))
    qkv_other = group_swap(qkv_mine)
    mine_spot = lax.dynamic_slice(vector, (6 * width + me * place,), (place,))
    six = [vector[k * width : (k + 1) * width] for k in range(6)]

    branch_two = (
        two_near_branch.astype(F32)
        + two_near_c.astype(F32)
        + cat(branch_two_xa, branch_two_xb).astype(F32)
    )
    layer_out = (middle + branch_two + contract_bias.astype(F32)).astype(BF16)
    qkv_final = ordered(qkv_mine, qkv_other, 0).astype(F32)
    return (
        layer_out,
        input_grad,
        six[0],
        six[1],
        qkv_final[:, :cols],
        mine_spot[:cols],
        qkv_final[:, cols : 2 * cols],
        qkv_final[:, 2 * cols :],
        mine_spot[2 * cols : 3 * cols],
        ordered(out_sum, out_other, 0).astype(F32),
        six[2],
        six[3],
        six[4],
        ordered(expand_mine, expand_other, 1).astype(F32),
        mine_spot[block:],
        ordered(contract_sum, contract_other, 0).astype(F32),
        six[5],
    )


def solution(mesh):
    rows = P(("dp", "mp"), None)
    in_cols, in_rows = P(None, "mp"), P("mp", None)
    placed = (
        rows,
        P("dp", None),
        P(),
        P(),
        in_cols,
        P("mp"),
        in_cols,
        in_cols,
        P("mp"),
        in_rows,
        P(),
        P(),
        P(),
        in_cols,
        P("mp"),
        in_rows,
        P(),
        rows,
    )
    return jax.shard_map(
        body,
        mesh=mesh,
        in_specs=placed,
        out_specs=(
            rows,
            rows,
            P(),
            P(),
            in_cols,
            P("mp"),
            in_cols,
            in_cols,
            P("mp"),
            in_rows,
            P(),
            P(),
            P(),
            in_cols,
            P("mp"),
            in_rows,
            P(),
        ),
        check_vma=False,
    )
```

```python
import functools

import jax
import jax.numpy as jnp
from jax import lax
from jax.experimental import pallas as pl
from jax.experimental.pallas import tpu as pltpu
from jax.sharding import PartitionSpec as P

HD = 64
SEG = 512
NSUM = 50
TAIL = 64
TEAM = 4
PAIR = 2 * HD
QB = 256
EPSILON = 1e-05
MASKED = -1e30
LIGHT = pl.CostEstimate(flops=1024, bytes_accessed=1024, transcendentals=0)
F32 = jnp.float32
BF16 = jnp.bfloat16


def gelu_and_slope(v):
    inner = 0.7978845608 * (v + 0.044715 * v * v * v)
    t = jnp.tanh(inner)
    value = 0.5 * v * (1.0 + t)
    slope = 0.5 * (1.0 + t) + 0.5 * v * (1.0 - t * t) * (
        0.7978845608 * (1.0 + 3.0 * 0.044715 * v * v)
    )
    return value, slope


def normalize(values, scaling, offset):
    centre = jnp.mean(values, axis=-1, keepdims=True)
    centred = values - centre
    spread = jnp.mean(centred * centred, axis=-1, keepdims=True)
    return centred * lax.rsqrt(spread + EPSILON) * scaling + offset


def slot_items(counts, slot_count):
    item_ends = jnp.cumsum(counts)
    places = jnp.arange(slot_count, dtype=jnp.int32)
    return jnp.sum((places[:, None] >= item_ends[None, :]).astype(jnp.int32), axis=1)


def dot(a, b):
    return jnp.dot(a, b, preferred_element_type=F32)


def dot_nt(a, b):
    return lax.dot_general(a, b, (((1,), (1,)), ((), ())), preferred_element_type=F32)


def dot_tn(a, b):
    return lax.dot_general(a, b, (((0,), (0,)), ((), ())), preferred_element_type=F32)


def head_only(block, h):
    lane = lax.broadcasted_iota(jnp.int32, block.shape, 1)
    return jnp.where((lane // HD) == h, block, jnp.zeros_like(block))


def causal(block):
    key = lax.broadcasted_iota(jnp.int32, block.shape, 0)
    query = lax.broadcasted_iota(jnp.int32, block.shape, 1)
    return jnp.where(query >= key, block, MASKED)


def hide_rows(block, count):
    key = lax.broadcasted_iota(jnp.int32, block.shape, 0)
    return jnp.where(key >= count, block, MASKED)


def key_blocks(info_ref, e):
    slots = info_ref.shape[0] - 2
    team, mine = info_ref[slots], info_ref[slots + 1]
    i = mine ^ e
    item = info_ref[team * TEAM + i]

    def hidden(other):
        same = info_ref[jnp.maximum(other, 0)] == item
        return jnp.where(jnp.logical_and(other >= 0, same), TAIL - NSUM, TAIL)

    rows = TEAM * SEG
    out = [(rows + 2 * f * TAIL, hidden((team - 1) * TEAM + (mine ^ f))) for f in range(TEAM)]
    for d in range(1, TEAM):
        j = i ^ d
        inside = j < i
        start = jnp.where(
            inside, (e ^ d) * SEG + SEG - TAIL, rows + (2 * (e ^ d) + 1) * TAIL
        )
        out.append((start, hidden(jnp.where(inside, team, team - 2) * TEAM + j)))
    return out


def attend_kernel(first, count, info_ref, qkv_ref, mix_ref, log_ref):
    def segment(e, carry):
        base = pl.multiple_of(e * SEG, SEG)
        place = pl.multiple_of((e - first) * SEG, SEG)
        extra = key_blocks(info_ref, e)
        keys = qkv_ref[pl.ds(base, SEG), PAIR : 2 * PAIR]
        value_t = qkv_ref[pl.ds(base, SEG), 2 * PAIR : 3 * PAIR].T
        extra_keys = [
            qkv_ref[pl.ds(pl.multiple_of(s, TAIL), TAIL), PAIR : 2 * PAIR] for s, _ in extra
        ]
        extra_values = [
            qkv_ref[pl.ds(pl.multiple_of(s, TAIL), TAIL), 2 * PAIR : 3 * PAIR] for s, _ in extra
        ]
        extra_keys = jnp.concatenate(extra_keys, axis=0)
        extra_value_t = jnp.concatenate(extra_values, axis=0).T
        for qb in range(SEG // QB):
            query = qkv_ref[pl.ds(base + qb * QB, QB), 0:PAIR]
            seen = (qb + 1) * QB
            outs = []
            for h in range(2):
                qh = head_only(query, h)
                own = dot_nt(keys[:seen], qh)
                parts = [own[: qb * QB]] if qb else []
                parts.append(causal(own[qb * QB :]))
                far = dot_nt(extra_keys, qh)
                for n, (_, hidden) in enumerate(extra):
                    parts.append(hide_rows(far[n * TAIL : (n + 1) * TAIL], hidden))
                high = functools.reduce(
                    jnp.maximum, [jnp.max(p, axis=0, keepdims=True) for p in parts]
                )
                parts = [jnp.exp(p - high) for p in parts]
                total = functools.reduce(
                    jnp.add, [jnp.sum(p, axis=0, keepdims=True) for p in parts]
                )
                cut = 2 if qb else 1
                p_own = jnp.concatenate([p.astype(BF16) for p in parts[:cut]], axis=0)
                p_far = jnp.concatenate([p.astype(BF16) for p in parts[cut:]], axis=0)
                rows = slice(h * HD, (h + 1) * HD)
                mixed = dot(value_t[rows, :seen], p_own) + dot(extra_value_t[rows], p_far)
                outs.append(mixed / total)
                log_ref[0, e - first, h : h + 1, qb * QB : (qb + 1) * QB] = high + jnp.log(total)
            mix_ref[pl.ds(place + qb * QB, QB), :] = jnp.concatenate(outs, axis=0).T.astype(BF16)
        return carry

    lax.fori_loop(first, first + count, segment, 0)


def attend(info, qkv, first, count):
    pieces = qkv.shape[1] // (3 * PAIR)
    rows = count * SEG
    return pl.pallas_call(
        functools.partial(attend_kernel, first, count),
        grid_spec=pltpu.PrefetchScalarGridSpec(
            num_scalar_prefetch=1,
            grid=(pieces,),
            in_specs=[pl.BlockSpec((qkv.shape[0], 3 * PAIR), lambda r, t: (0, r))],
            out_specs=[
                pl.BlockSpec((rows, PAIR), lambda r, t: (0, r)),
                pl.BlockSpec((1, count, 2, SEG), lambda r, t: (r, 0, 0, 0)),
            ],
        ),
        out_shape=[
            jax.ShapeDtypeStruct((rows, pieces * PAIR), BF16),
            jax.ShapeDtypeStruct((pieces, count, 2, SEG), F32),
        ],
        compiler_params=pltpu.CompilerParams(vmem_limit_bytes=56 * 1024 * 1024),
        cost_estimate=LIGHT,
        name="attend",
    )(info, qkv)


def attend_back_kernel(first, count, info_ref, qkv_ref, mix_ref, grad_ref, log_ref, *rest):
    key_acc, value_acc = rest[-2:]
    if len(rest) == 6:
        before_ref, out_ref = rest[:2]
        key_acc[...] = before_ref[:, PAIR : 2 * PAIR].astype(F32)
        value_acc[...] = before_ref[:, 2 * PAIR : 3 * PAIR].astype(F32)
        out_ref[:, 0:PAIR] = before_ref[:, 0:PAIR]
    else:
        out_ref = rest[0]
        key_acc[...] = jnp.zeros_like(key_acc)
        value_acc[...] = jnp.zeros_like(value_acc)
        out_ref[:, 0:PAIR] = jnp.zeros((out_ref.shape[0], PAIR), BF16)

    def segment(e, carry):
        base = pl.multiple_of(e * SEG, SEG)
        place = pl.multiple_of((e - first) * SEG, SEG)
        extra = key_blocks(info_ref, e)
        keys = qkv_ref[pl.ds(base, SEG), PAIR : 2 * PAIR]
        values = qkv_ref[pl.ds(base, SEG), 2 * PAIR : 3 * PAIR]
        key_t = keys.T
        extra_keys = jnp.concatenate(
            [qkv_ref[pl.ds(pl.multiple_of(s, TAIL), TAIL), PAIR : 2 * PAIR] for s, _ in extra],
            axis=0,
        )
        extra_values = jnp.concatenate(
            [qkv_ref[pl.ds(pl.multiple_of(s, TAIL), TAIL), 2 * PAIR : 3 * PAIR] for s, _ in extra],
            axis=0,
        )
        extra_key_t = extra_keys.T
        for qb in range(SEG // QB):
            here = pl.ds(base + qb * QB, QB)
            query = qkv_ref[here, 0:PAIR]
            grad = grad_ref[pl.ds(place + qb * QB, QB), :]
            both = (grad.astype(F32) * mix_ref[pl.ds(place + qb * QB, QB), :].astype(F32)).T
            seen = (qb + 1) * QB
            key_own, value_own, key_far, value_far = 0.0, 0.0, 0.0, 0.0
            query_grads = []
            for h in range(2):
                rows = slice(h * HD, (h + 1) * HD)
                qh, gh = head_only(query, h), head_only(grad, h)
                centre = jnp.sum(both[rows], axis=0, keepdims=True)
                log = log_ref[0, e - first, h : h + 1, qb * QB : (qb + 1) * QB]
                own = dot_nt(keys[:seen], qh)
                parts = [own[: qb * QB]] if qb else []
                parts.append(causal(own[qb * QB :]))
                own = jnp.exp((jnp.concatenate(parts, axis=0) if qb else parts[0]) - log)
                far = dot_nt(extra_keys, qh)
                far = jnp.concatenate(
                    [
                        hide_rows(far[n * TAIL : (n + 1) * TAIL], hidden)
                        for n, (_, hidden) in enumerate(extra)
                    ],
                    axis=0,
                )
                far = jnp.exp(far - log)
                own_step = (own * (dot_nt(values[:seen], gh) - centre)).astype(BF16)
                far_step = (far * (dot_nt(extra_values, gh) - centre)).astype(BF16)
                value_own += dot(own.astype(BF16), gh)
                value_far += dot(far.astype(BF16), gh)
                key_own += dot(own_step, qh)
                key_far += dot(far_step, qh)
                query_grads.append(dot(key_t[rows, :seen], own_step) + dot(extra_key_t[rows], far_step))
            query_grad = jnp.concatenate(query_grads, axis=0).T * (HD**-0.5)
            out_ref[here, 0:PAIR] = query_grad.astype(BF16)
            key_acc[pl.ds(base, seen), :] += key_own
            value_acc[pl.ds(base, seen), :] += value_own
            for n, (s, _) in enumerate(extra):
                there = pl.ds(pl.multiple_of(s, TAIL), TAIL)
                key_acc[there, :] += key_far[n * TAIL : (n + 1) * TAIL]
                value_acc[there, :] += value_far[n * TAIL : (n + 1) * TAIL]
        return carry

    lax.fori_loop(first, first + count, segment, 0)
    out_ref[:, PAIR : 2 * PAIR] = key_acc[...].astype(BF16)
    out_ref[:, 2 * PAIR : 3 * PAIR] = value_acc[...].astype(BF16)
    if len(rest) == 6:
        for f in range(TEAM):
            for k, far_ref in enumerate(rest[2:4]):
                at = TEAM * SEG + (2 * f + k) * TAIL
                here = slice(f * TAIL, (f + 1) * TAIL)
                far_ref[here, :PAIR] = key_acc[at : at + TAIL, :].astype(BF16)
                far_ref[here, PAIR:] = value_acc[at : at + TAIL, :].astype(BF16)


def attend_back(info, qkv, mixture, grad, logs, first, count, before=None):
    pieces = qkv.shape[1] // (3 * PAIR)
    rows = count * SEG
    wide = pl.BlockSpec((qkv.shape[0], 3 * PAIR), lambda r, t: (0, r))
    narrow = pl.BlockSpec((rows, PAIR), lambda r, t: (0, r))
    more = () if before is None else (before,)
    return pl.pallas_call(
        functools.partial(attend_back_kernel, first, count),
        grid_spec=pltpu.PrefetchScalarGridSpec(
            num_scalar_prefetch=1,
            grid=(pieces,),
            in_specs=[
                wide,
                narrow,
                narrow,
                pl.BlockSpec((1, count, 2, SEG), lambda r, t: (r, 0, 0, 0)),
            ]
            + [wide] * len(more),
            out_specs=[wide] + [pl.BlockSpec((TEAM * TAIL, 2 * PAIR), lambda r, t: (0, r))] * (2 * len(more)),
            scratch_shapes=[
                pltpu.VMEM((qkv.shape[0], PAIR), F32),
                pltpu.VMEM((qkv.shape[0], PAIR), F32),
            ],
        ),
        out_shape=[jax.ShapeDtypeStruct(qkv.shape, BF16)]
        + [jax.ShapeDtypeStruct((TEAM * TAIL, pieces * 2 * PAIR), BF16)] * (2 * len(more)),
        compiler_params=pltpu.CompilerParams(vmem_limit_bytes=56 * 1024 * 1024),
        cost_estimate=LIGHT,
        name="attend_back",
    )(info, qkv, mixture, grad, logs, *more)


def weight_grad_kernel(splits, halves, pairs, source_ref, target_ref, *refs):
    outs = refs[2 * pairs :]
    total = None
    for left, right in zip(refs[: 2 * pairs : 2], refs[1 : 2 * pairs : 2]):
        term = dot_tn(left[...], right[...])
        total = term if total is None else total + term
    total = total.astype(BF16)
    width = total.shape[1] // splits
    columns = [total[:, k * width : (k + 1) * width] for k in range(splits)]
    if not halves:
        for k in range(splits):
            outs[k][...] = columns[k]
        return
    step, steps = pl.program_id(0), pl.num_programs(0)

    @pl.when(step < steps // 2)
    def _():
        for k in range(splits):
            outs[2 * k][...] = columns[k]

    @pl.when(step >= steps // 2)
    def _():
        for k in range(splits):
            outs[2 * k + 1][...] = columns[k]


def weight_grad(pairs, column=0, columns=None, step=256, splits=1, source=None, target=None, halves=False):
    height = pairs[0][0].shape[1]
    columns = columns or pairs[0][1].shape[1]
    steps, width = height // step, columns // splits
    plain = jnp.arange(steps, dtype=jnp.int32)
    specs = []
    for left, right, n in pairs:
        specs.append(pl.BlockSpec((left.shape[0], step), lambda i, s, t: (0, s[i])))
        specs.append(pl.BlockSpec((left.shape[0], columns), lambda i, s, t, n=n: (n, column)))
    if halves:
        outs = [
            pl.BlockSpec((step, width), lambda i, s, t: (jnp.minimum(i, steps // 2 - 1), 0)),
            pl.BlockSpec((step, width), lambda i, s, t: (jnp.maximum(i - steps // 2, 0), 0)),
        ] * splits
        shapes = [jax.ShapeDtypeStruct((height // 2, width), BF16)] * (2 * splits)
    else:
        outs = [pl.BlockSpec((step, width), lambda i, s, t: (t[i], 0))] * splits
        shapes = [jax.ShapeDtypeStruct((height, width), BF16)] * splits
    return pl.pallas_call(
        functools.partial(weight_grad_kernel, splits, halves, len(pairs)),
        grid_spec=pltpu.PrefetchScalarGridSpec(
            num_scalar_prefetch=2, grid=(steps,), in_specs=specs, out_specs=outs
        ),
        out_shape=shapes,
        compiler_params=pltpu.CompilerParams(vmem_limit_bytes=56 * 1024 * 1024),
        cost_estimate=LIGHT,
        name="weight_grad",
    )(
        plain if source is None else source,
        plain if target is None else target,
        *[v for pair in pairs for v in pair[:2]],
    )


def pack_kernel(plan, which_ref, *refs):
    sources, out_ref, sems = refs[:-2], refs[-2], refs[-1]
    copies = []
    for n, (ref, (row, rows, column, columns, at_row, at_column)) in enumerate(zip(sources, plan)):
        if at_row == "held":
            at_row = pl.multiple_of(which_ref[0] * rows, rows)
        elif at_row == "other":
            at_row = pl.multiple_of((1 - which_ref[0]) * rows, rows)
        copies.append(
            pltpu.make_async_copy(
                ref.at[pl.ds(row, rows), pl.ds(column, columns)],
                out_ref.at[pl.ds(at_row, rows), pl.ds(at_column, columns)],
                sems.at[n],
            )
        )
    for copy in copies:
        copy.start()
    for copy in copies:
        copy.wait()


def pack(which, shape, parts):
    return pl.pallas_call(
        functools.partial(pack_kernel, [plan for _, plan in parts]),
        grid_spec=pltpu.PrefetchScalarGridSpec(
            num_scalar_prefetch=1,
            grid=(),
            in_specs=[pl.BlockSpec(memory_space=pl.ANY)] * len(parts),
            out_specs=pl.BlockSpec(memory_space=pltpu.VMEM),
            scratch_shapes=[pltpu.SemaphoreType.DMA((len(parts),))],
        ),
        out_shape=jax.ShapeDtypeStruct(shape, BF16),
        compiler_params=pltpu.CompilerParams(vmem_limit_bytes=32 * 1024 * 1024),
        cost_estimate=LIGHT,
        name="pack",
    )(which, *[v for v, _ in parts])


def pack_rows(which, parts):
    columns, row, plan = parts[0].shape[1], 0, []
    for v in parts:
        plan.append((v, (0, v.shape[0], 0, columns, row, 0)))
        row += v.shape[0]
    return pack(which, (row, columns), plan)


def pack_columns(which, parts, rows):
    column, plan = 0, []
    for v in parts:
        plan.append((v, (0, rows, 0, v.shape[1], 0, column)))
        column += v.shape[1]
    return pack(which, (rows, column), plan)


def project_kernel(pieces, which_ref, *refs):
    weights, rows, out_ref, first, last = (
        refs[: 2 * pieces],
        refs[2 * pieces : -3],
        refs[-3],
        refs[-2],
        refs[-1],
    )
    depth, block = first.shape[0], first.shape[1] // pieces
    for n in range(pieces):
        first[:, n * block : (n + 1) * block] = weights[2 * n][:depth, :block]
        last[:, n * block : (n + 1) * block] = weights[2 * n + 1][:depth, :block]
    bias = jnp.concatenate(
        [weights[2 * n][depth : depth + 1, :block].astype(F32) for n in range(pieces)], axis=1
    )
    lane = lax.broadcasted_iota(jnp.int32, bias.shape, 1)
    scale = jnp.where(lane % block < PAIR, HD**-0.5, 1.0)
    held = pl.ds(pl.multiple_of(which_ref[0] * depth, depth), depth)
    other = pl.ds(pl.multiple_of((1 - which_ref[0]) * depth, depth), depth)
    at = 0
    for ref in rows:
        chunk = min(256, ref.shape[0])
        for start in range(0, ref.shape[0], chunk):
            here = slice(start, start + chunk)
            value = dot(ref[here, held], first[...]) + dot(ref[here, other], last[...])
            out_ref[at + start : at + start + chunk, :] = ((value + bias) * scale).astype(BF16)
        at += ref.shape[0]


def project(which, weights, rows):
    pieces = len(weights)
    depth, block = rows[0].shape[1] // 2, 3 * PAIR
    height = sum(v.shape[0] for v in rows)
    return pl.pallas_call(
        functools.partial(project_kernel, pieces),
        grid_spec=pltpu.PrefetchScalarGridSpec(
            num_scalar_prefetch=1,
            grid=(),
            in_specs=[pl.BlockSpec(memory_space=pltpu.VMEM)] * (2 * pieces + len(rows)),
            out_specs=pl.BlockSpec(memory_space=pltpu.VMEM),
            scratch_shapes=[pltpu.VMEM((depth, pieces * block), BF16)] * 2,
        ),
        out_shape=jax.ShapeDtypeStruct((height, pieces * block), BF16),
        compiler_params=pltpu.CompilerParams(vmem_limit_bytes=56 * 1024 * 1024),
        cost_estimate=LIGHT,
        name="project",
    )(which, *[v for pair in weights for v in pair], *rows)


def matmul_kernel(transposed, parts, left_ref, right_ref, *rest):
    outs = rest[-parts:]
    rows = left_ref.shape[0] // parts
    chunk = min(256, rows)
    for start in range(0, left_ref.shape[0], chunk):
        here = slice(start, start + chunk)
        value = (dot_nt if transposed else dot)(left_ref[here, :], right_ref[...])
        if len(rest) > parts:
            value = value * rest[0][here, :].astype(F32)
        at = start % rows
        outs[start // rows][at : at + chunk, :] = value.astype(BF16)


def matmul(left, right, transposed, scale=None, place=0, rows=None, step=512, parts=1):
    rows = rows or left.shape[0]
    depth = left.shape[1]
    columns = right.shape[0] if transposed else right.shape[1]
    right_spec = (
        pl.BlockSpec((step, depth), lambda i: (i, 0))
        if transposed
        else pl.BlockSpec((depth, step), lambda i: (0, i))
    )
    more = () if scale is None else (scale,)
    out = pl.pallas_call(
        functools.partial(matmul_kernel, transposed, parts),
        grid=(columns // step,),
        in_specs=[pl.BlockSpec((rows, depth), lambda i: (place, 0)), right_spec]
        + [pl.BlockSpec((rows, step), lambda i: (0, i))] * len(more),
        out_specs=[pl.BlockSpec((rows // parts, step), lambda i: (0, i))] * parts,
        out_shape=[jax.ShapeDtypeStruct((rows // parts, columns), BF16)] * parts,
        compiler_params=pltpu.CompilerParams(vmem_limit_bytes=56 * 1024 * 1024),
        cost_estimate=LIGHT,
        name="matmul",
    )(left, right, *more)
    return out if parts > 1 else out[0]


def body(
    inputs,
    item_counts,
    first_gain,
    first_shift,
    query_weight,
    query_bias,
    key_weight,
    value_weight,
    value_bias,
    output_weight,
    output_bias,
    second_gain,
    second_shift,
    expand_weight,
    expand_bias,
    contract_weight,
    contract_bias,
    cotangent,
):
    n_mp, n_dp = lax.axis_size("mp"), lax.axis_size("dp")
    teams = n_mp // TEAM
    me = lax.axis_index("mp")
    team, mine = me // TEAM, me % TEAM
    second = lax.axis_index("dp") % 2

    def core_swap(v):
        return lax.ppermute(v, "mp", [(i, i ^ 1) for i in range(n_mp)])

    def chip_swap(v):
        return lax.ppermute(v, "mp", [(i, i ^ 2) for i in range(n_mp)])

    def ring_up(v, by=1):
        return lax.ppermute(v, "mp", [(i, (i + by * TEAM) % n_mp) for i in range(n_mp)])

    def ring_down(v):
        return lax.ppermute(v, "mp", [(i, (i - TEAM) % n_mp) for i in range(n_mp)])

    def line_up(v, by=1):
        return lax.ppermute(v, "mp", [(i, i + by * TEAM) for i in range(n_mp - by * TEAM)])

    def line_down(v, by=1):
        return lax.ppermute(v, "mp", [(i + by * TEAM, i) for i in range(n_mp - by * TEAM)])

    def group_swap(v, bit=1):
        return lax.ppermute(v, "dp", [(i, i ^ bit) for i in range(n_dp)])

    def half(v, axis, which):
        size = v.shape[axis] // 2
        return lax.dynamic_slice_in_dim(v, which * size, size, axis)

    def ordered(held, other, axis):
        return jnp.where(
            second == 0,
            jnp.concatenate([held, other], axis=axis),
            jnp.concatenate([other, held], axis=axis),
        )

    def add(*terms):
        return functools.reduce(jnp.add, [t.astype(F32) for t in terms]).astype(BF16)

    def other_groups(v):
        bit = 2
        while bit < n_dp:
            v = add(v, group_swap(v, bit))
            bit *= 2
        return v

    def sync(*values):
        return lax.optimization_barrier(values)

    slot_count = teams * TEAM
    items = slot_items(item_counts[0], slot_count)
    info = jnp.pad(items, (0, 2))
    at = lax.iota(jnp.int32, slot_count + 2)
    info = jnp.where(at == slot_count, team, jnp.where(at == slot_count + 1, mine, info))

    gain_first, shift_first = first_gain.astype(F32), first_shift.astype(F32)
    gain_second, shift_second = second_gain.astype(F32), second_shift.astype(F32)
    width = inputs.shape[1]
    cols = query_bias.shape[0]
    hid = expand_bias.shape[0]
    wide = hid // 2
    team_rows, near_rows = TEAM * SEG, 2 * SEG
    span = TEAM * TAIL
    block = 3 * PAIR
    pad = 16

    def across_swap(v):
        return lax.ppermute(v, "mp", [(i, i ^ 3) for i in range(n_mp)])

    def with_bias(weight, bias):
        return jnp.concatenate(
            [weight, jnp.broadcast_to(bias[None], (pad, bias.shape[0]))], axis=0
        )

    def send_in(terms):
        size = terms.shape[0] // 2
        return add(terms[:size], core_swap(terms[size:]))

    along = [[t * TEAM + i for t in range(teams)] for i in range(TEAM)]
    part = SEG // 2
    pairs_along = [
        [(first + d) * n_mp + t * TEAM + i for t in range(teams) for d in range(2)]
        for first in range(0, n_dp, 2)
        for i in range(TEAM)
    ]

    def scatter_sum(v):
        return lax.psum_scatter(
            v, ("dp", "mp"), scatter_dimension=0, axis_index_groups=pairs_along, tiled=True
        )

    def cat(*parts, axis=0):
        return jnp.concatenate(parts, axis=axis)

    which = jnp.reshape(second, (1,)).astype(jnp.int32)

    qkv_local = cat(query_weight, key_weight, value_weight, output_weight.T, axis=1)
    qkv_bias_local = cat(
        query_bias, jnp.zeros_like(query_bias), value_bias, jnp.zeros_like(query_bias)
    )
    packed = with_bias(half(qkv_local, 0, second), qkv_bias_local)
    q0_o = half(qkv_local, 0, 1 - second)
    hidden_in = inputs.astype(F32)
    normed = normalize(hidden_in, gain_first, shift_first).astype(BF16)
    packed, normed, normed_tail = sync(packed, normed, normed[SEG - TAIL :])
    q1 = ring_up(packed)
    normed_xa = chip_swap(normed[:part])
    normed_c = core_swap(normed)
    early = line_up(normed_tail)
    normed_b = normed[part:]
    q1, normed_xa, normed_c, early, normed_b = sync(q1, normed_xa, normed_c, early, normed_b)
    q2 = ring_up(q1)
    normed_xb = chip_swap(normed_b)
    q1_o = group_swap(q1)
    earlier = line_up(early)
    q2, q1_o, normed_x, rest = sync(q2, q1_o, cat(normed_xa, normed_xb), cat(early, earlier))
    q3 = ring_up(q2)
    q2_o = group_swap(q2)
    normed_xc = core_swap(normed_x)
    rest_x = chip_swap(rest)
    rest_xc = across_swap(rest)
    rest_c = core_swap(rest)
    tops = width // 2
    expand_own, expand_rest = half(expand_weight, 1, second), half(expand_weight, 1, 1 - second)
    expand_bias_own = half(expand_bias, 0, second)
    expand_bias_rest = half(expand_bias, 0, 1 - second)
    q3, q2_o, normed_xc, rest_x, rest_xc, rest_c, cot_a, cot_b, e0 = sync(
        q3,
        q2_o,
        normed_xc,
        rest_x,
        rest_xc,
        rest_c,
        cotangent[:part],
        cotangent[part:],
        with_bias(expand_own, expand_bias_own),
    )
    q3_o = group_swap(q3)
    e1 = ring_up(e0)
    cot_xa = chip_swap(cot_a)
    row_blocks = [normed, normed_c, normed_x, normed_xc, rest, rest_c, rest_x, rest_xc]
    qkv_a = project(which, [(packed, q0_o), (q1, q1_o), (q2, q2_o)], row_blocks)
    q3_o, cot_xa, qkv_a, e1, cot_b, cot = sync(q3_o, cot_xa, qkv_a, e1, cot_b, cotangent)
    e2 = ring_up(e1)
    e1_o = group_swap(e1)
    cot_xb = chip_swap(cot_b)
    cot_c = core_swap(cot)
    mix_far_a, log_far_a = attend(info, qkv_a, 2, 2)
    qkv_b = project(which, [(q3, q3_o)], row_blocks)
    mix_far_b, log_far_b = attend(info, qkv_b, 2, 2)
    held_pieces = ((packed, q0_o), (q1, q1_o), (q2, q2_o), (q3, q3_o))

    def whole(pieces, column, columns):
        plan = []
        for n, (v, o) in enumerate(pieces):
            plan.append((v, (0, tops, column, columns, "held", n * columns)))
            plan.append((o, (0, tops, column, columns, "other", n * columns)))
        return pack(which, (width, len(pieces) * columns), plan)

    out_all = whole(held_pieces, block, cols)
    mix_far = pack_columns(which, [mix_far_a, mix_far_b], near_rows)
    far, far_sent = matmul(mix_far, out_all, True, parts=2)
    cot_x = pack_rows(which, [cot_xa, cot_xb])
    e2, e1_o, cot_x, cot_c, qkv_a, qkv_b, far, far_sent, out_all, contract_weight = sync(
        e2, e1_o, cot_x, cot_c, qkv_a, qkv_b, far, far_sent, out_all, contract_weight
    )
    far_c = core_swap(far_sent)
    contract_own = half(contract_weight, 0, second)
    contract_rest = half(contract_weight, 0, 1 - second)
    far, far_c, qkv_a = sync(far, far_c, qkv_a)
    branch_in = add(far[part:], far_c[part:])
    branch_xa = chip_swap(add(far[:part], far_c[:part]))
    e3 = ring_up(e2)
    e2_o = group_swap(e2)
    mix_near_a, log_near_a = attend(info, qkv_a, 0, 2)
    branch_xa, e3, e2_o, mix_near_a, branch_in, contract_own, qkv_b = sync(
        branch_xa, e3, e2_o, mix_near_a, branch_in, contract_own, qkv_b
    )
    branch_xb = chip_swap(branch_in)
    cot_xc = core_swap(cot_x)
    k1 = ring_up(contract_own)
    e3_o = group_swap(e3)
    mix_near_b, log_near_b = attend(info, qkv_b, 0, 2)
    mix_near = pack_columns(which, [mix_near_a, mix_near_b], near_rows)
    near, near_sent = matmul(mix_near, out_all, True, parts=2)
    branch_xb, k1, e3_o, near, near_sent, mix_near, cot_xc = sync(
        branch_xb, k1, e3_o, near, near_sent, mix_near, cot_xc
    )
    near_c = core_swap(near_sent)
    near, near_c, k1 = sync(near, near_c, k1)
    branch_x = cat(branch_xa, branch_xb)
    branch = near.astype(F32) + near_c.astype(F32) + branch_x.astype(F32)
    middle = hidden_in + branch + output_bias.astype(F32)
    normed_two = normalize(middle, gain_second, shift_second).astype(BF16)
    normed_two, k1, e3_o, *held = sync(normed_two, k1, e3_o, *[v for p in held_pieces for v in p])
    two_xa = chip_swap(normed_two[:part])
    two_c = core_swap(normed_two)
    k2 = ring_up(k1)
    k1_o = group_swap(k1)
    expand_pairs = (e1, e1_o, e2, e2_o, e3, e3_o)
    expand_all = pack_columns(which, [expand_own, expand_rest, *expand_pairs], width)
    held = tuple(zip(held[0::2], held[1::2]))
    qkv_all = whole(held, 0, block)
    key_value_all = whole(held, PAIR, 2 * PAIR)
    expand_bias_all = cat(
        expand_bias_own, expand_bias_rest, *[v[width] for v in expand_pairs]
    ).astype(F32)
    two_xa, two_c, k2, k1_o, expand_all, expand_bias_all, normed_two, qkv_all, key_value_all = sync(
        two_xa, two_c, k2, k1_o, expand_all, expand_bias_all, normed_two, qkv_all, key_value_all
    )
    two_xb = chip_swap(normed_two[part:])
    k3 = ring_up(k2)
    k2_o = group_swap(k2)

    def front(rows):
        value, slope = gelu_and_slope(dot(rows, expand_all) + expand_bias_all)
        return value.astype(BF16), slope.astype(BF16)

    two_xac = core_swap(two_xa)
    two_near = pack_rows(which, [normed_two, two_c])
    active_near, slope_near = front(two_near)
    two_xb, k3, k2_o, active_near, slope_near, two_near, two_xac = sync(
        two_xb, k3, k2_o, active_near, slope_near, two_near, two_xac
    )
    two_xbc = core_swap(two_xb)
    two_xbc, k3, qkv_a, qkv_b, cot_c = sync(two_xbc, k3, qkv_a, qkv_b, cot_c)
    k3_o = group_swap(k3)
    two_far = pack_rows(which, [two_xa, two_xb, two_xac, two_xbc])
    active_far, slope_far = front(two_far)
    qkv = pack_columns(which, [qkv_a, qkv_b], qkv_a.shape[0])
    k3_o, active_far, slope_far, two_far, cot_x = sync(k3_o, active_far, slope_far, two_far, cot_x)
    contract_all = pack_rows(which, [contract_own, contract_rest, k1, k1_o, k2, k2_o, k3, k3_o])
    cot_far = pack_rows(which, [cot_x, cot_xc])
    before_far = matmul(cot_far, contract_all, True, slope_far)
    far, far_sent = matmul(before_far, expand_all, True, parts=2)
    far, far_sent, before_far, contract_all = sync(far, far_sent, before_far, contract_all)
    far_c = core_swap(far_sent)
    cot_near = pack_rows(which, [cot, cot_c])
    far, far_c, cot_near, slope_near = sync(far, far_c, cot_near, slope_near)
    two_grad_in = add(far[part:], far_c[part:])
    two_grad_xa = chip_swap(add(far[:part], far_c[:part]))
    before_near = matmul(cot_near, contract_all, True, slope_near)
    near, near_sent = matmul(before_near, expand_all, True, parts=2)
    two_grad_xa, two_grad_in, before_near, near, near_sent, active_near = sync(
        two_grad_xa, two_grad_in, before_near, near, near_sent, active_near
    )
    two_grad_xb = chip_swap(two_grad_in)
    near_c = core_swap(near_sent)
    hidden_order = []
    for r in range(teams):
        owner = (team + teams - r) % teams
        hidden_order += [owner * 2 + second, owner * 2 + 1 - second]
    hidden_order = jnp.stack(hidden_order).astype(jnp.int32)
    (contract_grad,) = weight_grad(
        [(active_near, cot_near, 0), (active_far, cot_far, 0)], step=wide, target=hidden_order
    )
    two_grad_xb, contract_grad, near, near_c = sync(two_grad_xb, contract_grad, near, near_c)
    contract_mine = scatter_sum(contract_grad)
    normed_two_grad = (
        near.astype(F32)
        + near_c.astype(F32)
        + cat(two_grad_xa, two_grad_xb).astype(F32)
    )
    cot_local = cotangent.astype(F32)
    _, pull_second = jax.vjp(normalize, middle, gain_second, shift_second)
    middle_part, second_gain_grad, second_shift_grad = pull_second(normed_two_grad)
    middle_grad = cot_local + middle_part
    middle_low, before_near, active_far = sync(middle_grad.astype(BF16), before_near, active_far)
    middle_xa = chip_swap(middle_low[:part])
    middle_c = core_swap(middle_low)
    expand_parts = weight_grad(
        [(two_near, before_near, 0), (two_far, before_far, 0)], splits=2 * teams
    )
    kept, sent = expand_parts[0::2], expand_parts[1::2]
    middle_low_b = middle_low[part:]
    middle_xa, middle_c, middle_low, middle_low_b, *sent = sync(
        middle_xa, middle_c, middle_low, middle_low_b, *sent
    )
    middle_xb = chip_swap(middle_low_b)
    middle_xac = core_swap(middle_xa)
    s3_o = group_swap(sent[3])
    middle_near = pack_rows(which, [middle_low, middle_c])
    mix_grad_near = matmul(middle_near, out_all, False)
    log_near = cat(log_near_a, log_near_b)
    (part_grad,) = attend_back(info, qkv, mix_near, mix_grad_near, log_near, 0, 2)
    middle_xb, s3_o, part_grad, middle_near, active_far, middle_xac, *sent = sync(
        middle_xb, s3_o, part_grad, middle_near, active_far, middle_xac, *sent
    )
    middle_xbc = core_swap(middle_xb)
    s3 = add(kept[3], s3_o)
    middle_xbc, s3, *sent = sync(middle_xbc, s3, *sent)
    s2_o = group_swap(sent[2])
    s1_o = group_swap(sent[1])
    a3 = ring_down(s3)
    middle_far = pack_rows(which, [middle_xa, middle_xb, middle_xac, middle_xbc])
    mix_grad_far = matmul(middle_far, out_all, False)
    log_far = cat(log_far_a, log_far_b)
    qkv_grad, one, two = attend_back(
        info, qkv, mix_far, mix_grad_far, log_far, 2, 2, part_grad
    )
    far, far_sent = matmul(qkv_grad, qkv_all, True, place=1, rows=near_rows, parts=2)
    place_order = jnp.stack([(team + teams - r) % teams for r in range(teams)]).astype(jnp.int32)
    (out_grad,) = weight_grad(
        [(sync(mix_near, far)[0], middle_near, 0), (mix_far, middle_far, 0)], step=cols, target=place_order
    )
    s2_o, s1_o, a3, far, far_sent, qkv_grad, contract_mine, one, two, sent0, out_grad = sync(
        s2_o, s1_o, a3, far, far_sent, qkv_grad, contract_mine, one, two, sent[0], out_grad
    )
    far_c = core_swap(far_sent)
    far, far_c, qkv_grad, out_grad = sync(far, far_c, qkv_grad, out_grad)
    out_mine = scatter_sum(out_grad)
    normed_in = add(far[part:], far_c[part:])
    normed_ga = chip_swap(add(far[:part], far_c[:part]))
    one = line_down(one)
    two = line_down(two, 2)
    s0_o = group_swap(sent0)
    contract_sum = other_groups(contract_mine)
    contract_other = group_swap(contract_sum)
    row_halves = jnp.arange(8, dtype=jnp.int32)
    row_halves = jnp.where(second == 0, row_halves, (row_halves + 4) % 8)
    grad_pairs = [
        (v, qkv_grad, n)
        for n, v in enumerate([normed, normed_c, normed_x, normed_xc, pack_rows(which, [rest, rest_c, rest_x, rest_xc])])
    ]
    kept2, sent2, kept3, sent3 = weight_grad(
        grad_pairs, 1, 2 * block, splits=2, source=row_halves, halves=True, step=width // 8
    )
    near, near_sent = matmul(qkv_grad, qkv_all, True, place=0, rows=near_rows, parts=2)
    a3_s2 = add(a3, add(kept[2], s2_o))
    (
        normed_ga,
        normed_in,
        one,
        two,
        s0_o,
        sent2,
        sent3,
        near,
        near_sent,
        qkv_grad,
        a3_s2,
        active_far,
        contract_other,
    ) = sync(
        normed_ga,
        normed_in,
        one,
        two,
        s0_o,
        sent2,
        sent3,
        near,
        near_sent,
        qkv_grad,
        a3_s2,
        active_far,
        contract_other,
    )
    normed_gb = chip_swap(normed_in)
    q3_in = group_swap(sent3)
    q2_in = group_swap(sent2)
    a2 = ring_down(a3_s2)
    near_c = core_swap(near_sent)

    def turn(v, by):
        rows, columns = v.shape
        shift = (by % teams) * 2 * PAIR
        if not shift:
            return v
        return pack(
            which,
            v.shape,
            [
                (v, (0, rows, shift, columns - shift, 0, 0)),
                (v, (0, rows, 0, shift, 0, columns - shift)),
            ],
        )

    late = add(turn(one, 1), turn(two, 2))
    late_terms = matmul(late, key_value_all, True)
    grad_pairs = [(v, qkv_grad, n) for v, _, n in grad_pairs]
    kept0, sent0, kept1, sent1 = weight_grad(
        grad_pairs, 0, 2 * block, splits=2, source=row_halves, halves=True, step=width // 8
    )
    two_far_branch, two_far_sent = matmul(active_far, contract_all, False, parts=2)
    (
        normed_gb,
        q3_in,
        q2_in,
        a2,
        near_c,
        late_terms,
        sent0,
        sent1,
        two_far_branch,
        two_far_sent,
        active_near,
        out_mine,
    ) = sync(
        normed_gb,
        q3_in,
        q2_in,
        a2,
        near_c,
        late_terms,
        sent0,
        sent1,
        two_far_branch,
        two_far_sent,
        active_near,
        out_mine,
    )
    out_c = core_swap(two_far_sent)
    late_n = core_swap(late_terms[TAIL : 2 * TAIL])
    late_x = chip_swap(late_terms[2 * TAIL : 3 * TAIL])
    late_xc = across_swap(late_terms[3 * TAIL :])
    q3_sum = add(kept3, q3_in)
    a2_s1 = add(a2, add(kept[1], s1_o))
    late_n, late_x, late_xc, q3_sum, a2_s1, sent0, sent1, out_c, active_near, q2_in = sync(
        late_n, late_x, late_xc, q3_sum, a2_s1, sent0, sent1, out_c, active_near, q2_in
    )
    branch_two_xa = chip_swap(add(two_far_branch[:part], out_c[:part]))
    branch_two_in = add(two_far_branch[part:], out_c[part:])
    q1_in = group_swap(sent1)
    qa3 = ring_down(q3_sum)
    normed_grad = near.astype(F32) + near_c.astype(F32) + cat(normed_ga, normed_gb).astype(F32)
    tail = functools.reduce(
        jnp.add, [v.astype(F32) for v in (late_terms[:TAIL], late_n, late_x, late_xc)]
    )
    normed_grad = normed_grad + cat(jnp.zeros((SEG - TAIL, width), F32), tail)
    _, pull_first = jax.vjp(normalize, hidden_in, gain_first, shift_first)
    input_part, first_gain_grad, first_shift_grad = pull_first(normed_grad)
    input_grad = (middle_grad + input_part).astype(BF16)
    qkv_bias_sums = jnp.sum(qkv_grad.astype(F32), axis=0)
    expand_bias_sums = jnp.sum(before_near.astype(F32), axis=0) + jnp.sum(
        before_far.astype(F32), axis=0
    )
    small = jnp.concatenate(
        [
            first_gain_grad,
            first_shift_grad,
            jnp.sum(middle_grad, axis=0),
            second_gain_grad,
            second_shift_grad,
            jnp.sum(cot_local, axis=0),
        ]
    )
    place = block + hid
    owners = jnp.zeros((n_mp * place,), F32)
    for r in range(teams):
        owner = (team + teams - r) % teams
        mine_hid = ordered(
            expand_bias_sums[2 * r * wide : (2 * r + 1) * wide],
            expand_bias_sums[(2 * r + 1) * wide : (2 * r + 2) * wide],
            0,
        )
        piece = jnp.concatenate(
            [qkv_bias_sums[r * block : (r + 1) * block], mine_hid]
        )
        owners = lax.dynamic_update_slice(owners, piece, ((owner * TEAM + mine) * place,))

    vector, q1_in, qa3, branch_two_xa, branch_two_in, sent0, a2_s1 = sync(
        cat(small, owners), q1_in, qa3, branch_two_xa, branch_two_in, sent0, a2_s1
    )

    def add_shifts(shifts, here):
        shifts = jnp.stack(shifts)
        return functools.reduce(jnp.add, [shifts[here(i)] for i in range(shifts.shape[0])])

    shifts = [vector, core_swap(vector), chip_swap(vector), across_swap(vector)]
    q0_in = group_swap(sent0)
    a1 = ring_down(a2_s1)
    qa3_sum = add(qa3, add(kept2, q2_in))
    q0_in, a1, qa3_sum, active_near, *shifts = sync(q0_in, a1, qa3_sum, active_near, *shifts)
    vector = add_shifts(shifts, lambda i: mine ^ i)
    shifts = [vector] + [ring_up(vector, r) for r in range(1, teams)]
    qa2 = ring_down(qa3_sum)
    expand_mine = other_groups(add(a1, add(kept[0], s0_o)))
    expand_other = group_swap(expand_mine)
    two_near_branch, two_near_sent = matmul(active_near, contract_all, False, parts=2)
    qa2, expand_other, two_near_branch, two_near_sent, branch_two_in, out_mine, *shifts = sync(
        qa2, expand_other, two_near_branch, two_near_sent, branch_two_in, out_mine, *shifts
    )
    vector = add_shifts(shifts, lambda i: (team + teams - i) % teams)
    bit = 1
    while bit < n_dp:
        vector = vector + group_swap(vector, bit)
        bit *= 2
    qa1 = ring_down(add(qa2, add(kept1, q1_in)))
    branch_two_xb = chip_swap(branch_two_in)
    two_near_c = core_swap(two_near_sent)
    out_sum = other_groups(out_mine)
    out_other = group_swap(out_sum)
    vector, qa1, branch_two_xb, two_near_c, out_other = sync(
        vector, qa1, branch_two_xb, two_near_c, out_other
    )
    qkv_mine = other_groups(add(qa1, add(kept0, q0_in)))
    qkv_other = group_swap(qkv_mine)
    mine_spot = lax.dynamic_slice(vector, (6 * width + me * place,), (place,))
    six = [vector[k * width : (k + 1) * width] for k in range(6)]

    branch_two = (
        two_near_branch.astype(F32)
        + two_near_c.astype(F32)
        + cat(branch_two_xa, branch_two_xb).astype(F32)
    )
    layer_out = (middle + branch_two + contract_bias.astype(F32)).astype(BF16)
    qkv_final = ordered(qkv_mine, qkv_other, 0).astype(F32)
    return (
        layer_out,
        input_grad,
        six[0],
        six[1],
        qkv_final[:, :cols],
        mine_spot[:cols],
        qkv_final[:, cols : 2 * cols],
        qkv_final[:, 2 * cols :],
        mine_spot[2 * cols : 3 * cols],
        ordered(out_sum, out_other, 0).astype(F32),
        six[2],
        six[3],
        six[4],
        ordered(expand_mine, expand_other, 1).astype(F32),
        mine_spot[block:],
        ordered(contract_sum, contract_other, 0).astype(F32),
        six[5],
    )


def solution(mesh):
    rows = P(("dp", "mp"), None)
    in_cols, in_rows = P(None, "mp"), P("mp", None)
    placed = (
        rows,
        P("dp", None),
        P(),
        P(),
        in_cols,
        P("mp"),
        in_cols,
        in_cols,
        P("mp"),
        in_rows,
        P(),
        P(),
        P(),
        in_cols,
        P("mp"),
        in_rows,
        P(),
        rows,
    )
    return jax.shard_map(
        body,
        mesh=mesh,
        in_specs=placed,
        out_specs=(
            rows,
            rows,
            P(),
            P(),
            in_cols,
            P("mp"),
            in_cols,
            in_cols,
            P("mp"),
            in_rows,
            P(),
            P(),
            P(),
            in_cols,
            P("mp"),
            in_rows,
            P(),
        ),
        check_vma=False,
    )
```

```python
import functools

import jax
import jax.numpy as jnp
from jax import lax
from jax.experimental import pallas as pl
from jax.experimental.pallas import tpu as pltpu
from jax.sharding import PartitionSpec as P

HD = 64
SEG = 512
NSUM = 50
TAIL = 64
TEAM = 4
PAIR = 2 * HD
QB = 256
EPSILON = 1e-05
MASKED = -1e30
LIGHT = pl.CostEstimate(flops=1024, bytes_accessed=1024, transcendentals=0)
F32 = jnp.float32
BF16 = jnp.bfloat16


def gelu_and_slope(v):
    inner = 0.7978845608 * (v + 0.044715 * v * v * v)
    t = jnp.tanh(inner)
    value = 0.5 * v * (1.0 + t)
    slope = 0.5 * (1.0 + t) + 0.5 * v * (1.0 - t * t) * (
        0.7978845608 * (1.0 + 3.0 * 0.044715 * v * v)
    )
    return value, slope


def normalize(values, scaling, offset):
    centre = jnp.mean(values, axis=-1, keepdims=True)
    centred = values - centre
    spread = jnp.mean(centred * centred, axis=-1, keepdims=True)
    return centred * lax.rsqrt(spread + EPSILON) * scaling + offset


def slot_items(counts, slot_count):
    item_ends = jnp.cumsum(counts)
    places = jnp.arange(slot_count, dtype=jnp.int32)
    return jnp.sum((places[:, None] >= item_ends[None, :]).astype(jnp.int32), axis=1)


def dot(a, b):
    return jnp.dot(a, b, preferred_element_type=F32)


def dot_nt(a, b):
    return lax.dot_general(a, b, (((1,), (1,)), ((), ())), preferred_element_type=F32)


def dot_tn(a, b):
    return lax.dot_general(a, b, (((0,), (0,)), ((), ())), preferred_element_type=F32)


def head_only(block, h):
    lane = lax.broadcasted_iota(jnp.int32, block.shape, 1)
    return jnp.where((lane // HD) == h, block, jnp.zeros_like(block))


def causal(block):
    key = lax.broadcasted_iota(jnp.int32, block.shape, 0)
    query = lax.broadcasted_iota(jnp.int32, block.shape, 1)
    return jnp.where(query >= key, block, MASKED)


def hide_rows(block, count):
    key = lax.broadcasted_iota(jnp.int32, block.shape, 0)
    return jnp.where(key >= count, block, MASKED)


def key_blocks(info_ref, e):
    slots = info_ref.shape[0] - 2
    team, mine = info_ref[slots], info_ref[slots + 1]
    i = mine ^ e
    item = info_ref[team * TEAM + i]

    def hidden(other):
        same = info_ref[jnp.maximum(other, 0)] == item
        return jnp.where(jnp.logical_and(other >= 0, same), TAIL - NSUM, TAIL)

    rows = TEAM * SEG
    out = [(rows + 2 * f * TAIL, hidden((team - 1) * TEAM + (mine ^ f))) for f in range(TEAM)]
    for d in range(1, TEAM):
        j = i ^ d
        inside = j < i
        start = jnp.where(
            inside, (e ^ d) * SEG + SEG - TAIL, rows + (2 * (e ^ d) + 1) * TAIL
        )
        out.append((start, hidden(jnp.where(inside, team, team - 2) * TEAM + j)))
    return out


def attend_kernel(first, count, info_ref, qkv_ref, mix_ref, log_ref):
    def segment(e, carry):
        base = pl.multiple_of(e * SEG, SEG)
        place = pl.multiple_of((e - first) * SEG, SEG)
        extra = key_blocks(info_ref, e)
        keys = qkv_ref[pl.ds(base, SEG), PAIR : 2 * PAIR]
        value_t = qkv_ref[pl.ds(base, SEG), 2 * PAIR : 3 * PAIR].T
        extra_keys = [
            qkv_ref[pl.ds(pl.multiple_of(s, TAIL), TAIL), PAIR : 2 * PAIR] for s, _ in extra
        ]
        extra_values = [
            qkv_ref[pl.ds(pl.multiple_of(s, TAIL), TAIL), 2 * PAIR : 3 * PAIR] for s, _ in extra
        ]
        extra_keys = jnp.concatenate(extra_keys, axis=0)
        extra_value_t = jnp.concatenate(extra_values, axis=0).T
        for qb in range(SEG // QB):
            query = qkv_ref[pl.ds(base + qb * QB, QB), 0:PAIR]
            seen = (qb + 1) * QB
            outs = []
            for h in range(2):
                qh = head_only(query, h)
                own = dot_nt(keys[:seen], qh)
                parts = [own[: qb * QB]] if qb else []
                parts.append(causal(own[qb * QB :]))
                far = dot_nt(extra_keys, qh)
                for n, (_, hidden) in enumerate(extra):
                    parts.append(hide_rows(far[n * TAIL : (n + 1) * TAIL], hidden))
                high = functools.reduce(
                    jnp.maximum, [jnp.max(p, axis=0, keepdims=True) for p in parts]
                )
                parts = [jnp.exp(p - high) for p in parts]
                total = functools.reduce(
                    jnp.add, [jnp.sum(p, axis=0, keepdims=True) for p in parts]
                )
                cut = 2 if qb else 1
                p_own = jnp.concatenate([p.astype(BF16) for p in parts[:cut]], axis=0)
                p_far = jnp.concatenate([p.astype(BF16) for p in parts[cut:]], axis=0)
                rows = slice(h * HD, (h + 1) * HD)
                mixed = dot(value_t[rows, :seen], p_own) + dot(extra_value_t[rows], p_far)
                outs.append(mixed / total)
                log_ref[0, e - first, h : h + 1, qb * QB : (qb + 1) * QB] = high + jnp.log(total)
            mix_ref[pl.ds(place + qb * QB, QB), :] = jnp.concatenate(outs, axis=0).T.astype(BF16)
        return carry

    lax.fori_loop(first, first + count, segment, 0)


def attend(info, qkv, first, count):
    pieces = qkv.shape[1] // (3 * PAIR)
    rows = count * SEG
    return pl.pallas_call(
        functools.partial(attend_kernel, first, count),
        grid_spec=pltpu.PrefetchScalarGridSpec(
            num_scalar_prefetch=1,
            grid=(pieces,),
            in_specs=[pl.BlockSpec((qkv.shape[0], 3 * PAIR), lambda r, t: (0, r))],
            out_specs=[
                pl.BlockSpec((rows, PAIR), lambda r, t: (0, r)),
                pl.BlockSpec((1, count, 2, SEG), lambda r, t: (r, 0, 0, 0)),
            ],
        ),
        out_shape=[
            jax.ShapeDtypeStruct((rows, pieces * PAIR), BF16),
            jax.ShapeDtypeStruct((pieces, count, 2, SEG), F32),
        ],
        compiler_params=pltpu.CompilerParams(vmem_limit_bytes=56 * 1024 * 1024),
        cost_estimate=LIGHT,
        name="attend",
    )(info, qkv)


def attend_back_kernel(first, count, info_ref, qkv_ref, mix_ref, grad_ref, log_ref, *rest):
    key_acc, value_acc = rest[-2:]
    if len(rest) == 6:
        before_ref, out_ref = rest[:2]
        key_acc[...] = before_ref[:, PAIR : 2 * PAIR].astype(F32)
        value_acc[...] = before_ref[:, 2 * PAIR : 3 * PAIR].astype(F32)
        out_ref[:, 0:PAIR] = before_ref[:, 0:PAIR]
    else:
        out_ref = rest[0]
        key_acc[...] = jnp.zeros_like(key_acc)
        value_acc[...] = jnp.zeros_like(value_acc)
        out_ref[:, 0:PAIR] = jnp.zeros((out_ref.shape[0], PAIR), BF16)

    def segment(e, carry):
        base = pl.multiple_of(e * SEG, SEG)
        place = pl.multiple_of((e - first) * SEG, SEG)
        extra = key_blocks(info_ref, e)
        keys = qkv_ref[pl.ds(base, SEG), PAIR : 2 * PAIR]
        values = qkv_ref[pl.ds(base, SEG), 2 * PAIR : 3 * PAIR]
        key_t = keys.T
        extra_keys = jnp.concatenate(
            [qkv_ref[pl.ds(pl.multiple_of(s, TAIL), TAIL), PAIR : 2 * PAIR] for s, _ in extra],
            axis=0,
        )
        extra_values = jnp.concatenate(
            [qkv_ref[pl.ds(pl.multiple_of(s, TAIL), TAIL), 2 * PAIR : 3 * PAIR] for s, _ in extra],
            axis=0,
        )
        extra_key_t = extra_keys.T
        for qb in range(SEG // QB):
            here = pl.ds(base + qb * QB, QB)
            query = qkv_ref[here, 0:PAIR]
            grad = grad_ref[pl.ds(place + qb * QB, QB), :]
            both = (grad.astype(F32) * mix_ref[pl.ds(place + qb * QB, QB), :].astype(F32)).T
            seen = (qb + 1) * QB
            key_own, value_own, key_far, value_far = 0.0, 0.0, 0.0, 0.0
            query_grads = []
            for h in range(2):
                rows = slice(h * HD, (h + 1) * HD)
                qh, gh = head_only(query, h), head_only(grad, h)
                centre = jnp.sum(both[rows], axis=0, keepdims=True)
                log = log_ref[0, e - first, h : h + 1, qb * QB : (qb + 1) * QB]
                own = dot_nt(keys[:seen], qh)
                parts = [own[: qb * QB]] if qb else []
                parts.append(causal(own[qb * QB :]))
                own = jnp.exp((jnp.concatenate(parts, axis=0) if qb else parts[0]) - log)
                far = dot_nt(extra_keys, qh)
                far = jnp.concatenate(
                    [
                        hide_rows(far[n * TAIL : (n + 1) * TAIL], hidden)
                        for n, (_, hidden) in enumerate(extra)
                    ],
                    axis=0,
                )
                far = jnp.exp(far - log)
                own_step = (own * (dot_nt(values[:seen], gh) - centre)).astype(BF16)
                far_step = (far * (dot_nt(extra_values, gh) - centre)).astype(BF16)
                value_own += dot(own.astype(BF16), gh)
                value_far += dot(far.astype(BF16), gh)
                key_own += dot(own_step, qh)
                key_far += dot(far_step, qh)
                query_grads.append(dot(key_t[rows, :seen], own_step) + dot(extra_key_t[rows], far_step))
            query_grad = jnp.concatenate(query_grads, axis=0).T * (HD**-0.5)
            out_ref[here, 0:PAIR] = query_grad.astype(BF16)
            key_acc[pl.ds(base, seen), :] += key_own
            value_acc[pl.ds(base, seen), :] += value_own
            for n, (s, _) in enumerate(extra):
                there = pl.ds(pl.multiple_of(s, TAIL), TAIL)
                key_acc[there, :] += key_far[n * TAIL : (n + 1) * TAIL]
                value_acc[there, :] += value_far[n * TAIL : (n + 1) * TAIL]
        return carry

    lax.fori_loop(first, first + count, segment, 0)
    out_ref[:, PAIR : 2 * PAIR] = key_acc[...].astype(BF16)
    out_ref[:, 2 * PAIR : 3 * PAIR] = value_acc[...].astype(BF16)
    if len(rest) == 6:
        for f in range(TEAM):
            for k, far_ref in enumerate(rest[2:4]):
                at = TEAM * SEG + (2 * f + k) * TAIL
                here = slice(f * TAIL, (f + 1) * TAIL)
                far_ref[here, :PAIR] = key_acc[at : at + TAIL, :].astype(BF16)
                far_ref[here, PAIR:] = value_acc[at : at + TAIL, :].astype(BF16)


def attend_back(info, qkv, mixture, grad, logs, first, count, before=None):
    pieces = qkv.shape[1] // (3 * PAIR)
    rows = count * SEG
    wide = pl.BlockSpec((qkv.shape[0], 3 * PAIR), lambda r, t: (0, r))
    narrow = pl.BlockSpec((rows, PAIR), lambda r, t: (0, r))
    more = () if before is None else (before,)
    return pl.pallas_call(
        functools.partial(attend_back_kernel, first, count),
        grid_spec=pltpu.PrefetchScalarGridSpec(
            num_scalar_prefetch=1,
            grid=(pieces,),
            in_specs=[
                wide,
                narrow,
                narrow,
                pl.BlockSpec((1, count, 2, SEG), lambda r, t: (r, 0, 0, 0)),
            ]
            + [wide] * len(more),
            out_specs=[wide] + [pl.BlockSpec((TEAM * TAIL, 2 * PAIR), lambda r, t: (0, r))] * (2 * len(more)),
            scratch_shapes=[
                pltpu.VMEM((qkv.shape[0], PAIR), F32),
                pltpu.VMEM((qkv.shape[0], PAIR), F32),
            ],
        ),
        out_shape=[jax.ShapeDtypeStruct(qkv.shape, BF16)]
        + [jax.ShapeDtypeStruct((TEAM * TAIL, pieces * 2 * PAIR), BF16)] * (2 * len(more)),
        compiler_params=pltpu.CompilerParams(vmem_limit_bytes=56 * 1024 * 1024),
        cost_estimate=LIGHT,
        name="attend_back",
    )(info, qkv, mixture, grad, logs, *more)


def weight_grad_kernel(splits, halves, pairs, source_ref, target_ref, *refs):
    outs = refs[2 * pairs :]
    total = None
    for left, right in zip(refs[: 2 * pairs : 2], refs[1 : 2 * pairs : 2]):
        term = dot_tn(left[...], right[...])
        total = term if total is None else total + term
    total = total.astype(BF16)
    width = total.shape[1] // splits
    columns = [total[:, k * width : (k + 1) * width] for k in range(splits)]
    if not halves:
        for k in range(splits):
            outs[k][...] = columns[k]
        return
    step, steps = pl.program_id(0), pl.num_programs(0)

    @pl.when(step < steps // 2)
    def _():
        for k in range(splits):
            outs[2 * k][...] = columns[k]

    @pl.when(step >= steps // 2)
    def _():
        for k in range(splits):
            outs[2 * k + 1][...] = columns[k]


def weight_grad(pairs, column=0, columns=None, step=256, splits=1, source=None, target=None, halves=False):
    height = pairs[0][0].shape[1]
    columns = columns or pairs[0][1].shape[1]
    steps, width = height // step, columns // splits
    plain = jnp.arange(steps, dtype=jnp.int32)
    specs = []
    for left, right, n in pairs:
        specs.append(pl.BlockSpec((left.shape[0], step), lambda i, s, t: (0, s[i])))
        specs.append(pl.BlockSpec((left.shape[0], columns), lambda i, s, t, n=n: (n, column)))
    if halves:
        outs = [
            pl.BlockSpec((step, width), lambda i, s, t: (jnp.minimum(i, steps // 2 - 1), 0)),
            pl.BlockSpec((step, width), lambda i, s, t: (jnp.maximum(i - steps // 2, 0), 0)),
        ] * splits
        shapes = [jax.ShapeDtypeStruct((height // 2, width), BF16)] * (2 * splits)
    else:
        outs = [pl.BlockSpec((step, width), lambda i, s, t: (t[i], 0))] * splits
        shapes = [jax.ShapeDtypeStruct((height, width), BF16)] * splits
    return pl.pallas_call(
        functools.partial(weight_grad_kernel, splits, halves, len(pairs)),
        grid_spec=pltpu.PrefetchScalarGridSpec(
            num_scalar_prefetch=2, grid=(steps,), in_specs=specs, out_specs=outs
        ),
        out_shape=shapes,
        compiler_params=pltpu.CompilerParams(vmem_limit_bytes=56 * 1024 * 1024),
        cost_estimate=LIGHT,
        name="weight_grad",
    )(
        plain if source is None else source,
        plain if target is None else target,
        *[v for pair in pairs for v in pair[:2]],
    )


def pack_kernel(plan, which_ref, *refs):
    sources, out_ref, sems = refs[:-2], refs[-2], refs[-1]
    copies = []
    for n, (ref, (row, rows, column, columns, at_row, at_column)) in enumerate(zip(sources, plan)):
        if at_row == "held":
            at_row = pl.multiple_of(which_ref[0] * rows, rows)
        elif at_row == "other":
            at_row = pl.multiple_of((1 - which_ref[0]) * rows, rows)
        copies.append(
            pltpu.make_async_copy(
                ref.at[pl.ds(row, rows), pl.ds(column, columns)],
                out_ref.at[pl.ds(at_row, rows), pl.ds(at_column, columns)],
                sems.at[n],
            )
        )
    for copy in copies:
        copy.start()
    for copy in copies:
        copy.wait()


def pack(which, shape, parts):
    return pl.pallas_call(
        functools.partial(pack_kernel, [plan for _, plan in parts]),
        grid_spec=pltpu.PrefetchScalarGridSpec(
            num_scalar_prefetch=1,
            grid=(),
            in_specs=[pl.BlockSpec(memory_space=pl.ANY)] * len(parts),
            out_specs=pl.BlockSpec(memory_space=pltpu.VMEM),
            scratch_shapes=[pltpu.SemaphoreType.DMA((len(parts),))],
        ),
        out_shape=jax.ShapeDtypeStruct(shape, BF16),
        compiler_params=pltpu.CompilerParams(vmem_limit_bytes=32 * 1024 * 1024),
        cost_estimate=LIGHT,
        name="pack",
    )(which, *[v for v, _ in parts])


def pack_rows(which, parts):
    columns, row, plan = parts[0].shape[1], 0, []
    for v in parts:
        plan.append((v, (0, v.shape[0], 0, columns, row, 0)))
        row += v.shape[0]
    return pack(which, (row, columns), plan)


def pack_columns(which, parts, rows):
    column, plan = 0, []
    for v in parts:
        plan.append((v, (0, rows, 0, v.shape[1], 0, column)))
        column += v.shape[1]
    return pack(which, (rows, column), plan)


def project_kernel(pieces, which_ref, *refs):
    weights, rows, out_ref, first, last = (
        refs[: 2 * pieces],
        refs[2 * pieces : -3],
        refs[-3],
        refs[-2],
        refs[-1],
    )
    depth, block = first.shape[0], first.shape[1] // pieces
    for n in range(pieces):
        first[:, n * block : (n + 1) * block] = weights[2 * n][:depth, :block]
        last[:, n * block : (n + 1) * block] = weights[2 * n + 1][:depth, :block]
    bias = jnp.concatenate(
        [weights[2 * n][depth : depth + 1, :block].astype(F32) for n in range(pieces)], axis=1
    )
    lane = lax.broadcasted_iota(jnp.int32, bias.shape, 1)
    scale = jnp.where(lane % block < PAIR, HD**-0.5, 1.0)
    held = pl.ds(pl.multiple_of(which_ref[0] * depth, depth), depth)
    other = pl.ds(pl.multiple_of((1 - which_ref[0]) * depth, depth), depth)
    at = 0
    for ref in rows:
        chunk = min(256, ref.shape[0])
        for start in range(0, ref.shape[0], chunk):
            here = slice(start, start + chunk)
            value = dot(ref[here, held], first[...]) + dot(ref[here, other], last[...])
            out_ref[at + start : at + start + chunk, :] = ((value + bias) * scale).astype(BF16)
        at += ref.shape[0]


def project(which, weights, rows):
    pieces = len(weights)
    depth, block = rows[0].shape[1] // 2, 3 * PAIR
    height = sum(v.shape[0] for v in rows)
    return pl.pallas_call(
        functools.partial(project_kernel, pieces),
        grid_spec=pltpu.PrefetchScalarGridSpec(
            num_scalar_prefetch=1,
            grid=(),
            in_specs=[pl.BlockSpec(memory_space=pltpu.VMEM)] * (2 * pieces + len(rows)),
            out_specs=pl.BlockSpec(memory_space=pltpu.VMEM),
            scratch_shapes=[pltpu.VMEM((depth, pieces * block), BF16)] * 2,
        ),
        out_shape=jax.ShapeDtypeStruct((height, pieces * block), BF16),
        compiler_params=pltpu.CompilerParams(vmem_limit_bytes=56 * 1024 * 1024),
        cost_estimate=LIGHT,
        name="project",
    )(which, *[v for pair in weights for v in pair], *rows)


def matmul_kernel(transposed, parts, left_ref, right_ref, *rest):
    outs = rest[-parts:]
    rows = left_ref.shape[0] // parts
    chunk = min(256, rows)
    for start in range(0, left_ref.shape[0], chunk):
        here = slice(start, start + chunk)
        value = (dot_nt if transposed else dot)(left_ref[here, :], right_ref[...])
        if len(rest) > parts:
            value = value * rest[0][here, :].astype(F32)
        at = start % rows
        outs[start // rows][at : at + chunk, :] = value.astype(BF16)


def matmul(left, right, transposed, scale=None, place=0, rows=None, step=512, parts=1):
    rows = rows or left.shape[0]
    depth = left.shape[1]
    columns = right.shape[0] if transposed else right.shape[1]
    right_spec = (
        pl.BlockSpec((step, depth), lambda i: (i, 0))
        if transposed
        else pl.BlockSpec((depth, step), lambda i: (0, i))
    )
    more = () if scale is None else (scale,)
    out = pl.pallas_call(
        functools.partial(matmul_kernel, transposed, parts),
        grid=(columns // step,),
        in_specs=[pl.BlockSpec((rows, depth), lambda i: (place, 0)), right_spec]
        + [pl.BlockSpec((rows, step), lambda i: (0, i))] * len(more),
        out_specs=[pl.BlockSpec((rows // parts, step), lambda i: (0, i))] * parts,
        out_shape=[jax.ShapeDtypeStruct((rows // parts, columns), BF16)] * parts,
        compiler_params=pltpu.CompilerParams(vmem_limit_bytes=56 * 1024 * 1024),
        cost_estimate=LIGHT,
        name="matmul",
    )(left, right, *more)
    return out if parts > 1 else out[0]


def body(
    inputs,
    item_counts,
    first_gain,
    first_shift,
    query_weight,
    query_bias,
    key_weight,
    value_weight,
    value_bias,
    output_weight,
    output_bias,
    second_gain,
    second_shift,
    expand_weight,
    expand_bias,
    contract_weight,
    contract_bias,
    cotangent,
):
    n_mp, n_dp = lax.axis_size("mp"), lax.axis_size("dp")
    teams = n_mp // TEAM
    me = lax.axis_index("mp")
    team, mine = me // TEAM, me % TEAM
    second = lax.axis_index("dp") % 2

    def core_swap(v):
        return lax.ppermute(v, "mp", [(i, i ^ 1) for i in range(n_mp)])

    def chip_swap(v):
        return lax.ppermute(v, "mp", [(i, i ^ 2) for i in range(n_mp)])

    def ring_up(v, by=1):
        return lax.ppermute(v, "mp", [(i, (i + by * TEAM) % n_mp) for i in range(n_mp)])

    def ring_down(v):
        return lax.ppermute(v, "mp", [(i, (i - TEAM) % n_mp) for i in range(n_mp)])

    def line_up(v, by=1):
        return lax.ppermute(v, "mp", [(i, i + by * TEAM) for i in range(n_mp - by * TEAM)])

    def line_down(v, by=1):
        return lax.ppermute(v, "mp", [(i + by * TEAM, i) for i in range(n_mp - by * TEAM)])

    def group_swap(v, bit=1):
        return lax.ppermute(v, "dp", [(i, i ^ bit) for i in range(n_dp)])

    def half(v, axis, which):
        size = v.shape[axis] // 2
        return lax.dynamic_slice_in_dim(v, which * size, size, axis)

    def ordered(held, other, axis):
        return jnp.where(
            second == 0,
            jnp.concatenate([held, other], axis=axis),
            jnp.concatenate([other, held], axis=axis),
        )

    def add(*terms):
        return functools.reduce(jnp.add, [t.astype(F32) for t in terms]).astype(BF16)

    def other_groups(v):
        bit = 2
        while bit < n_dp:
            v = add(v, group_swap(v, bit))
            bit *= 2
        return v

    def sync(*values):
        return lax.optimization_barrier(values)

    slot_count = teams * TEAM
    items = slot_items(item_counts[0], slot_count)
    info = jnp.pad(items, (0, 2))
    at = lax.iota(jnp.int32, slot_count + 2)
    info = jnp.where(at == slot_count, team, jnp.where(at == slot_count + 1, mine, info))

    gain_first, shift_first = first_gain.astype(F32), first_shift.astype(F32)
    gain_second, shift_second = second_gain.astype(F32), second_shift.astype(F32)
    width = inputs.shape[1]
    cols = query_bias.shape[0]
    hid = expand_bias.shape[0]
    wide = hid // 2
    team_rows, near_rows = TEAM * SEG, 2 * SEG
    span = TEAM * TAIL
    block = 3 * PAIR
    pad = 16

    def across_swap(v):
        return lax.ppermute(v, "mp", [(i, i ^ 3) for i in range(n_mp)])

    def with_bias(weight, bias):
        return jnp.concatenate(
            [weight, jnp.broadcast_to(bias[None], (pad, bias.shape[0]))], axis=0
        )

    def send_in(terms):
        size = terms.shape[0] // 2
        return add(terms[:size], core_swap(terms[size:]))

    along = [[t * TEAM + i for t in range(teams)] for i in range(TEAM)]
    part = SEG // 2
    pairs_along = [
        [(first + d) * n_mp + t * TEAM + i for t in range(teams) for d in range(2)]
        for first in range(0, n_dp, 2)
        for i in range(TEAM)
    ]

    def scatter_sum(v):
        return lax.psum_scatter(
            v, ("dp", "mp"), scatter_dimension=0, axis_index_groups=pairs_along, tiled=True
        )

    def cat(*parts, axis=0):
        return jnp.concatenate(parts, axis=axis)

    which = jnp.reshape(second, (1,)).astype(jnp.int32)

    qkv_local = cat(query_weight, key_weight, value_weight, output_weight.T, axis=1)
    qkv_bias_local = cat(
        query_bias, jnp.zeros_like(query_bias), value_bias, jnp.zeros_like(query_bias)
    )
    packed = with_bias(half(qkv_local, 0, second), qkv_bias_local)
    q0_o = half(qkv_local, 0, 1 - second)
    hidden_in = inputs.astype(F32)
    normed = normalize(hidden_in, gain_first, shift_first).astype(BF16)
    packed, normed, normed_tail = sync(packed, normed, normed[SEG - TAIL :])
    q1 = ring_up(packed)
    normed_xa = chip_swap(normed[:part])
    normed_c = core_swap(normed)
    early = line_up(normed_tail)
    normed_b = normed[part:]
    q1, normed_xa, normed_c, early, normed_b = sync(q1, normed_xa, normed_c, early, normed_b)
    q2 = ring_up(q1)
    normed_xb = chip_swap(normed_b)
    q1_o = group_swap(q1)
    earlier = line_up(early)
    q2, q1_o, normed_x, rest = sync(q2, q1_o, cat(normed_xa, normed_xb), cat(early, earlier))
    q3 = ring_up(q2)
    q2_o = group_swap(q2)
    normed_xc = core_swap(normed_x)
    rest_x = chip_swap(rest)
    rest_xc = across_swap(rest)
    rest_c = core_swap(rest)
    tops = width // 2
    expand_own, expand_rest = half(expand_weight, 1, second), half(expand_weight, 1, 1 - second)
    expand_bias_own = half(expand_bias, 0, second)
    expand_bias_rest = half(expand_bias, 0, 1 - second)
    q3, q2_o, normed_xc, rest_x, rest_xc, rest_c, cot_a, cot_b, e0 = sync(
        q3,
        q2_o,
        normed_xc,
        rest_x,
        rest_xc,
        rest_c,
        cotangent[:part],
        cotangent[part:],
        with_bias(expand_own, expand_bias_own),
    )
    q3_o = group_swap(q3)
    e1 = ring_up(e0)
    cot_xa = chip_swap(cot_a)
    row_blocks = [normed, normed_c, normed_x, normed_xc, rest, rest_c, rest_x, rest_xc]
    qkv_a = project(which, [(packed, q0_o), (q1, q1_o), (q2, q2_o)], row_blocks)
    q3_o, cot_xa, qkv_a, e1, cot_b, cot = sync(q3_o, cot_xa, qkv_a, e1, cot_b, cotangent)
    e2 = ring_up(e1)
    e1_o = group_swap(e1)
    cot_xb = chip_swap(cot_b)
    cot_c = core_swap(cot)
    mix_far_a, log_far_a = attend(info, qkv_a, 2, 2)
    qkv_b = project(which, [(q3, q3_o)], row_blocks)
    mix_far_b, log_far_b = attend(info, qkv_b, 2, 2)
    held_pieces = ((packed, q0_o), (q1, q1_o), (q2, q2_o), (q3, q3_o))

    def whole(pieces, column, columns):
        plan = []
        for n, (v, o) in enumerate(pieces):
            plan.append((v, (0, tops, column, columns, "held", n * columns)))
            plan.append((o, (0, tops, column, columns, "other", n * columns)))
        return pack(which, (width, len(pieces) * columns), plan)

    out_all = whole(held_pieces, block, cols)
    mix_far = pack_columns(which, [mix_far_a, mix_far_b], near_rows)
    far, far_sent = matmul(mix_far, out_all, True, parts=2)
    cot_x = pack_rows(which, [cot_xa, cot_xb])
    e2, e1_o, cot_x, cot_c, qkv_a, qkv_b, far, far_sent, out_all, contract_weight = sync(
        e2, e1_o, cot_x, cot_c, qkv_a, qkv_b, far, far_sent, out_all, contract_weight
    )
    far_c = core_swap(far_sent)
    contract_own = half(contract_weight, 0, second)
    contract_rest = half(contract_weight, 0, 1 - second)
    far, far_c, qkv_a = sync(far, far_c, qkv_a)
    branch_in = add(far[part:], far_c[part:])
    branch_xa = chip_swap(add(far[:part], far_c[:part]))
    e3 = ring_up(e2)
    e2_o = group_swap(e2)
    mix_near_a, log_near_a = attend(info, qkv_a, 0, 2)
    branch_xa, e3, e2_o, mix_near_a, branch_in, contract_own, qkv_b = sync(
        branch_xa, e3, e2_o, mix_near_a, branch_in, contract_own, qkv_b
    )
    branch_xb = chip_swap(branch_in)
    cot_xc = core_swap(cot_x)
    k1 = ring_up(contract_own)
    e3_o = group_swap(e3)
    mix_near_b, log_near_b = attend(info, qkv_b, 0, 2)
    mix_near = pack_columns(which, [mix_near_a, mix_near_b], near_rows)
    near, near_sent = matmul(mix_near, out_all, True, parts=2)
    branch_xb, k1, e3_o, near, near_sent, mix_near, cot_xc = sync(
        branch_xb, k1, e3_o, near, near_sent, mix_near, cot_xc
    )
    near_c = core_swap(near_sent)
    near, near_c, k1 = sync(near, near_c, k1)
    branch_x = cat(branch_xa, branch_xb)
    branch = near.astype(F32) + near_c.astype(F32) + branch_x.astype(F32)
    middle = hidden_in + branch + output_bias.astype(F32)
    normed_two = normalize(middle, gain_second, shift_second).astype(BF16)
    normed_two, k1, e3_o, *held = sync(normed_two, k1, e3_o, *[v for p in held_pieces for v in p])
    two_xa = chip_swap(normed_two[:part])
    two_c = core_swap(normed_two)
    k2 = ring_up(k1)
    k1_o = group_swap(k1)
    expand_pairs = (e1, e1_o, e2, e2_o, e3, e3_o)
    expand_all = pack_columns(which, [expand_own, expand_rest, *expand_pairs], width)
    held = tuple(zip(held[0::2], held[1::2]))
    qkv_all = whole(held, 0, block)
    key_value_all = whole(held, PAIR, 2 * PAIR)
    expand_bias_all = cat(
        expand_bias_own, expand_bias_rest, *[v[width] for v in expand_pairs]
    ).astype(F32)
    two_xa, two_c, k2, k1_o, expand_all, expand_bias_all, normed_two, qkv_all, key_value_all = sync(
        two_xa, two_c, k2, k1_o, expand_all, expand_bias_all, normed_two, qkv_all, key_value_all
    )
    two_xb = chip_swap(normed_two[part:])
    k3 = ring_up(k2)
    k2_o = group_swap(k2)

    def front(rows):
        value, slope = gelu_and_slope(dot(rows, expand_all) + expand_bias_all)
        return value.astype(BF16), slope.astype(BF16)

    two_xac = core_swap(two_xa)
    two_near = pack_rows(which, [normed_two, two_c])
    active_near, slope_near = front(two_near)
    two_xb, k3, k2_o, active_near, slope_near, two_near, two_xac = sync(
        two_xb, k3, k2_o, active_near, slope_near, two_near, two_xac
    )
    two_xbc = core_swap(two_xb)
    two_xbc, k3, qkv_a, qkv_b, cot_c = sync(two_xbc, k3, qkv_a, qkv_b, cot_c)
    k3_o = group_swap(k3)
    two_far = pack_rows(which, [two_xa, two_xb, two_xac, two_xbc])
    active_far, slope_far = front(two_far)
    qkv = pack_columns(which, [qkv_a, qkv_b], qkv_a.shape[0])
    k3_o, active_far, slope_far, two_far, cot_x = sync(k3_o, active_far, slope_far, two_far, cot_x)
    contract_all = pack_rows(which, [contract_own, contract_rest, k1, k1_o, k2, k2_o, k3, k3_o])
    cot_far = pack_rows(which, [cot_x, cot_xc])
    before_far = matmul(cot_far, contract_all, True, slope_far)
    far, far_sent = matmul(before_far, expand_all, True, parts=2)
    far, far_sent, before_far, contract_all = sync(far, far_sent, before_far, contract_all)
    far_c = core_swap(far_sent)
    cot_near = pack_rows(which, [cot, cot_c])
    far, far_c, cot_near, slope_near = sync(far, far_c, cot_near, slope_near)
    two_grad_in = add(far[part:], far_c[part:])
    two_grad_xa = chip_swap(add(far[:part], far_c[:part]))
    before_near = matmul(cot_near, contract_all, True, slope_near)
    near, near_sent = matmul(before_near, expand_all, True, parts=2)
    two_grad_xa, two_grad_in, before_near, near, near_sent, active_near = sync(
        two_grad_xa, two_grad_in, before_near, near, near_sent, active_near
    )
    two_grad_xb = chip_swap(two_grad_in)
    near_c = core_swap(near_sent)
    hidden_order = []
    for r in range(teams):
        owner = (team + teams - r) % teams
        hidden_order += [owner * 2 + second, owner * 2 + 1 - second]
    hidden_order = jnp.stack(hidden_order).astype(jnp.int32)
    (contract_grad,) = weight_grad(
        [(active_near, cot_near, 0), (active_far, cot_far, 0)], step=wide, target=hidden_order
    )
    two_grad_xb, contract_grad, near, near_c = sync(two_grad_xb, contract_grad, near, near_c)
    contract_mine = scatter_sum(contract_grad)
    normed_two_grad = (
        near.astype(F32)
        + near_c.astype(F32)
        + cat(two_grad_xa, two_grad_xb).astype(F32)
    )
    cot_local = cotangent.astype(F32)
    _, pull_second = jax.vjp(normalize, middle, gain_second, shift_second)
    middle_part, second_gain_grad, second_shift_grad = pull_second(normed_two_grad)
    middle_grad = cot_local + middle_part
    middle_low, before_near, active_far = sync(middle_grad.astype(BF16), before_near, active_far)
    middle_xa = chip_swap(middle_low[:part])
    middle_c = core_swap(middle_low)
    expand_parts = weight_grad(
        [(two_near, before_near, 0), (two_far, before_far, 0)], splits=2 * teams
    )
    kept, sent = expand_parts[0::2], expand_parts[1::2]
    middle_low_b = middle_low[part:]
    middle_xa, middle_c, middle_low, middle_low_b, *sent = sync(
        middle_xa, middle_c, middle_low, middle_low_b, *sent
    )
    middle_xb = chip_swap(middle_low_b)
    middle_xac = core_swap(middle_xa)
    s3_o = group_swap(sent[3])
    middle_near = pack_rows(which, [middle_low, middle_c])
    mix_grad_near = matmul(middle_near, out_all, False)
    log_near = cat(log_near_a, log_near_b)
    (part_grad,) = attend_back(info, qkv, mix_near, mix_grad_near, log_near, 0, 2)
    middle_xb, s3_o, part_grad, middle_near, active_far, middle_xac, *sent = sync(
        middle_xb, s3_o, part_grad, middle_near, active_far, middle_xac, *sent
    )
    middle_xbc = core_swap(middle_xb)
    s3 = add(kept[3], s3_o)
    middle_xbc, s3, *sent = sync(middle_xbc, s3, *sent)
    s2_o = group_swap(sent[2])
    s1_o = group_swap(sent[1])
    a3 = ring_down(s3)
    middle_far = pack_rows(which, [middle_xa, middle_xb, middle_xac, middle_xbc])
    mix_grad_far = matmul(middle_far, out_all, False)
    log_far = cat(log_far_a, log_far_b)
    qkv_grad, one, two = attend_back(
        info, qkv, mix_far, mix_grad_far, log_far, 2, 2, part_grad
    )
    far, far_sent = matmul(qkv_grad, qkv_all, True, place=1, rows=near_rows, parts=2)
    place_order = jnp.stack([(team + teams - r) % teams for r in range(teams)]).astype(jnp.int32)
    (out_grad,) = weight_grad(
        [(sync(mix_near, far)[0], middle_near, 0), (mix_far, middle_far, 0)], step=cols, target=place_order
    )
    s2_o, s1_o, a3, far, far_sent, qkv_grad, contract_mine, one, two, sent0, out_grad = sync(
        s2_o, s1_o, a3, far, far_sent, qkv_grad, contract_mine, one, two, sent[0], out_grad
    )
    far_c = core_swap(far_sent)
    far, far_c, qkv_grad, out_grad = sync(far, far_c, qkv_grad, out_grad)
    out_mine = scatter_sum(out_grad)
    normed_in = add(far[part:], far_c[part:])
    normed_ga = chip_swap(add(far[:part], far_c[:part]))
    one = line_down(one)
    two = line_down(two, 2)
    s0_o = group_swap(sent0)
    contract_sum = other_groups(contract_mine)
    contract_other = group_swap(contract_sum)
    row_halves = jnp.arange(8, dtype=jnp.int32)
    row_halves = jnp.where(second == 0, row_halves, (row_halves + 4) % 8)
    grad_pairs = [
        (v, qkv_grad, n)
        for n, v in enumerate([normed, normed_c, normed_x, normed_xc, pack_rows(which, [rest, rest_c, rest_x, rest_xc])])
    ]
    kept2, sent2, kept3, sent3 = weight_grad(
        grad_pairs, 1, 2 * block, splits=2, source=row_halves, halves=True, step=width // 8
    )
    near, near_sent = matmul(qkv_grad, qkv_all, True, place=0, rows=near_rows, parts=2)
    a3_s2 = add(a3, add(kept[2], s2_o))
    (
        normed_ga,
        normed_in,
        one,
        two,
        s0_o,
        sent2,
        sent3,
        near,
        near_sent,
        qkv_grad,
        a3_s2,
        active_far,
        contract_other,
    ) = sync(
        normed_ga,
        normed_in,
        one,
        two,
        s0_o,
        sent2,
        sent3,
        near,
        near_sent,
        qkv_grad,
        a3_s2,
        active_far,
        contract_other,
    )
    normed_gb = chip_swap(normed_in)
    q3_in = group_swap(sent3)
    q2_in = group_swap(sent2)
    a2 = ring_down(a3_s2)
    near_c = core_swap(near_sent)

    def turn(v, by):
        rows, columns = v.shape
        shift = (by % teams) * 2 * PAIR
        if not shift:
            return v
        return pack(
            which,
            v.shape,
            [
                (v, (0, rows, shift, columns - shift, 0, 0)),
                (v, (0, rows, 0, shift, 0, columns - shift)),
            ],
        )

    late = add(turn(one, 1), turn(two, 2))
    late_terms = matmul(late, key_value_all, True)
    grad_pairs = [(v, qkv_grad, n) for v, _, n in grad_pairs]
    kept0, sent0, kept1, sent1 = weight_grad(
        grad_pairs, 0, 2 * block, splits=2, source=row_halves, halves=True, step=width // 8
    )
    two_far_branch, two_far_sent = matmul(active_far, contract_all, False, parts=2)
    (
        normed_gb,
        q3_in,
        q2_in,
        a2,
        near_c,
        late_terms,
        sent0,
        sent1,
        two_far_branch,
        two_far_sent,
        active_near,
        out_mine,
    ) = sync(
        normed_gb,
        q3_in,
        q2_in,
        a2,
        near_c,
        late_terms,
        sent0,
        sent1,
        two_far_branch,
        two_far_sent,
        active_near,
        out_mine,
    )
    late_n = core_swap(late_terms[TAIL : 2 * TAIL])
    late_x = chip_swap(late_terms[2 * TAIL : 3 * TAIL])
    late_xc = across_swap(late_terms[3 * TAIL :])
    q1_in = group_swap(sent1)
    a1 = ring_down(add(a2, add(kept[1], s1_o)))
    q3_sum = add(kept3, q3_in)
    late_n, late_x, late_xc, q1_in, a1, q3_sum, sent0, active_near, q2_in, two_far_sent = sync(
        late_n, late_x, late_xc, q1_in, a1, q3_sum, sent0, active_near, q2_in, two_far_sent
    )
    out_c = core_swap(two_far_sent)
    q0_in = group_swap(sent0)
    qa3 = ring_down(q3_sum)
    normed_grad = near.astype(F32) + near_c.astype(F32) + cat(normed_ga, normed_gb).astype(F32)
    tail = functools.reduce(
        jnp.add, [v.astype(F32) for v in (late_terms[:TAIL], late_n, late_x, late_xc)]
    )
    normed_grad = normed_grad + cat(jnp.zeros((SEG - TAIL, width), F32), tail)
    _, pull_first = jax.vjp(normalize, hidden_in, gain_first, shift_first)
    input_part, first_gain_grad, first_shift_grad = pull_first(normed_grad)
    input_grad = (middle_grad + input_part).astype(BF16)
    qkv_bias_sums = jnp.sum(qkv_grad.astype(F32), axis=0)
    expand_bias_sums = jnp.sum(before_near.astype(F32), axis=0) + jnp.sum(
        before_far.astype(F32), axis=0
    )
    small = jnp.concatenate(
        [
            first_gain_grad,
            first_shift_grad,
            jnp.sum(middle_grad, axis=0),
            second_gain_grad,
            second_shift_grad,
            jnp.sum(cot_local, axis=0),
        ]
    )
    place = block + hid
    owners = jnp.zeros((n_mp * place,), F32)
    for r in range(teams):
        owner = (team + teams - r) % teams
        mine_hid = ordered(
            expand_bias_sums[2 * r * wide : (2 * r + 1) * wide],
            expand_bias_sums[(2 * r + 1) * wide : (2 * r + 2) * wide],
            0,
        )
        piece = jnp.concatenate(
            [qkv_bias_sums[r * block : (r + 1) * block], mine_hid]
        )
        owners = lax.dynamic_update_slice(owners, piece, ((owner * TEAM + mine) * place,))

    vector, q0_in, qa3, out_c, a1 = sync(cat(small, owners), q0_in, qa3, out_c, a1)

    def add_shifts(shifts, here):
        shifts = jnp.stack(shifts)
        return functools.reduce(jnp.add, [shifts[here(i)] for i in range(shifts.shape[0])])

    shifts = [vector, core_swap(vector), chip_swap(vector), across_swap(vector)]
    branch_two_xa = chip_swap(add(two_far_branch[:part], out_c[:part]))
    branch_two_in = add(two_far_branch[part:], out_c[part:])
    qa2 = ring_down(add(qa3, add(kept2, q2_in)))
    branch_two_xa, branch_two_in, qa2, active_near, a1, *shifts = sync(
        branch_two_xa, branch_two_in, qa2, active_near, a1, *shifts
    )
    vector = add_shifts(shifts, lambda i: mine ^ i)
    shifts = [vector] + [ring_up(vector, r) for r in range(1, teams)]
    qa1 = ring_down(add(qa2, add(kept1, q1_in)))
    expand_mine = other_groups(add(a1, add(kept[0], s0_o)))
    expand_other = group_swap(expand_mine)
    two_near_branch, two_near_sent = matmul(active_near, contract_all, False, parts=2)
    qa1, expand_other, two_near_branch, two_near_sent, branch_two_in, out_mine, *shifts = sync(
        qa1, expand_other, two_near_branch, two_near_sent, branch_two_in, out_mine, *shifts
    )
    vector = add_shifts(shifts, lambda i: (team + teams - i) % teams)
    bit = 1
    while bit < n_dp:
        vector = vector + group_swap(vector, bit)
        bit *= 2
    qkv_mine = other_groups(add(qa1, add(kept0, q0_in)))
    qkv_other = group_swap(qkv_mine)
    branch_two_xb = chip_swap(branch_two_in)
    two_near_c = core_swap(two_near_sent)
    out_sum = other_groups(out_mine)
    out_other = group_swap(out_sum)
    mine_spot = lax.dynamic_slice(vector, (6 * width + me * place,), (place,))
    six = [vector[k * width : (k + 1) * width] for k in range(6)]

    branch_two = (
        two_near_branch.astype(F32)
        + two_near_c.astype(F32)
        + cat(branch_two_xa, branch_two_xb).astype(F32)
    )
    layer_out = (middle + branch_two + contract_bias.astype(F32)).astype(BF16)
    qkv_final = ordered(qkv_mine, qkv_other, 0).astype(F32)
    return (
        layer_out,
        input_grad,
        six[0],
        six[1],
        qkv_final[:, :cols],
        mine_spot[:cols],
        qkv_final[:, cols : 2 * cols],
        qkv_final[:, 2 * cols :],
        mine_spot[2 * cols : 3 * cols],
        ordered(out_sum, out_other, 0).astype(F32),
        six[2],
        six[3],
        six[4],
        ordered(expand_mine, expand_other, 1).astype(F32),
        mine_spot[block:],
        ordered(contract_sum, contract_other, 0).astype(F32),
        six[5],
    )


def solution(mesh):
    rows = P(("dp", "mp"), None)
    in_cols, in_rows = P(None, "mp"), P("mp", None)
    placed = (
        rows,
        P("dp", None),
        P(),
        P(),
        in_cols,
        P("mp"),
        in_cols,
        in_cols,
        P("mp"),
        in_rows,
        P(),
        P(),
        P(),
        in_cols,
        P("mp"),
        in_rows,
        P(),
        rows,
    )
    return jax.shard_map(
        body,
        mesh=mesh,
        in_specs=placed,
        out_specs=(
            rows,
            rows,
            P(),
            P(),
            in_cols,
            P("mp"),
            in_cols,
            in_cols,
            P("mp"),
            in_rows,
            P(),
            P(),
            P(),
            in_cols,
            P("mp"),
            in_rows,
            P(),
        ),
        check_vma=False,
    )
```

```python
import functools

import jax
import jax.numpy as jnp
from jax import lax
from jax.experimental import pallas as pl
from jax.experimental.pallas import tpu as pltpu
from jax.sharding import PartitionSpec as P

HD = 64
SEG = 512
NSUM = 50
TAIL = 64
TEAM = 4
PAIR = 2 * HD
QB = 256
EPSILON = 1e-05
MASKED = -1e30
LIGHT = pl.CostEstimate(flops=1024, bytes_accessed=1024, transcendentals=0)
F32 = jnp.float32
BF16 = jnp.bfloat16


def gelu_and_slope(v):
    inner = 0.7978845608 * (v + 0.044715 * v * v * v)
    t = jnp.tanh(inner)
    value = 0.5 * v * (1.0 + t)
    slope = 0.5 * (1.0 + t) + 0.5 * v * (1.0 - t * t) * (
        0.7978845608 * (1.0 + 3.0 * 0.044715 * v * v)
    )
    return value, slope


def normalize(values, scaling, offset):
    centre = jnp.mean(values, axis=-1, keepdims=True)
    centred = values - centre
    spread = jnp.mean(centred * centred, axis=-1, keepdims=True)
    return centred * lax.rsqrt(spread + EPSILON) * scaling + offset


def slot_items(counts, slot_count):
    item_ends = jnp.cumsum(counts)
    places = jnp.arange(slot_count, dtype=jnp.int32)
    return jnp.sum((places[:, None] >= item_ends[None, :]).astype(jnp.int32), axis=1)


def dot(a, b):
    return jnp.dot(a, b, preferred_element_type=F32)


def dot_nt(a, b):
    return lax.dot_general(a, b, (((1,), (1,)), ((), ())), preferred_element_type=F32)


def dot_tn(a, b):
    return lax.dot_general(a, b, (((0,), (0,)), ((), ())), preferred_element_type=F32)


def head_only(block, h):
    lane = lax.broadcasted_iota(jnp.int32, block.shape, 1)
    return jnp.where((lane // HD) == h, block, jnp.zeros_like(block))


def causal(block):
    key = lax.broadcasted_iota(jnp.int32, block.shape, 0)
    query = lax.broadcasted_iota(jnp.int32, block.shape, 1)
    return jnp.where(query >= key, block, MASKED)


def hide_rows(block, count):
    key = lax.broadcasted_iota(jnp.int32, block.shape, 0)
    return jnp.where(key >= count, block, MASKED)


def key_blocks(info_ref, e):
    slots = info_ref.shape[0] - 2
    team, mine = info_ref[slots], info_ref[slots + 1]
    i = mine ^ e
    item = info_ref[team * TEAM + i]

    def hidden(other):
        same = info_ref[jnp.maximum(other, 0)] == item
        return jnp.where(jnp.logical_and(other >= 0, same), TAIL - NSUM, TAIL)

    rows = TEAM * SEG
    out = [(rows + 2 * f * TAIL, hidden((team - 1) * TEAM + (mine ^ f))) for f in range(TEAM)]
    for d in range(1, TEAM):
        j = i ^ d
        inside = j < i
        start = jnp.where(
            inside, (e ^ d) * SEG + SEG - TAIL, rows + (2 * (e ^ d) + 1) * TAIL
        )
        out.append((start, hidden(jnp.where(inside, team, team - 2) * TEAM + j)))
    return out


def attend_kernel(first, count, info_ref, qkv_ref, mix_ref, log_ref):
    def segment(e, carry):
        base = pl.multiple_of(e * SEG, SEG)
        place = pl.multiple_of((e - first) * SEG, SEG)
        extra = key_blocks(info_ref, e)
        keys = qkv_ref[pl.ds(base, SEG), PAIR : 2 * PAIR]
        value_t = qkv_ref[pl.ds(base, SEG), 2 * PAIR : 3 * PAIR].T
        extra_keys = [
            qkv_ref[pl.ds(pl.multiple_of(s, TAIL), TAIL), PAIR : 2 * PAIR] for s, _ in extra
        ]
        extra_values = [
            qkv_ref[pl.ds(pl.multiple_of(s, TAIL), TAIL), 2 * PAIR : 3 * PAIR] for s, _ in extra
        ]
        extra_keys = jnp.concatenate(extra_keys, axis=0)
        extra_value_t = jnp.concatenate(extra_values, axis=0).T
        for qb in range(SEG // QB):
            query = qkv_ref[pl.ds(base + qb * QB, QB), 0:PAIR]
            seen = (qb + 1) * QB
            outs = []
            for h in range(2):
                qh = head_only(query, h)
                own = dot_nt(keys[:seen], qh)
                parts = [own[: qb * QB]] if qb else []
                parts.append(causal(own[qb * QB :]))
                far = dot_nt(extra_keys, qh)
                for n, (_, hidden) in enumerate(extra):
                    parts.append(hide_rows(far[n * TAIL : (n + 1) * TAIL], hidden))
                high = functools.reduce(
                    jnp.maximum, [jnp.max(p, axis=0, keepdims=True) for p in parts]
                )
                parts = [jnp.exp(p - high) for p in parts]
                total = functools.reduce(
                    jnp.add, [jnp.sum(p, axis=0, keepdims=True) for p in parts]
                )
                cut = 2 if qb else 1
                p_own = jnp.concatenate([p.astype(BF16) for p in parts[:cut]], axis=0)
                p_far = jnp.concatenate([p.astype(BF16) for p in parts[cut:]], axis=0)
                rows = slice(h * HD, (h + 1) * HD)
                mixed = dot(value_t[rows, :seen], p_own) + dot(extra_value_t[rows], p_far)
                outs.append(mixed / total)
                log_ref[0, e - first, h : h + 1, qb * QB : (qb + 1) * QB] = high + jnp.log(total)
            mix_ref[pl.ds(place + qb * QB, QB), :] = jnp.concatenate(outs, axis=0).T.astype(BF16)
        return carry

    lax.fori_loop(first, first + count, segment, 0)


def attend(info, qkv, first, count):
    pieces = qkv.shape[1] // (3 * PAIR)
    rows = count * SEG
    return pl.pallas_call(
        functools.partial(attend_kernel, first, count),
        grid_spec=pltpu.PrefetchScalarGridSpec(
            num_scalar_prefetch=1,
            grid=(pieces,),
            in_specs=[pl.BlockSpec((qkv.shape[0], 3 * PAIR), lambda r, t: (0, r))],
            out_specs=[
                pl.BlockSpec((rows, PAIR), lambda r, t: (0, r)),
                pl.BlockSpec((1, count, 2, SEG), lambda r, t: (r, 0, 0, 0)),
            ],
        ),
        out_shape=[
            jax.ShapeDtypeStruct((rows, pieces * PAIR), BF16),
            jax.ShapeDtypeStruct((pieces, count, 2, SEG), F32),
        ],
        compiler_params=pltpu.CompilerParams(vmem_limit_bytes=56 * 1024 * 1024),
        cost_estimate=LIGHT,
        name="attend",
    )(info, qkv)


def attend_back_kernel(first, count, info_ref, qkv_ref, mix_ref, grad_ref, log_ref, *rest):
    key_acc, value_acc = rest[-2:]
    if len(rest) == 6:
        before_ref, out_ref = rest[:2]
        key_acc[...] = before_ref[:, PAIR : 2 * PAIR].astype(F32)
        value_acc[...] = before_ref[:, 2 * PAIR : 3 * PAIR].astype(F32)
        out_ref[:, 0:PAIR] = before_ref[:, 0:PAIR]
    else:
        out_ref = rest[0]
        key_acc[...] = jnp.zeros_like(key_acc)
        value_acc[...] = jnp.zeros_like(value_acc)
        out_ref[:, 0:PAIR] = jnp.zeros((out_ref.shape[0], PAIR), BF16)

    def segment(e, carry):
        base = pl.multiple_of(e * SEG, SEG)
        place = pl.multiple_of((e - first) * SEG, SEG)
        extra = key_blocks(info_ref, e)
        keys = qkv_ref[pl.ds(base, SEG), PAIR : 2 * PAIR]
        values = qkv_ref[pl.ds(base, SEG), 2 * PAIR : 3 * PAIR]
        key_t = keys.T
        extra_keys = jnp.concatenate(
            [qkv_ref[pl.ds(pl.multiple_of(s, TAIL), TAIL), PAIR : 2 * PAIR] for s, _ in extra],
            axis=0,
        )
        extra_values = jnp.concatenate(
            [qkv_ref[pl.ds(pl.multiple_of(s, TAIL), TAIL), 2 * PAIR : 3 * PAIR] for s, _ in extra],
            axis=0,
        )
        extra_key_t = extra_keys.T
        for qb in range(SEG // QB):
            here = pl.ds(base + qb * QB, QB)
            query = qkv_ref[here, 0:PAIR]
            grad = grad_ref[pl.ds(place + qb * QB, QB), :]
            both = (grad.astype(F32) * mix_ref[pl.ds(place + qb * QB, QB), :].astype(F32)).T
            seen = (qb + 1) * QB
            key_own, value_own, key_far, value_far = 0.0, 0.0, 0.0, 0.0
            query_grads = []
            for h in range(2):
                rows = slice(h * HD, (h + 1) * HD)
                qh, gh = head_only(query, h), head_only(grad, h)
                centre = jnp.sum(both[rows], axis=0, keepdims=True)
                log = log_ref[0, e - first, h : h + 1, qb * QB : (qb + 1) * QB]
                own = dot_nt(keys[:seen], qh)
                parts = [own[: qb * QB]] if qb else []
                parts.append(causal(own[qb * QB :]))
                own = jnp.exp((jnp.concatenate(parts, axis=0) if qb else parts[0]) - log)
                far = dot_nt(extra_keys, qh)
                far = jnp.concatenate(
                    [
                        hide_rows(far[n * TAIL : (n + 1) * TAIL], hidden)
                        for n, (_, hidden) in enumerate(extra)
                    ],
                    axis=0,
                )
                far = jnp.exp(far - log)
                own_step = (own * (dot_nt(values[:seen], gh) - centre)).astype(BF16)
                far_step = (far * (dot_nt(extra_values, gh) - centre)).astype(BF16)
                value_own += dot(own.astype(BF16), gh)
                value_far += dot(far.astype(BF16), gh)
                key_own += dot(own_step, qh)
                key_far += dot(far_step, qh)
                query_grads.append(dot(key_t[rows, :seen], own_step) + dot(extra_key_t[rows], far_step))
            query_grad = jnp.concatenate(query_grads, axis=0).T * (HD**-0.5)
            out_ref[here, 0:PAIR] = query_grad.astype(BF16)
            key_acc[pl.ds(base, seen), :] += key_own
            value_acc[pl.ds(base, seen), :] += value_own
            for n, (s, _) in enumerate(extra):
                there = pl.ds(pl.multiple_of(s, TAIL), TAIL)
                key_acc[there, :] += key_far[n * TAIL : (n + 1) * TAIL]
                value_acc[there, :] += value_far[n * TAIL : (n + 1) * TAIL]
        return carry

    lax.fori_loop(first, first + count, segment, 0)
    out_ref[:, PAIR : 2 * PAIR] = key_acc[...].astype(BF16)
    out_ref[:, 2 * PAIR : 3 * PAIR] = value_acc[...].astype(BF16)
    if len(rest) == 6:
        for f in range(TEAM):
            for k, far_ref in enumerate(rest[2:4]):
                at = TEAM * SEG + (2 * f + k) * TAIL
                here = slice(f * TAIL, (f + 1) * TAIL)
                far_ref[here, :PAIR] = key_acc[at : at + TAIL, :].astype(BF16)
                far_ref[here, PAIR:] = value_acc[at : at + TAIL, :].astype(BF16)


def attend_back(info, qkv, mixture, grad, logs, first, count, before=None):
    pieces = qkv.shape[1] // (3 * PAIR)
    rows = count * SEG
    wide = pl.BlockSpec((qkv.shape[0], 3 * PAIR), lambda r, t: (0, r))
    narrow = pl.BlockSpec((rows, PAIR), lambda r, t: (0, r))
    more = () if before is None else (before,)
    return pl.pallas_call(
        functools.partial(attend_back_kernel, first, count),
        grid_spec=pltpu.PrefetchScalarGridSpec(
            num_scalar_prefetch=1,
            grid=(pieces,),
            in_specs=[
                wide,
                narrow,
                narrow,
                pl.BlockSpec((1, count, 2, SEG), lambda r, t: (r, 0, 0, 0)),
            ]
            + [wide] * len(more),
            out_specs=[wide] + [pl.BlockSpec((TEAM * TAIL, 2 * PAIR), lambda r, t: (0, r))] * (2 * len(more)),
            scratch_shapes=[
                pltpu.VMEM((qkv.shape[0], PAIR), F32),
                pltpu.VMEM((qkv.shape[0], PAIR), F32),
            ],
        ),
        out_shape=[jax.ShapeDtypeStruct(qkv.shape, BF16)]
        + [jax.ShapeDtypeStruct((TEAM * TAIL, pieces * 2 * PAIR), BF16)] * (2 * len(more)),
        compiler_params=pltpu.CompilerParams(vmem_limit_bytes=56 * 1024 * 1024),
        cost_estimate=LIGHT,
        name="attend_back",
    )(info, qkv, mixture, grad, logs, *more)


def weight_grad_kernel(splits, halves, pairs, source_ref, target_ref, *refs):
    outs = refs[2 * pairs :]
    total = None
    for left, right in zip(refs[: 2 * pairs : 2], refs[1 : 2 * pairs : 2]):
        term = dot_tn(left[...], right[...])
        total = term if total is None else total + term
    total = total.astype(BF16)
    width = total.shape[1] // splits
    columns = [total[:, k * width : (k + 1) * width] for k in range(splits)]
    if not halves:
        for k in range(splits):
            outs[k][...] = columns[k]
        return
    step, steps = pl.program_id(0), pl.num_programs(0)

    @pl.when(step < steps // 2)
    def _():
        for k in range(splits):
            outs[2 * k][...] = columns[k]

    @pl.when(step >= steps // 2)
    def _():
        for k in range(splits):
            outs[2 * k + 1][...] = columns[k]


def weight_grad(pairs, column=0, columns=None, step=256, splits=1, source=None, target=None, halves=False):
    height = pairs[0][0].shape[1]
    columns = columns or pairs[0][1].shape[1]
    steps, width = height // step, columns // splits
    plain = jnp.arange(steps, dtype=jnp.int32)
    specs = []
    for left, right, n in pairs:
        specs.append(pl.BlockSpec((left.shape[0], step), lambda i, s, t: (0, s[i])))
        specs.append(pl.BlockSpec((left.shape[0], columns), lambda i, s, t, n=n: (n, column)))
    if halves:
        outs = [
            pl.BlockSpec((step, width), lambda i, s, t: (jnp.minimum(i, steps // 2 - 1), 0)),
            pl.BlockSpec((step, width), lambda i, s, t: (jnp.maximum(i - steps // 2, 0), 0)),
        ] * splits
        shapes = [jax.ShapeDtypeStruct((height // 2, width), BF16)] * (2 * splits)
    else:
        outs = [pl.BlockSpec((step, width), lambda i, s, t: (t[i], 0))] * splits
        shapes = [jax.ShapeDtypeStruct((height, width), BF16)] * splits
    return pl.pallas_call(
        functools.partial(weight_grad_kernel, splits, halves, len(pairs)),
        grid_spec=pltpu.PrefetchScalarGridSpec(
            num_scalar_prefetch=2, grid=(steps,), in_specs=specs, out_specs=outs
        ),
        out_shape=shapes,
        compiler_params=pltpu.CompilerParams(vmem_limit_bytes=56 * 1024 * 1024),
        cost_estimate=LIGHT,
        name="weight_grad",
    )(
        plain if source is None else source,
        plain if target is None else target,
        *[v for pair in pairs for v in pair[:2]],
    )


def pack_kernel(plan, which_ref, *refs):
    sources, out_ref, sems = refs[:-2], refs[-2], refs[-1]
    copies = []
    for n, (ref, (row, rows, column, columns, at_row, at_column)) in enumerate(zip(sources, plan)):
        if at_row == "held":
            at_row = pl.multiple_of(which_ref[0] * rows, rows)
        elif at_row == "other":
            at_row = pl.multiple_of((1 - which_ref[0]) * rows, rows)
        copies.append(
            pltpu.make_async_copy(
                ref.at[pl.ds(row, rows), pl.ds(column, columns)],
                out_ref.at[pl.ds(at_row, rows), pl.ds(at_column, columns)],
                sems.at[n],
            )
        )
    for copy in copies:
        copy.start()
    for copy in copies:
        copy.wait()


def pack(which, shape, parts):
    return pl.pallas_call(
        functools.partial(pack_kernel, [plan for _, plan in parts]),
        grid_spec=pltpu.PrefetchScalarGridSpec(
            num_scalar_prefetch=1,
            grid=(),
            in_specs=[pl.BlockSpec(memory_space=pl.ANY)] * len(parts),
            out_specs=pl.BlockSpec(memory_space=pltpu.VMEM),
            scratch_shapes=[pltpu.SemaphoreType.DMA((len(parts),))],
        ),
        out_shape=jax.ShapeDtypeStruct(shape, BF16),
        compiler_params=pltpu.CompilerParams(vmem_limit_bytes=32 * 1024 * 1024),
        cost_estimate=LIGHT,
        name="pack",
    )(which, *[v for v, _ in parts])


def pack_rows(which, parts):
    columns, row, plan = parts[0].shape[1], 0, []
    for v in parts:
        plan.append((v, (0, v.shape[0], 0, columns, row, 0)))
        row += v.shape[0]
    return pack(which, (row, columns), plan)


def pack_columns(which, parts, rows):
    column, plan = 0, []
    for v in parts:
        plan.append((v, (0, rows, 0, v.shape[1], 0, column)))
        column += v.shape[1]
    return pack(which, (rows, column), plan)


def project_kernel(pieces, which_ref, *refs):
    weights, rows, out_ref, first, last = (
        refs[: 2 * pieces],
        refs[2 * pieces : -3],
        refs[-3],
        refs[-2],
        refs[-1],
    )
    depth, block = first.shape[0], first.shape[1] // pieces
    for n in range(pieces):
        first[:, n * block : (n + 1) * block] = weights[2 * n][:depth, :block]
        last[:, n * block : (n + 1) * block] = weights[2 * n + 1][:depth, :block]
    bias = jnp.concatenate(
        [weights[2 * n][depth : depth + 1, :block].astype(F32) for n in range(pieces)], axis=1
    )
    lane = lax.broadcasted_iota(jnp.int32, bias.shape, 1)
    scale = jnp.where(lane % block < PAIR, HD**-0.5, 1.0)
    held = pl.ds(pl.multiple_of(which_ref[0] * depth, depth), depth)
    other = pl.ds(pl.multiple_of((1 - which_ref[0]) * depth, depth), depth)
    at = 0
    for ref in rows:
        chunk = min(256, ref.shape[0])
        for start in range(0, ref.shape[0], chunk):
            here = slice(start, start + chunk)
            value = dot(ref[here, held], first[...]) + dot(ref[here, other], last[...])
            out_ref[at + start : at + start + chunk, :] = ((value + bias) * scale).astype(BF16)
        at += ref.shape[0]


def project(which, weights, rows):
    pieces = len(weights)
    depth, block = rows[0].shape[1] // 2, 3 * PAIR
    height = sum(v.shape[0] for v in rows)
    return pl.pallas_call(
        functools.partial(project_kernel, pieces),
        grid_spec=pltpu.PrefetchScalarGridSpec(
            num_scalar_prefetch=1,
            grid=(),
            in_specs=[pl.BlockSpec(memory_space=pltpu.VMEM)] * (2 * pieces + len(rows)),
            out_specs=pl.BlockSpec(memory_space=pltpu.VMEM),
            scratch_shapes=[pltpu.VMEM((depth, pieces * block), BF16)] * 2,
        ),
        out_shape=jax.ShapeDtypeStruct((height, pieces * block), BF16),
        compiler_params=pltpu.CompilerParams(vmem_limit_bytes=56 * 1024 * 1024),
        cost_estimate=LIGHT,
        name="project",
    )(which, *[v for pair in weights for v in pair], *rows)


def matmul_kernel(transposed, parts, left_ref, right_ref, *rest):
    outs = rest[-parts:]
    rows = left_ref.shape[0] // parts
    chunk = min(256, rows)
    for start in range(0, left_ref.shape[0], chunk):
        here = slice(start, start + chunk)
        value = (dot_nt if transposed else dot)(left_ref[here, :], right_ref[...])
        if len(rest) > parts:
            value = value * rest[0][here, :].astype(F32)
        at = start % rows
        outs[start // rows][at : at + chunk, :] = value.astype(BF16)


def matmul(left, right, transposed, scale=None, place=0, rows=None, step=512, parts=1):
    rows = rows or left.shape[0]
    depth = left.shape[1]
    columns = right.shape[0] if transposed else right.shape[1]
    right_spec = (
        pl.BlockSpec((step, depth), lambda i: (i, 0))
        if transposed
        else pl.BlockSpec((depth, step), lambda i: (0, i))
    )
    more = () if scale is None else (scale,)
    out = pl.pallas_call(
        functools.partial(matmul_kernel, transposed, parts),
        grid=(columns // step,),
        in_specs=[pl.BlockSpec((rows, depth), lambda i: (place, 0)), right_spec]
        + [pl.BlockSpec((rows, step), lambda i: (0, i))] * len(more),
        out_specs=[pl.BlockSpec((rows // parts, step), lambda i: (0, i))] * parts,
        out_shape=[jax.ShapeDtypeStruct((rows // parts, columns), BF16)] * parts,
        compiler_params=pltpu.CompilerParams(vmem_limit_bytes=56 * 1024 * 1024),
        cost_estimate=LIGHT,
        name="matmul",
    )(left, right, *more)
    return out if parts > 1 else out[0]


def body(
    inputs,
    item_counts,
    first_gain,
    first_shift,
    query_weight,
    query_bias,
    key_weight,
    value_weight,
    value_bias,
    output_weight,
    output_bias,
    second_gain,
    second_shift,
    expand_weight,
    expand_bias,
    contract_weight,
    contract_bias,
    cotangent,
):
    n_mp, n_dp = lax.axis_size("mp"), lax.axis_size("dp")
    teams = n_mp // TEAM
    me = lax.axis_index("mp")
    team, mine = me // TEAM, me % TEAM
    second = lax.axis_index("dp") % 2

    def core_swap(v):
        return lax.ppermute(v, "mp", [(i, i ^ 1) for i in range(n_mp)])

    def chip_swap(v):
        return lax.ppermute(v, "mp", [(i, i ^ 2) for i in range(n_mp)])

    def ring_up(v, by=1):
        return lax.ppermute(v, "mp", [(i, (i + by * TEAM) % n_mp) for i in range(n_mp)])

    def ring_down(v):
        return lax.ppermute(v, "mp", [(i, (i - TEAM) % n_mp) for i in range(n_mp)])

    def line_up(v, by=1):
        return lax.ppermute(v, "mp", [(i, i + by * TEAM) for i in range(n_mp - by * TEAM)])

    def line_down(v, by=1):
        return lax.ppermute(v, "mp", [(i + by * TEAM, i) for i in range(n_mp - by * TEAM)])

    def group_swap(v, bit=1):
        return lax.ppermute(v, "dp", [(i, i ^ bit) for i in range(n_dp)])

    def half(v, axis, which):
        size = v.shape[axis] // 2
        return lax.dynamic_slice_in_dim(v, which * size, size, axis)

    def ordered(held, other, axis):
        return jnp.where(
            second == 0,
            jnp.concatenate([held, other], axis=axis),
            jnp.concatenate([other, held], axis=axis),
        )

    def add(*terms):
        return functools.reduce(jnp.add, [t.astype(F32) for t in terms]).astype(BF16)

    def other_groups(v):
        bit = 2
        while bit < n_dp:
            v = add(v, group_swap(v, bit))
            bit *= 2
        return v

    def sync(*values):
        return lax.optimization_barrier(values)

    slot_count = teams * TEAM
    items = slot_items(item_counts[0], slot_count)
    info = jnp.pad(items, (0, 2))
    at = lax.iota(jnp.int32, slot_count + 2)
    info = jnp.where(at == slot_count, team, jnp.where(at == slot_count + 1, mine, info))

    gain_first, shift_first = first_gain.astype(F32), first_shift.astype(F32)
    gain_second, shift_second = second_gain.astype(F32), second_shift.astype(F32)
    width = inputs.shape[1]
    cols = query_bias.shape[0]
    hid = expand_bias.shape[0]
    wide = hid // 2
    team_rows, near_rows = TEAM * SEG, 2 * SEG
    span = TEAM * TAIL
    block = 3 * PAIR
    pad = 16

    def across_swap(v):
        return lax.ppermute(v, "mp", [(i, i ^ 3) for i in range(n_mp)])

    def with_bias(weight, bias):
        return jnp.concatenate(
            [weight, jnp.broadcast_to(bias[None], (pad, bias.shape[0]))], axis=0
        )

    def send_in(terms):
        size = terms.shape[0] // 2
        return add(terms[:size], core_swap(terms[size:]))

    along = [[t * TEAM + i for t in range(teams)] for i in range(TEAM)]
    part = SEG // 2
    pairs_along = [
        [(first + d) * n_mp + t * TEAM + i for t in range(teams) for d in range(2)]
        for first in range(0, n_dp, 2)
        for i in range(TEAM)
    ]

    def scatter_sum(v):
        return lax.psum_scatter(
            v, ("dp", "mp"), scatter_dimension=0, axis_index_groups=pairs_along, tiled=True
        )

    def cat(*parts, axis=0):
        return jnp.concatenate(parts, axis=axis)

    which = jnp.reshape(second, (1,)).astype(jnp.int32)

    qkv_local = cat(query_weight, key_weight, value_weight, output_weight.T, axis=1)
    qkv_bias_local = cat(
        query_bias, jnp.zeros_like(query_bias), value_bias, jnp.zeros_like(query_bias)
    )
    packed = with_bias(half(qkv_local, 0, second), qkv_bias_local)
    q0_o = half(qkv_local, 0, 1 - second)
    hidden_in = inputs.astype(F32)
    normed = normalize(hidden_in, gain_first, shift_first).astype(BF16)
    packed, normed, normed_tail = sync(packed, normed, normed[SEG - TAIL :])
    q1 = ring_up(packed)
    normed_xa = chip_swap(normed[:part])
    normed_c = core_swap(normed)
    early = line_up(normed_tail)
    normed_b = normed[part:]
    q1, normed_xa, normed_c, early, normed_b = sync(q1, normed_xa, normed_c, early, normed_b)
    q2 = ring_up(q1)
    normed_xb = chip_swap(normed_b)
    q1_o = group_swap(q1)
    earlier = line_up(early)
    q2, q1_o, normed_x, rest = sync(q2, q1_o, cat(normed_xa, normed_xb), cat(early, earlier))
    q3 = ring_up(q2)
    q2_o = group_swap(q2)
    normed_xc = core_swap(normed_x)
    rest_x = chip_swap(rest)
    rest_xc = across_swap(rest)
    rest_c = core_swap(rest)
    tops = width // 2
    expand_own, expand_rest = half(expand_weight, 1, second), half(expand_weight, 1, 1 - second)
    expand_bias_own = half(expand_bias, 0, second)
    expand_bias_rest = half(expand_bias, 0, 1 - second)
    q3, q2_o, normed_xc, rest_x, rest_xc, rest_c, cot_a, cot_b, e0 = sync(
        q3,
        q2_o,
        normed_xc,
        rest_x,
        rest_xc,
        rest_c,
        cotangent[:part],
        cotangent[part:],
        with_bias(expand_own, expand_bias_own),
    )
    q3_o = group_swap(q3)
    e1 = ring_up(e0)
    cot_xa = chip_swap(cot_a)
    row_blocks = [normed, normed_c, normed_x, normed_xc, rest, rest_c, rest_x, rest_xc]
    qkv_a = project(which, [(packed, q0_o), (q1, q1_o), (q2, q2_o)], row_blocks)
    q3_o, cot_xa, qkv_a, e1, cot_b, cot = sync(q3_o, cot_xa, qkv_a, e1, cot_b, cotangent)
    e2 = ring_up(e1)
    e1_o = group_swap(e1)
    cot_xb = chip_swap(cot_b)
    cot_c = core_swap(cot)
    mix_far_a, log_far_a = attend(info, qkv_a, 2, 2)
    qkv_b = project(which, [(q3, q3_o)], row_blocks)
    mix_far_b, log_far_b = attend(info, qkv_b, 2, 2)
    held_pieces = ((packed, q0_o), (q1, q1_o), (q2, q2_o), (q3, q3_o))

    def whole(pieces, column, columns):
        plan = []
        for n, (v, o) in enumerate(pieces):
            plan.append((v, (0, tops, column, columns, "held", n * columns)))
            plan.append((o, (0, tops, column, columns, "other", n * columns)))
        return pack(which, (width, len(pieces) * columns), plan)

    out_all = whole(held_pieces, block, cols)
    mix_far = pack_columns(which, [mix_far_a, mix_far_b], near_rows)
    far, far_sent = matmul(mix_far, out_all, True, parts=2)
    cot_x = pack_rows(which, [cot_xa, cot_xb])
    e2, e1_o, cot_x, cot_c, qkv_a, qkv_b, far, far_sent, out_all, contract_weight = sync(
        e2, e1_o, cot_x, cot_c, qkv_a, qkv_b, far, far_sent, out_all, contract_weight
    )
    far_c = core_swap(far_sent)
    contract_own = half(contract_weight, 0, second)
    contract_rest = half(contract_weight, 0, 1 - second)
    far, far_c, qkv_a = sync(far, far_c, qkv_a)
    branch_in = add(far[part:], far_c[part:])
    branch_xa = chip_swap(add(far[:part], far_c[:part]))
    e3 = ring_up(e2)
    e2_o = group_swap(e2)
    mix_near_a, log_near_a = attend(info, qkv_a, 0, 2)
    branch_xa, e3, e2_o, mix_near_a, branch_in, contract_own, qkv_b = sync(
        branch_xa, e3, e2_o, mix_near_a, branch_in, contract_own, qkv_b
    )
    branch_xb = chip_swap(branch_in)
    cot_xc = core_swap(cot_x)
    k1 = ring_up(contract_own)
    e3_o = group_swap(e3)
    mix_near_b, log_near_b = attend(info, qkv_b, 0, 2)
    mix_near = pack_columns(which, [mix_near_a, mix_near_b], near_rows)
    near, near_sent = matmul(mix_near, out_all, True, parts=2)
    branch_xb, k1, e3_o, near, near_sent, mix_near, cot_xc = sync(
        branch_xb, k1, e3_o, near, near_sent, mix_near, cot_xc
    )
    near_c = core_swap(near_sent)
    near, near_c, k1 = sync(near, near_c, k1)
    branch_x = cat(branch_xa, branch_xb)
    branch = near.astype(F32) + near_c.astype(F32) + branch_x.astype(F32)
    middle = hidden_in + branch + output_bias.astype(F32)
    normed_two = normalize(middle, gain_second, shift_second).astype(BF16)
    normed_two, k1, e3_o, *held = sync(normed_two, k1, e3_o, *[v for p in held_pieces for v in p])
    two_xa = chip_swap(normed_two[:part])
    two_c = core_swap(normed_two)
    k2 = ring_up(k1)
    k1_o = group_swap(k1)
    expand_pairs = (e1, e1_o, e2, e2_o, e3, e3_o)
    expand_all = pack_columns(which, [expand_own, expand_rest, *expand_pairs], width)
    held = tuple(zip(held[0::2], held[1::2]))
    qkv_all = whole(held, 0, block)
    key_value_all = whole(held, PAIR, 2 * PAIR)
    expand_bias_all = cat(
        expand_bias_own, expand_bias_rest, *[v[width] for v in expand_pairs]
    ).astype(F32)
    two_xa, two_c, k2, k1_o, expand_all, expand_bias_all, normed_two, qkv_all, key_value_all = sync(
        two_xa, two_c, k2, k1_o, expand_all, expand_bias_all, normed_two, qkv_all, key_value_all
    )
    two_xb = chip_swap(normed_two[part:])
    k3 = ring_up(k2)
    k2_o = group_swap(k2)

    def front(rows):
        value, slope = gelu_and_slope(dot(rows, expand_all) + expand_bias_all)
        return value.astype(BF16), slope.astype(BF16)

    two_xac = core_swap(two_xa)
    two_near = pack_rows(which, [normed_two, two_c])
    active_near, slope_near = front(two_near)
    two_xb, k3, k2_o, active_near, slope_near, two_near, two_xac = sync(
        two_xb, k3, k2_o, active_near, slope_near, two_near, two_xac
    )
    two_xbc = core_swap(two_xb)
    two_xbc, k3, qkv_a, qkv_b, cot_c = sync(two_xbc, k3, qkv_a, qkv_b, cot_c)
    k3_o = group_swap(k3)
    two_far = pack_rows(which, [two_xa, two_xb, two_xac, two_xbc])
    active_far, slope_far = front(two_far)
    qkv = pack_columns(which, [qkv_a, qkv_b], qkv_a.shape[0])
    cot_far = pack_rows(which, [cot_x, cot_xc])
    k3_o, active_far, slope_far, two_far, cot_far, qkv = sync(
        k3_o, active_far, slope_far, two_far, cot_far, qkv
    )
    contract_all = pack_rows(which, [contract_own, contract_rest, k1, k1_o, k2, k2_o, k3, k3_o])
    before_far = matmul(cot_far, contract_all, True, slope_far)
    far, far_sent = matmul(before_far, expand_all, True, parts=2)
    far, far_sent, before_far, contract_all = sync(far, far_sent, before_far, contract_all)
    far_c = core_swap(far_sent)
    cot_near = pack_rows(which, [cot, cot_c])
    far, far_c, cot_near, slope_near = sync(far, far_c, cot_near, slope_near)
    two_grad_in = add(far[part:], far_c[part:])
    two_grad_xa = chip_swap(add(far[:part], far_c[:part]))
    before_near = matmul(cot_near, contract_all, True, slope_near)
    near, near_sent = matmul(before_near, expand_all, True, parts=2)
    two_grad_xa, two_grad_in, before_near, near, near_sent, active_near = sync(
        two_grad_xa, two_grad_in, before_near, near, near_sent, active_near
    )
    two_grad_xb = chip_swap(two_grad_in)
    near_c = core_swap(near_sent)
    hidden_order = []
    for r in range(teams):
        owner = (team + teams - r) % teams
        hidden_order += [owner * 2 + second, owner * 2 + 1 - second]
    hidden_order = jnp.stack(hidden_order).astype(jnp.int32)
    (contract_grad,) = weight_grad(
        [(active_near, cot_near, 0), (active_far, cot_far, 0)], step=wide, target=hidden_order
    )
    two_grad_xb, contract_grad, near, near_c = sync(two_grad_xb, contract_grad, near, near_c)
    contract_mine = scatter_sum(contract_grad)
    normed_two_grad = (
        near.astype(F32)
        + near_c.astype(F32)
        + cat(two_grad_xa, two_grad_xb).astype(F32)
    )
    cot_local = cotangent.astype(F32)
    _, pull_second = jax.vjp(normalize, middle, gain_second, shift_second)
    middle_part, second_gain_grad, second_shift_grad = pull_second(normed_two_grad)
    middle_grad = cot_local + middle_part
    middle_low, before_near, active_far = sync(middle_grad.astype(BF16), before_near, active_far)
    middle_xa = chip_swap(middle_low[:part])
    middle_c = core_swap(middle_low)
    expand_parts = weight_grad(
        [(two_near, before_near, 0), (two_far, before_far, 0)], splits=2 * teams
    )
    kept, sent = expand_parts[0::2], expand_parts[1::2]
    middle_low_b = middle_low[part:]
    middle_xa, middle_c, middle_low, middle_low_b, *sent = sync(
        middle_xa, middle_c, middle_low, middle_low_b, *sent
    )
    middle_xb = chip_swap(middle_low_b)
    middle_xac = core_swap(middle_xa)
    s3_o = group_swap(sent[3])
    middle_near = pack_rows(which, [middle_low, middle_c])
    mix_grad_near = matmul(middle_near, out_all, False)
    log_near = cat(log_near_a, log_near_b)
    (part_grad,) = attend_back(info, qkv, mix_near, mix_grad_near, log_near, 0, 2)
    middle_xb, s3_o, part_grad, middle_near, active_far, middle_xac, *sent = sync(
        middle_xb, s3_o, part_grad, middle_near, active_far, middle_xac, *sent
    )
    middle_xbc = core_swap(middle_xb)
    s3 = add(kept[3], s3_o)
    middle_xbc, s3, *sent = sync(middle_xbc, s3, *sent)
    s2_o = group_swap(sent[2])
    s1_o = group_swap(sent[1])
    a3 = ring_down(s3)
    middle_far = pack_rows(which, [middle_xa, middle_xb, middle_xac, middle_xbc])
    mix_grad_far = matmul(middle_far, out_all, False)
    log_far = cat(log_far_a, log_far_b)
    qkv_grad, one, two = attend_back(
        info, qkv, mix_far, mix_grad_far, log_far, 2, 2, part_grad
    )
    far, far_sent = matmul(qkv_grad, qkv_all, True, place=1, rows=near_rows, parts=2)
    place_order = jnp.stack([(team + teams - r) % teams for r in range(teams)]).astype(jnp.int32)
    (out_grad,) = weight_grad(
        [(sync(mix_near, far)[0], middle_near, 0), (mix_far, middle_far, 0)], step=cols, target=place_order
    )
    s2_o, s1_o, a3, far, far_sent, qkv_grad, contract_mine, one, two, sent0, out_grad = sync(
        s2_o, s1_o, a3, far, far_sent, qkv_grad, contract_mine, one, two, sent[0], out_grad
    )
    far_c = core_swap(far_sent)
    far, far_c, qkv_grad, out_grad = sync(far, far_c, qkv_grad, out_grad)
    out_mine = scatter_sum(out_grad)
    normed_in = add(far[part:], far_c[part:])
    normed_ga = chip_swap(add(far[:part], far_c[:part]))
    one = line_down(one)
    two = line_down(two, 2)
    s0_o = group_swap(sent0)
    contract_sum = other_groups(contract_mine)
    contract_other = group_swap(contract_sum)
    row_halves = jnp.arange(8, dtype=jnp.int32)
    row_halves = jnp.where(second == 0, row_halves, (row_halves + 4) % 8)
    grad_pairs = [
        (v, qkv_grad, n)
        for n, v in enumerate([normed, normed_c, normed_x, normed_xc, pack_rows(which, [rest, rest_c, rest_x, rest_xc])])
    ]
    kept2, sent2, kept3, sent3 = weight_grad(
        grad_pairs, 1, 2 * block, splits=2, source=row_halves, halves=True, step=width // 8
    )
    near, near_sent = matmul(qkv_grad, qkv_all, True, place=0, rows=near_rows, parts=2)
    a3_s2 = add(a3, add(kept[2], s2_o))
    (
        normed_ga,
        normed_in,
        one,
        two,
        s0_o,
        sent2,
        sent3,
        near,
        near_sent,
        qkv_grad,
        a3_s2,
        active_far,
        contract_other,
    ) = sync(
        normed_ga,
        normed_in,
        one,
        two,
        s0_o,
        sent2,
        sent3,
        near,
        near_sent,
        qkv_grad,
        a3_s2,
        active_far,
        contract_other,
    )
    normed_gb = chip_swap(normed_in)
    q3_in = group_swap(sent3)
    q2_in = group_swap(sent2)
    a2 = ring_down(a3_s2)
    near_c = core_swap(near_sent)

    def turn(v, by):
        rows, columns = v.shape
        shift = (by % teams) * 2 * PAIR
        if not shift:
            return v
        return pack(
            which,
            v.shape,
            [
                (v, (0, rows, shift, columns - shift, 0, 0)),
                (v, (0, rows, 0, shift, 0, columns - shift)),
            ],
        )

    late = add(turn(one, 1), turn(two, 2))
    late_terms = matmul(late, key_value_all, True)
    grad_pairs = [(v, qkv_grad, n) for v, _, n in grad_pairs]
    kept0, sent0, kept1, sent1 = weight_grad(
        grad_pairs, 0, 2 * block, splits=2, source=row_halves, halves=True, step=width // 8
    )
    two_far_branch, two_far_sent = matmul(active_far, contract_all, False, parts=2)
    (
        normed_gb,
        q3_in,
        q2_in,
        a2,
        near_c,
        late_terms,
        sent0,
        sent1,
        two_far_branch,
        two_far_sent,
        active_near,
        out_mine,
    ) = sync(
        normed_gb,
        q3_in,
        q2_in,
        a2,
        near_c,
        late_terms,
        sent0,
        sent1,
        two_far_branch,
        two_far_sent,
        active_near,
        out_mine,
    )
    late_n = core_swap(late_terms[TAIL : 2 * TAIL])
    late_x = chip_swap(late_terms[2 * TAIL : 3 * TAIL])
    late_xc = across_swap(late_terms[3 * TAIL :])
    q1_in = group_swap(sent1)
    a1 = ring_down(add(a2, add(kept[1], s1_o)))
    q3_sum = add(kept3, q3_in)
    late_n, late_x, late_xc, q1_in, a1, q3_sum, sent0, active_near, q2_in, two_far_sent = sync(
        late_n, late_x, late_xc, q1_in, a1, q3_sum, sent0, active_near, q2_in, two_far_sent
    )
    out_c = core_swap(two_far_sent)
    q0_in = group_swap(sent0)
    qa3 = ring_down(q3_sum)
    normed_grad = near.astype(F32) + near_c.astype(F32) + cat(normed_ga, normed_gb).astype(F32)
    tail = functools.reduce(
        jnp.add, [v.astype(F32) for v in (late_terms[:TAIL], late_n, late_x, late_xc)]
    )
    normed_grad = normed_grad + cat(jnp.zeros((SEG - TAIL, width), F32), tail)
    _, pull_first = jax.vjp(normalize, hidden_in, gain_first, shift_first)
    input_part, first_gain_grad, first_shift_grad = pull_first(normed_grad)
    input_grad = (middle_grad + input_part).astype(BF16)
    qkv_bias_sums = jnp.sum(qkv_grad.astype(F32), axis=0)
    expand_bias_sums = jnp.sum(before_near.astype(F32), axis=0) + jnp.sum(
        before_far.astype(F32), axis=0
    )
    small = jnp.concatenate(
        [
            first_gain_grad,
            first_shift_grad,
            jnp.sum(middle_grad, axis=0),
            second_gain_grad,
            second_shift_grad,
            jnp.sum(cot_local, axis=0),
        ]
    )
    place = block + hid
    owners = jnp.zeros((n_mp * place,), F32)
    for r in range(teams):
        owner = (team + teams - r) % teams
        mine_hid = ordered(
            expand_bias_sums[2 * r * wide : (2 * r + 1) * wide],
            expand_bias_sums[(2 * r + 1) * wide : (2 * r + 2) * wide],
            0,
        )
        piece = jnp.concatenate(
            [qkv_bias_sums[r * block : (r + 1) * block], mine_hid]
        )
        owners = lax.dynamic_update_slice(owners, piece, ((owner * TEAM + mine) * place,))

    vector, q0_in, qa3, out_c, a1 = sync(cat(small, owners), q0_in, qa3, out_c, a1)

    def add_shifts(shifts, here):
        shifts = jnp.stack(shifts)
        return functools.reduce(jnp.add, [shifts[here(i)] for i in range(shifts.shape[0])])

    shifts = [vector, core_swap(vector), chip_swap(vector), across_swap(vector)]
    branch_two_xa = chip_swap(add(two_far_branch[:part], out_c[:part]))
    branch_two_in = add(two_far_branch[part:], out_c[part:])
    qa2 = ring_down(add(qa3, add(kept2, q2_in)))
    branch_two_xa, branch_two_in, qa2, active_near, a1, *shifts = sync(
        branch_two_xa, branch_two_in, qa2, active_near, a1, *shifts
    )
    vector = add_shifts(shifts, lambda i: mine ^ i)
    shifts = [vector] + [ring_up(vector, r) for r in range(1, teams)]
    qa1 = ring_down(add(qa2, add(kept1, q1_in)))
    expand_mine = other_groups(add(a1, add(kept[0], s0_o)))
    expand_other = group_swap(expand_mine)
    two_near_branch, two_near_sent = matmul(active_near, contract_all, False, parts=2)
    qa1, expand_other, two_near_branch, two_near_sent, branch_two_in, out_mine, *shifts = sync(
        qa1, expand_other, two_near_branch, two_near_sent, branch_two_in, out_mine, *shifts
    )
    vector = add_shifts(shifts, lambda i: (team + teams - i) % teams)
    bit = 1
    while bit < n_dp:
        vector = vector + group_swap(vector, bit)
        bit *= 2
    qkv_mine = other_groups(add(qa1, add(kept0, q0_in)))
    qkv_other = group_swap(qkv_mine)
    branch_two_xb = chip_swap(branch_two_in)
    two_near_c = core_swap(two_near_sent)
    out_sum = other_groups(out_mine)
    out_other = group_swap(out_sum)
    mine_spot = lax.dynamic_slice(vector, (6 * width + me * place,), (place,))
    six = [vector[k * width : (k + 1) * width] for k in range(6)]

    branch_two = (
        two_near_branch.astype(F32)
        + two_near_c.astype(F32)
        + cat(branch_two_xa, branch_two_xb).astype(F32)
    )
    layer_out = (middle + branch_two + contract_bias.astype(F32)).astype(BF16)
    qkv_final = ordered(qkv_mine, qkv_other, 0).astype(F32)
    return (
        layer_out,
        input_grad,
        six[0],
        six[1],
        qkv_final[:, :cols],
        mine_spot[:cols],
        qkv_final[:, cols : 2 * cols],
        qkv_final[:, 2 * cols :],
        mine_spot[2 * cols : 3 * cols],
        ordered(out_sum, out_other, 0).astype(F32),
        six[2],
        six[3],
        six[4],
        ordered(expand_mine, expand_other, 1).astype(F32),
        mine_spot[block:],
        ordered(contract_sum, contract_other, 0).astype(F32),
        six[5],
    )


def solution(mesh):
    rows = P(("dp", "mp"), None)
    in_cols, in_rows = P(None, "mp"), P("mp", None)
    placed = (
        rows,
        P("dp", None),
        P(),
        P(),
        in_cols,
        P("mp"),
        in_cols,
        in_cols,
        P("mp"),
        in_rows,
        P(),
        P(),
        P(),
        in_cols,
        P("mp"),
        in_rows,
        P(),
        rows,
    )
    return jax.shard_map(
        body,
        mesh=mesh,
        in_specs=placed,
        out_specs=(
            rows,
            rows,
            P(),
            P(),
            in_cols,
            P("mp"),
            in_cols,
            in_cols,
            P("mp"),
            in_rows,
            P(),
            P(),
            P(),
            in_cols,
            P("mp"),
            in_rows,
            P(),
        ),
        check_vma=False,
    )
```
